32 devices in a mesh: parts: 2 (over y), wide: 8 (over z, x), narrow: 2 (over core).
Axes of the slice: x: 2, y: 2, z: 4, core: 2. Of those that a mesh axis runs over, the one named last changes fastest.
Arguments:
- queries: bfloat16 [2, 16, 4096], P(None, ('parts', 'wide'), 'narrow'), parts along dimension 1, may hold values from -96 to 96
- new_kv: bfloat16 [2, 16, 2, 1024], P(None, ('parts', 'wide'), None, 'narrow'), parts along dimension 1, may hold values from -5 to 5
- cache_keys: bfloat16 [16, 8, 128, 128], P(('parts', 'wide'), 'narrow'), parts along dimension 0, may hold values from -6 to 6
- stored_values: bfloat16 [16, 8, 128, 128], P(('parts', 'wide'), 'narrow'), parts along dimension 0, may hold values from -6 to 6
- lengths: int32 [16], P(('parts', 'wide')), parts along dimension 0, may hold values from 2 to 126
- residual: bfloat16 [2, 16, 4096], P(None, ('parts', 'wide'), 'narrow'), parts along dimension 1, may hold values from -32 to 32
- norm_gain: float32 [4096], P('narrow'), may hold values from 0.1 to 1.9
- gate_weight: bfloat16 [4096, 2, 28672], P(None, 'narrow', 'wide'), may hold values from -0.09375 to 0.09375
- up_weight: bfloat16 [4096, 2, 28672], P(None, 'narrow', 'wide'), may hold values from -0.09375 to 0.09375
Outputs:
- attended: bfloat16 [2, 16, 4096], P(None, ('parts', 'wide'), 'narrow'), parts along dimension 1
- activated: bfloat16 [2, 16, 14336], P(None, ('parts', 'wide'), 'narrow'), parts along dimension 1
The draws below stay inside these ranges and needn't reach their ends.
There are 2 independent parts, one for each index of `parts`. The reference program is written for one: setup_inputs(seed, part) draws one part's arguments, and reference() takes and returns one part's arrays. A program takes and returns all parts, laid end to end along the dimension named above; an argument that names none is the same for every part. Nothing has to cross between parts.
All inputs are finite; a program needn't handle non-finite values.
Results may differ from the reference program's by a relative error of at most 0.0062.
Values may be sent and summed in bfloat16 or wider, within the bound.
No kernel may reach another device: no remote copies, remote signals or barrier semaphores. Data moves between devices by JAX's collectives and lax.ppermute only.
A program may use at most 128 MiB of HBM per device.

```python
import jax
import jax.numpy as jnp
from jax import lax

D = 4096
HEAD_SIZE = 128
QUERY_HEADS = 32
KEY_VALUE_HEADS = 8
FF = 14336
DECODE_STEPS = 2
HISTORY_SLOTS = 128
ROLLOUT_SLOTS = 8
ROLLOUTS = 6


def new_pairs(key):
    return jax.random.normal(jax.random.fold_in(key, 101), (DECODE_STEPS, ROLLOUT_SLOTS, 2, KEY_VALUE_HEADS * HEAD_SIZE), jnp.float32)


def first_keys(key):
    return jax.random.normal(jax.random.fold_in(key, 102), (ROLLOUT_SLOTS, KEY_VALUE_HEADS, HEAD_SIZE), jnp.float32)


def draw_new_kv(key, part):
    return jnp.clip(new_pairs(key), -5.0, 5.0).astype(jnp.bfloat16)


def draw_cache_keys(key, part):
    leading = first_keys(key)
    key = jax.random.fold_in(key, 3)
    remaining_rows = jax.random.normal(key, (ROLLOUT_SLOTS, KEY_VALUE_HEADS, HISTORY_SLOTS - 1, HEAD_SIZE), jnp.float32)
    whole = jnp.concatenate([leading[:, :, None], remaining_rows], 2)
    return jnp.clip(whole, -6.0, 6.0).astype(jnp.bfloat16)


def draw_queries(key, part):
    key_value_pairs = jnp.clip(new_pairs(key), -5.0, 5.0)
    local_keys = key_value_pairs[:, :, 0].reshape(DECODE_STEPS, ROLLOUT_SLOTS, KEY_VALUE_HEADS, 1, HEAD_SIZE)
    inner_product = jax.random.fold_in(key, 4)
    random_noise = jax.random.normal(inner_product, (DECODE_STEPS, ROLLOUT_SLOTS, KEY_VALUE_HEADS, QUERY_HEADS // KEY_VALUE_HEADS, HEAD_SIZE), jnp.float32)
    base = random_noise + 0.4 * local_keys
    return jnp.clip(base, -96.0, 96.0).reshape(DECODE_STEPS, ROLLOUT_SLOTS, QUERY_HEADS * HEAD_SIZE).astype(jnp.bfloat16)


def draw_lengths(key, part):
    key = jax.random.fold_in(key, 5)
    drawn = jax.random.randint(key, (ROLLOUT_SLOTS,), 2, HISTORY_SLOTS - DECODE_STEPS + 1)
    picked = jax.random.randint(jax.random.fold_in(key, 6), (), 0, ROLLOUTS)
    return jnp.where(jnp.arange(ROLLOUT_SLOTS) == picked, HISTORY_SLOTS - DECODE_STEPS, drawn).astype(jnp.int32)


def draw_residual(key, part):
    key = jax.random.fold_in(key, 7)
    row_scale = jnp.exp(jax.random.uniform(jax.random.fold_in(key, 8), (DECODE_STEPS, ROLLOUT_SLOTS, 1), jnp.float32, jnp.log(0.3), jnp.log(3.0)))
    ramp = jnp.exp(jnp.log(3.0) * jnp.arange(D).astype(jnp.float32) / D)
    col_scale = ramp * jnp.exp(jax.random.uniform(jax.random.fold_in(key, 9), (D,), jnp.float32, -0.5, 0.5))
    base = jax.random.normal(key, (DECODE_STEPS, ROLLOUT_SLOTS, D), jnp.float32)
    return jnp.clip(base * row_scale * col_scale, -32.0, 32.0).astype(jnp.bfloat16)


def block_scale(own_key, extent, split, least, top_value):
    def one(position, parts):
        draws = jax.random.uniform(jax.random.fold_in(jax.random.fold_in(own_key, 6), position), (parts,), jnp.float32, least / len(split), top_value / len(split))
        return jnp.repeat(jnp.exp(draws), extent[position] // parts).reshape((-1,) + (1,) * (len(extent) - position - 1))

    loudness = one(*split[0])
    for cut in split[1:]:
        loudness = loudness * one(*cut)
    return loudness


def noise(key, dims, spread, most, pieces=(), dtype=jnp.bfloat16):
    entries = spread * jax.random.normal(key, dims, jnp.float32)
    if pieces:
        entries = entries * block_scale(key, dims, pieces, -0.22, 0.18)
    return jnp.clip(entries, -most, most).astype(dtype)


def setup_inputs(seed: int = 0, part: int = 0) -> dict:
    splits = jax.random.split(jax.random.key(seed), 10)
    part_splits = jax.random.split(jax.random.fold_in(splits[9], part), 10)
    return {
        "queries": draw_queries(jax.random.fold_in(jax.random.fold_in(splits[9], part), 71), part),
        "new_kv": draw_new_kv(jax.random.fold_in(jax.random.fold_in(splits[9], part), 71), part),
        "cache_keys": draw_cache_keys(jax.random.fold_in(jax.random.fold_in(splits[9], part), 71), part),
        "stored_values": noise(part_splits[3], (ROLLOUT_SLOTS, KEY_VALUE_HEADS, HISTORY_SLOTS, HEAD_SIZE), 1.0, 6.0, ((0, 8), (1, 2))),
        "lengths": draw_lengths(jax.random.fold_in(jax.random.fold_in(splits[9], part), 71), part),
        "residual": draw_residual(jax.random.fold_in(jax.random.fold_in(splits[9], part), 71), part),
        "norm_gain": jnp.clip(1.0 + 0.18 * jax.random.normal(splits[6], (D,), jnp.float32), 0.1, 1.9),
        "gate_weight": noise(splits[7], (D, 2, 2 * FF), D ** -0.5, 0.09375, ((1, 2), (2, 8))),
        "up_weight": noise(splits[8], (D, 2, 2 * FF), D ** -0.5, 0.09375, ((1, 2), (2, 8))),
    }


def attend_one(items):
    query_rows, newest_token, keys, values, length = items
    query_group = QUERY_HEADS // KEY_VALUE_HEADS
    scale = 1.0 / HEAD_SIZE ** 0.5
    query_vector = query_rows.astype(jnp.float32).reshape(DECODE_STEPS, KEY_VALUE_HEADS, query_group, HEAD_SIZE)
    newest_keys = newest_token[:, 0].astype(jnp.float32).reshape(DECODE_STEPS, KEY_VALUE_HEADS, HEAD_SIZE)
    newest_values = newest_token[:, 1].astype(jnp.float32).reshape(DECODE_STEPS, KEY_VALUE_HEADS, HEAD_SIZE)
    cached = jnp.einsum('shgd,hpd->shgp', query_vector, keys.astype(jnp.float32)) * scale
    recent = jnp.einsum('shgd,thd->shgt', query_vector, newest_keys) * scale
    valid = (jnp.arange(HISTORY_SLOTS) < length)[None, None, None, :]
    causal = (jnp.arange(DECODE_STEPS)[None, :] <= jnp.arange(DECODE_STEPS)[:, None])[:, None, None, :]
    cached = jnp.where(valid, cached, -1e+30)
    recent = jnp.where(causal, recent, -1e+30)
    top = jnp.maximum(lax.optimization_barrier(jnp.max(cached, -1)), lax.optimization_barrier(jnp.max(recent, -1)))
    e_cached = jnp.where(valid, jnp.exp(cached - top[..., None]), 0.0)
    e_recent = jnp.where(causal, jnp.exp(recent - top[..., None]), 0.0)
    total = lax.optimization_barrier(jnp.sum(e_cached, -1)) + lax.optimization_barrier(jnp.sum(e_recent, -1))
    w_cached = (e_cached / total[..., None]).astype(jnp.bfloat16).astype(jnp.float32)
    w_recent = (e_recent / total[..., None]).astype(jnp.bfloat16).astype(jnp.float32)
    out = jnp.einsum('shgp,hpd->shgd', w_cached, values.astype(jnp.float32))
    out = out + jnp.einsum('shgt,thd->shgd', w_recent, newest_values)
    return out.reshape(DECODE_STEPS, QUERY_HEADS * HEAD_SIZE).astype(jnp.bfloat16)

def reference(queries, new_kv, cache_keys, stored_values, lengths, residual, norm_gain, gate_weight, up_weight):
    live = ROLLOUTS
    per_rollout = lax.map(attend_one, (jnp.transpose(queries[:, :live], (1, 0, 2)), jnp.transpose(new_kv[:, :live], (1, 0, 2, 3)), cache_keys[:live], stored_values[:live], lengths[:live]))
    attended = jnp.transpose(per_rollout, (1, 0, 2))
    mixed = residual[:, :live].astype(jnp.float32) + attended.astype(jnp.float32)
    mean_sq = lax.optimization_barrier(jnp.sum(mixed * mixed, -1)) / D
    normed = (mixed * lax.rsqrt(mean_sq + 1e-05)[..., None] * norm_gain).astype(jnp.bfloat16)
    rows = normed.reshape(DECODE_STEPS * live, D)
    gate_cols = gate_weight[:, :, 3 * FF // 2:].reshape(D, FF)
    up_cols = up_weight[:, :, 3 * FF // 2:].reshape(D, FF)
    gate = jnp.dot(rows, gate_cols, preferred_element_type=jnp.float32)
    up = jnp.dot(rows, up_cols, preferred_element_type=jnp.float32)
    activated = (jax.nn.silu(gate) * up).astype(jnp.bfloat16).reshape(DECODE_STEPS, live, FF)
    pad_att = jnp.zeros((DECODE_STEPS, ROLLOUT_SLOTS - live, D), jnp.bfloat16)
    pad_act = jnp.zeros((DECODE_STEPS, ROLLOUT_SLOTS - live, FF), jnp.bfloat16)
    return (jnp.concatenate([attended, pad_att], 1), jnp.concatenate([activated, pad_act], 1))
```

```python
import functools

import jax
import jax.numpy as jnp
from jax import lax
from jax.experimental import pallas as pl
from jax.experimental.pallas import tpu as pltpu
from jax.sharding import PartitionSpec as P

D = 4096
HEAD_SIZE = 128
STEPS = 2
TAIL = 128
EPS = 1e-05


def attend_kernel(serving, lengths, q, kv, keys, values, residual, gain, attended, sent):
    owner = lax.axis_index("wide") < serving
    heads, hist, _ = keys.shape
    width = q.shape[1]
    group = width // (heads * HEAD_SIZE)

    @pl.when(jnp.logical_not(owner))
    def _():
        attended[...] = jnp.zeros_like(attended)
        sent[...] = jnp.zeros_like(sent)

    @pl.when(owner)
    def _():
        length = lengths[0]
        slot = lax.broadcasted_iota(jnp.int32, (hist, HEAD_SIZE), 0)
        rows = group * STEPS
        place = lax.broadcasted_iota(jnp.int32, (rows, hist), 1)
        step = lax.broadcasted_iota(jnp.int32, (rows, hist), 0) % STEPS
        first = hist - STEPS
        seen = (place < length) | ((place >= first) & (place - first <= step))
        squares = jnp.zeros((STEPS, 1), jnp.float32)
        for h in range(heads):
            lanes = slice(h * HEAD_SIZE, (h + 1) * HEAD_SIZE)
            k, v = keys[h], values[h]
            for t in range(STEPS):
                k = jnp.where(slot == first + t, kv[t, 0:1, lanes], k)
                v = jnp.where(slot == first + t, kv[t, 1:2, lanes], v)
            cols = [(h * group + g) * HEAD_SIZE for g in range(group)]
            query = jnp.concatenate(
                [q[:, c : c + HEAD_SIZE].astype(jnp.float32) for c in cols], 0
            ).astype(jnp.bfloat16)
            scores = lax.dot_general(
                query, k, (((1,), (1,)), ((), ())), preferred_element_type=jnp.float32
            ) * (1.0 / HEAD_SIZE**0.5)
            scores = jnp.where(seen, scores, -1e30)
            top = jnp.max(scores, -1, keepdims=True)
            e = jnp.where(seen, jnp.exp(scores - top), 0.0)
            weights = (e / jnp.sum(e, -1, keepdims=True)).astype(jnp.bfloat16)
            out = jnp.dot(weights, v, preferred_element_type=jnp.float32)
            for g, c in enumerate(cols):
                here = slice(c, c + HEAD_SIZE)
                got = out[g * STEPS : (g + 1) * STEPS].astype(jnp.bfloat16)
                attended[:, here] = got
                mixed = residual[:, here].astype(jnp.float32) + got.astype(jnp.float32)
                squares += jnp.sum(mixed * mixed, -1, keepdims=True)
                sent[:, here] = (mixed * gain[:, here]).astype(jnp.bfloat16)
        high = squares.astype(jnp.bfloat16)
        low = (squares - high.astype(jnp.float32)).astype(jnp.bfloat16)
        lane = lax.broadcasted_iota(jnp.int32, (STEPS, TAIL), 1)
        sent[:, width:] = jnp.where(
            lane == 0,
            high.astype(jnp.float32),
            jnp.where(lane == 1, low.astype(jnp.float32), 0.0),
        ).astype(jnp.bfloat16)


def forward_kernel(serving, narrow, tile, gathered, gate, up, *rest):
    outs = rest[:serving]
    x, scale, gates, ups, sems = rest[serving:]
    wide = lax.axis_index("wide")
    features, columns = gate.shape
    tiles = columns // tile
    half = features // narrow
    depth = gates.shape[0]

    def copies(j):
        here = pl.ds(j * tile, tile)
        s = j % depth
        return (
            pltpu.make_async_copy(gate.at[:, here], gates.at[s], sems.at[0, s]),
            pltpu.make_async_copy(up.at[:, here], ups.at[s], sems.at[1, s]),
        )

    @pl.when(wide < serving)
    def _():
        for out in outs:
            out[...] = jnp.zeros_like(out)

    @pl.when(wide >= serving)
    def _():
        for j in range(min(depth, tiles)):
            for c in copies(j):
                c.start()
        rows, tails = [], []
        for i in range(serving):
            owner = lax.rem(i + wide - serving, serving)
            parts = [gathered[owner * narrow + n] for n in range(narrow)]
            rows.append(jnp.concatenate([p[:, :half] for p in parts], 1).astype(jnp.float32))
            tails.append(sum(p[:, half:].astype(jnp.float32) for p in parts))
        pad = x.shape[0] - STEPS * serving
        if pad:
            rows.append(jnp.zeros((pad, features), jnp.float32))
            tails.append(jnp.zeros((pad, TAIL), jnp.float32))
        x[...] = jnp.concatenate(rows, 0).astype(jnp.bfloat16)
        squares = jnp.sum(jnp.concatenate(tails, 0), -1, keepdims=True)
        scale[...] = jnp.broadcast_to(lax.rsqrt(squares / D + EPS), scale.shape)
        for j in range(tiles):
            for c in copies(j):
                c.wait()
            s = j % depth
            r = scale[:, 0:1]
            g = jnp.dot(x[...], gates[s], preferred_element_type=jnp.float32) * r
            u = jnp.dot(x[...], ups[s], preferred_element_type=jnp.float32) * r
            hidden = (g / (1.0 + jnp.exp(-g)) * u).astype(jnp.bfloat16)
            for i, out in enumerate(outs):
                out[:, j * tile : (j + 1) * tile] = hidden[i * STEPS : (i + 1) * STEPS]
            if j + depth < tiles:
                for c in copies(j + depth):
                    c.start()


def shards(queries, new_kv, keys, values, lengths, residual, gain, gate, up):
    wide = lax.axis_size("wide")
    narrow = lax.axis_size("narrow")
    serving = wide * 3 // 4
    workers = wide - serving
    half = queries.shape[2]
    features, _, columns = gate.shape
    vmem = pl.BlockSpec(memory_space=pltpu.VMEM)
    attended, sent = pl.pallas_call(
        functools.partial(attend_kernel, serving),
        out_shape=(
            jax.ShapeDtypeStruct((STEPS, half), jnp.bfloat16),
            jax.ShapeDtypeStruct((STEPS, half + TAIL), jnp.bfloat16),
        ),
        in_specs=[pl.BlockSpec(memory_space=pltpu.SMEM)] + [vmem] * 6,
        out_specs=(vmem, vmem),
        compiler_params=pltpu.CompilerParams(vmem_limit_bytes=8 << 20),
    )(
        lengths,
        queries.reshape(STEPS, half),
        new_kv.reshape(STEPS, 2, -1),
        keys.reshape(keys.shape[1:]),
        values.reshape(values.shape[1:]),
        residual.reshape(STEPS, half),
        gain.reshape(1, half),
    )
    gathered = lax.all_gather(sent, ("wide", "narrow"), axis=0)
    tile = next((t for t in (512, 256, 128) if columns % t == 0), columns)
    depth = min(3, columns // tile)
    padded = -(-STEPS * serving // 16) * 16
    hidden = pl.pallas_call(
        functools.partial(forward_kernel, serving, narrow, tile),
        out_shape=[jax.ShapeDtypeStruct((STEPS, columns), jnp.bfloat16)] * serving,
        in_specs=[vmem, pl.BlockSpec(memory_space=pl.ANY), pl.BlockSpec(memory_space=pl.ANY)],
        out_specs=[vmem] * serving,
        scratch_shapes=[
            pltpu.VMEM((padded, features), jnp.bfloat16),
            pltpu.VMEM((padded, 128), jnp.float32),
            pltpu.VMEM((depth, features, tile), jnp.bfloat16),
            pltpu.VMEM((depth, features, tile), jnp.bfloat16),
            pltpu.SemaphoreType.DMA((2, depth)),
        ],
        compiler_params=pltpu.CompilerParams(vmem_limit_bytes=48 << 20),
    )(gathered, gate.reshape(features, columns), up.reshape(features, columns))
    back = [
        lax.ppermute(h, "wide", [(serving + k, (i + k) % serving) for k in range(workers)])
        for i, h in enumerate(hidden)
    ]
    me = lax.axis_index("wide")
    pieces = []
    for k in range(workers):
        mine = lax.rem(me + serving - k, serving)
        piece = back[0]
        for i in range(1, serving):
            piece = jnp.where(mine == i, back[i], piece)
        pieces.append(jnp.where(me < serving, piece, jnp.zeros((), jnp.bfloat16)))
    activated = jnp.concatenate(pieces, 1)
    return attended.reshape(STEPS, 1, half), activated.reshape(STEPS, 1, -1)


def solution(mesh):
    rows = P(None, ("parts", "wide"), "narrow")
    placed = (
        rows,
        P(None, ("parts", "wide"), None, "narrow"),
        P(("parts", "wide"), "narrow", None, None),
        P(("parts", "wide"), "narrow", None, None),
        P(("parts", "wide")),
        rows,
        P("narrow"),
        P(None, "narrow", "wide"),
        P(None, "narrow", "wide"),
    )
    return jax.shard_map(
        shards, mesh=mesh, in_specs=placed, out_specs=(rows, rows), check_vma=False
    )
```

```python
import functools

import jax
import jax.numpy as jnp
from jax import lax
from jax.experimental import pallas as pl
from jax.experimental.pallas import tpu as pltpu
from jax.sharding import PartitionSpec as P

D = 4096
HEAD_SIZE = 128
STEPS = 2
TAIL = 128
EPS = 1e-05
FETCH = (2, 2, 1, 2)


def pair(squares):
    high = squares.astype(jnp.bfloat16).astype(jnp.float32)
    lane = lax.broadcasted_iota(jnp.int32, (squares.shape[0], TAIL), 1)
    both = jnp.where(lane == 0, high, jnp.where(lane == 1, squares - high, 0.0))
    return both.astype(jnp.bfloat16)


def fetches(share, spans, gate, up, held, sems):
    tile = held.shape[3]
    base = lax.axis_index("parts") * (gate.shape[1] // share) if share > 1 else 0
    copies = []
    for c, j in enumerate(spans):
        here = pl.ds(pl.multiple_of(base + j * tile, 128) if share > 1 else j * tile, tile)
        for m, matrix in enumerate((gate, up)):
            copies.append(pltpu.make_async_copy(matrix.at[:, here], held.at[c, m], sems.at[c, m]))
    return copies


def fetch_kernel(serving, share, spans, _, gate, up, held, sems):
    @pl.when(lax.axis_index("wide") >= serving)
    def _():
        copies = fetches(share, spans, gate, up, held, sems)
        for c in copies:
            c.start()
        for c in copies:
            c.wait()


def attend_kernel(serving, share, spans, lengths, *refs):
    sources, gate, up, attended, sent, weights_held = refs[:6], *refs[6:11]
    held, sems, weight_sems = refs[11:17], refs[17], refs[18]
    q, kv, keys, values, residual, gain = held
    owner = lax.axis_index("wide") < serving
    heads, hist, _ = keys.shape
    width = q.shape[1]
    group = width // (heads * HEAD_SIZE)

    @pl.when(jnp.logical_not(owner))
    def _():
        copies = fetches(share, spans, gate, up, weights_held, weight_sems)
        for c in copies:
            c.start()
        attended[...] = jnp.zeros_like(attended)
        sent[...] = jnp.zeros_like(sent)
        for c in copies:
            c.wait()

    @pl.when(owner)
    def _():
        copies = [
            pltpu.make_async_copy(source, place, sems.at[i])
            for i, (source, place) in enumerate(zip(sources, held))
        ]
        for c in copies:
            c.start()
        for c in copies:
            c.wait()
        length = lengths[0]
        slot = lax.broadcasted_iota(jnp.int32, (hist, HEAD_SIZE), 0)
        rows = group * STEPS
        place = lax.broadcasted_iota(jnp.int32, (rows, hist), 1)
        step = lax.broadcasted_iota(jnp.int32, (rows, hist), 0) % STEPS
        first = hist - STEPS
        seen = (place < length) | ((place >= first) & (place - first <= step))
        squares = jnp.zeros((STEPS, 1), jnp.float32)
        for h in range(heads):
            lanes = slice(h * HEAD_SIZE, (h + 1) * HEAD_SIZE)
            k, v = keys[h], values[h]
            for t in range(STEPS):
                k = jnp.where(slot == first + t, kv[t, 0:1, lanes], k)
                v = jnp.where(slot == first + t, kv[t, 1:2, lanes], v)
            cols = [(h * group + g) * HEAD_SIZE for g in range(group)]
            query = jnp.concatenate(
                [q[:, c : c + HEAD_SIZE].astype(jnp.float32) for c in cols], 0
            ).astype(jnp.bfloat16)
            scores = lax.dot_general(
                query, k, (((1,), (1,)), ((), ())), preferred_element_type=jnp.float32
            ) * (1.0 / HEAD_SIZE**0.5)
            scores = jnp.where(seen, scores, -1e30)
            top = jnp.max(scores, -1, keepdims=True)
            e = jnp.where(seen, jnp.exp(scores - top), 0.0)
            weights = (e / jnp.sum(e, -1, keepdims=True)).astype(jnp.bfloat16)
            out = jnp.dot(weights, v, preferred_element_type=jnp.float32)
            for g, c in enumerate(cols):
                here = slice(c, c + HEAD_SIZE)
                got = out[g * STEPS : (g + 1) * STEPS].astype(jnp.bfloat16)
                attended[:, here] = got
                mixed = residual[:, here].astype(jnp.float32) + got.astype(jnp.float32)
                squares += jnp.sum(mixed * mixed, -1, keepdims=True)
                sent[:, here] = (mixed * gain[:, here]).astype(jnp.bfloat16)
        sent[:, width:] = pair(squares)


def collect_kernel(blocks, workers, narrow, share, spans, *refs):
    arrived, (gate, up, _, rows, held, sems) = refs[:blocks], refs[blocks:]
    me = lax.axis_index("wide") - blocks * workers
    features = gate.shape[0]
    half = features // narrow

    @pl.when(me >= 0)
    def _():
        copies = fetches(share, spans, gate, up, held, sems)
        for c in copies:
            c.start()
        lines, tails = [], []
        for block in arrived:
            for shift in range(workers):
                owner = lax.rem(me + shift, workers)
                parts = [block[owner * narrow + n] for n in range(narrow)]
                lines.append(jnp.concatenate([p[:, :half] for p in parts], 1).astype(jnp.float32))
                tails.append(sum(p[:, half:].astype(jnp.float32) for p in parts))
        pad = rows.shape[0] - STEPS * blocks * workers
        if pad:
            lines.append(jnp.zeros((pad, features), jnp.float32))
            tails.append(jnp.zeros((pad, TAIL), jnp.float32))
        rows[:, :features] = jnp.concatenate(lines, 0).astype(jnp.bfloat16)
        rows[:, features:] = pair(jnp.sum(jnp.concatenate(tails, 0), -1, keepdims=True))
        for c in copies:
            c.wait()


def forward_kernel(serving, counts, *refs):
    held = refs[: len(counts)]
    rest = refs[len(counts) :]
    batches = len(rest) // 2
    rows, outs = rest[:batches], rest[batches:]
    features, tile = held[0].shape[2:]

    @pl.when(lax.axis_index("wide") >= serving)
    def _():
        x = jnp.concatenate([r[:, :features] for r in rows], 0)
        tails = jnp.concatenate([r[:, features:].astype(jnp.float32) for r in rows], 0)
        r = lax.rsqrt(jnp.sum(tails, -1, keepdims=True) / D + EPS)
        j = 0
        for piece, count in zip(held, counts):
            for c in range(count):
                g = jnp.dot(x, piece[c, 0], preferred_element_type=jnp.float32) * r
                u = jnp.dot(x, piece[c, 1], preferred_element_type=jnp.float32) * r
                hidden = g / (1.0 + jnp.exp(-g)) * u
                for b, out in enumerate(outs):
                    first = b * rows[0].shape[0]
                    for i in range(serving):
                        here = slice(first + i * STEPS, first + (i + 1) * STEPS)
                        out[i, :, j * tile : (j + 1) * tile] = hidden[here].astype(jnp.bfloat16)
                j += 1


def split_kernel(serving, *refs):
    batches, outs = refs[:-serving], refs[-serving:]
    local = batches[0].shape[2]

    @pl.when(lax.axis_index("wide") >= serving)
    def _():
        for p in range(len(batches)):

            @pl.when(lax.axis_index("parts") == p if len(batches) > 1 else True)
            def _():
                for d, batch in enumerate(batches):
                    q = (p + d) % len(batches)
                    for i, out in enumerate(outs):
                        out[:, q * local : (q + 1) * local] = batch[i]


def divide(count, shares):
    total, edges, run = sum(shares), [0], 0
    for s in shares:
        run += s
        edges.append(round(count * run / total))
    return [list(range(a, b)) for a, b in zip(edges, edges[1:])]


def swap(x, pairs):
    return lax.ppermute(x, "wide", pairs + [(b, a) for a, b in pairs])


def shards(queries, new_kv, keys, values, lengths, residual, gain, gate, up):
    wide = lax.axis_size("wide")
    narrow = lax.axis_size("narrow")
    parts = lax.axis_size("parts")
    serving = wide * 3 // 4
    workers = wide - serving
    blocks = serving // workers
    half = queries.shape[2]
    features, _, columns = gate.shape
    share = parts if columns % (parts * 128) == 0 else 1
    local = columns // share
    tile = next((t for t in (256, 128) if local % t == 0), local)
    spans = divide(local // tile, FETCH)
    vmem = pl.BlockSpec(memory_space=pltpu.VMEM)
    hbm = pl.BlockSpec(memory_space=pltpu.HBM)

    def in_hbm(a):
        return pltpu.with_memory_space_constraint(a, pltpu.HBM)

    def held(span):
        return pltpu.VMEM((max(len(span), 1), 2, features, tile), jnp.bfloat16)

    def fetch_sems(span):
        return pltpu.SemaphoreType.DMA((max(len(span), 1), 2))

    def fetch_time(span):
        moved = len(span) * 4 * features * tile
        return pl.CostEstimate(flops=0, bytes_accessed=moved, transcendentals=0)

    gate = in_hbm(gate.reshape(features, columns))
    up = in_hbm(up.reshape(features, columns))
    operands = (
        queries.reshape(STEPS, half),
        new_kv.reshape(STEPS, 2, -1),
        keys.reshape(keys.shape[1:]),
        values.reshape(values.shape[1:]),
        residual.reshape(STEPS, half),
        gain.reshape(1, half),
    )
    attended, sent, first = pl.pallas_call(
        functools.partial(attend_kernel, serving, share, spans[0]),
        out_shape=(
            jax.ShapeDtypeStruct((STEPS, half), jnp.bfloat16),
            jax.ShapeDtypeStruct((STEPS, half + TAIL), jnp.bfloat16),
            held(spans[0]),
        ),
        in_specs=[pl.BlockSpec(memory_space=pltpu.SMEM)] + [hbm] * 8,
        out_specs=(vmem, vmem, vmem),
        scratch_shapes=[pltpu.VMEM(o.shape, o.dtype) for o in operands]
        + [pltpu.SemaphoreType.DMA((6,)), fetch_sems(spans[0])],
        compiler_params=pltpu.CompilerParams(vmem_limit_bytes=16 << 20),
        cost_estimate=fetch_time(spans[0]),
    )(lengths, *map(in_hbm, operands), gate, up)
    weights = [first]

    def fetch(span, after):
        weights.append(
            pl.pallas_call(
                functools.partial(fetch_kernel, serving, share, span),
                out_shape=held(span),
                in_specs=[pl.BlockSpec(memory_space=pl.ANY), hbm, hbm],
                out_specs=vmem,
                scratch_shapes=[fetch_sems(span)],
                compiler_params=pltpu.CompilerParams(vmem_limit_bytes=16 << 20),
                cost_estimate=fetch_time(span),
            )(after, gate, up)
        )

    order = range(blocks)[::-1]
    groups = [
        [w * narrow + n for w in range(at, at + workers) for n in range(narrow)]
        for at in range(0, wide, workers)
    ]
    block = lax.all_gather(sent, ("wide", "narrow"), axis=0, axis_index_groups=groups)
    arrived = [
        lax.ppermute(block, "wide", [(b * workers + j, serving + j) for j in range(workers)])
        for b in order
    ]
    fetch(spans[1], block)
    padded = -(-STEPS * serving // 16) * 16
    rows, third = pl.pallas_call(
        functools.partial(collect_kernel, blocks, workers, narrow, share, spans[2]),
        out_shape=(jax.ShapeDtypeStruct((padded, features + TAIL), jnp.bfloat16), held(spans[2])),
        in_specs=[vmem] * blocks + [hbm, hbm, pl.BlockSpec(memory_space=pl.ANY)],
        out_specs=(vmem, vmem),
        scratch_shapes=[fetch_sems(spans[2])],
        compiler_params=pltpu.CompilerParams(vmem_limit_bytes=16 << 20),
        cost_estimate=fetch_time(spans[2]),
    )(*arrived, gate, up, weights[-1])
    weights.append(third)
    batch = [rows]
    for d in range(1, share):
        batch.append(lax.ppermute(rows, "parts", [((p + d) % parts, p) for p in range(parts)]))
    fetch(spans[3], rows)
    hidden = pl.pallas_call(
        functools.partial(forward_kernel, serving, [len(span) for span in spans]),
        out_shape=[jax.ShapeDtypeStruct((serving, STEPS, local), jnp.bfloat16)] * share,
        in_specs=[vmem] * (len(weights) + share),
        out_specs=[vmem] * share,
        compiler_params=pltpu.CompilerParams(vmem_limit_bytes=16 << 20),
    )(*weights, *batch)
    finished = [hidden[0]]
    for d in range(1, share):
        finished.append(
            lax.ppermute(hidden[share - d], "parts", [((p + d) % parts, p) for p in range(parts)])
        )
    messages = pl.pallas_call(
        functools.partial(split_kernel, serving),
        out_shape=[jax.ShapeDtypeStruct((STEPS, columns), jnp.bfloat16)] * serving,
        in_specs=[vmem] * share,
        out_specs=[vmem] * serving,
        compiler_params=pltpu.CompilerParams(vmem_limit_bytes=16 << 20),
    )(*finished)
    back = [
        [
            swap(
                messages[i * workers + s],
                [(serving + k, b * workers + (k + s) % workers) for k in range(workers)],
            )
            for s in range(workers)
        ]
        for i, b in enumerate(order)
    ]
    me = lax.axis_index("wide")
    pieces = []
    for k in range(workers):
        piece = jnp.zeros((), jnp.bfloat16)
        for i, b in enumerate(order):
            for s in range(workers):
                mine = me == b * workers + (k + s) % workers
                piece = jnp.where(mine, back[i][s], piece)
        pieces.append(piece)
    activated = jnp.concatenate(pieces, 1)
    return attended.reshape(STEPS, 1, half), activated.reshape(STEPS, 1, -1)


def solution(mesh):
    rows = P(None, ("parts", "wide"), "narrow")
    placed = (
        rows,
        P(None, ("parts", "wide"), None, "narrow"),
        P(("parts", "wide"), "narrow", None, None),
        P(("parts", "wide"), "narrow", None, None),
        P(("parts", "wide")),
        rows,
        P("narrow"),
        P(None, "narrow", "wide"),
        P(None, "narrow", "wide"),
    )
    return jax.shard_map(
        shards, mesh=mesh, in_specs=placed, out_specs=(rows, rows), check_vma=False
    )
```

```python
import functools

import jax
import jax.numpy as jnp
from jax import lax
from jax.experimental import pallas as pl
from jax.experimental.pallas import tpu as pltpu
from jax.sharding import PartitionSpec as P

D = 4096
HEAD_SIZE = 128
STEPS = 2
TAIL = 128
EPS = 1e-05
DEPTH = 256
EARLY = 5
SLOTS = 6


def pair(squares):
    high = squares.astype(jnp.bfloat16).astype(jnp.float32)
    lane = lax.broadcasted_iota(jnp.int32, (squares.shape[0], TAIL), 1)
    both = jnp.where(lane == 0, high, jnp.where(lane == 1, squares - high, 0.0))
    return both.astype(jnp.bfloat16)


def fetches(share, c, slot, gate, up, held, sems):
    depth, local = held.shape[2:]
    here = pl.ds(c * depth, depth)
    copies = []
    for m, matrix in enumerate((gate, up)):
        source = matrix.at[here]
        if share > 1:
            base = pl.multiple_of(lax.axis_index("parts") * local, 128)
            source = matrix.at[here, pl.ds(base, local)]
        copies.append(pltpu.make_async_copy(source, held.at[slot, m], sems.at[slot, m]))
    return copies


def fetch_kernel(serving, share, _, gate, up, held, sems):
    @pl.when(lax.axis_index("wide") >= serving)
    def _():
        copies = [fetches(share, c, c, gate, up, held, sems) for c in range(held.shape[0])]
        for some in copies:
            for c in some:
                c.start()
        for some in copies:
            for c in some:
                c.wait()


def blank_kernel(out):
    out[...] = jnp.zeros_like(out)


def attend_kernel(serving, lengths, *refs):
    sources, (attended, sent), held, sems = refs[:6], refs[6:8], refs[8:14], refs[14]
    q, kv, keys, values, residual, gain = held
    owner = lax.axis_index("wide") < serving
    heads, hist, _ = keys.shape
    width = q.shape[1]
    group = width // (heads * HEAD_SIZE)

    @pl.when(jnp.logical_not(owner))
    def _():
        attended[...] = jnp.zeros_like(attended)
        sent[...] = jnp.zeros_like(sent)

    @pl.when(owner)
    def _():
        copies = [
            pltpu.make_async_copy(source, place, sems.at[i])
            for i, (source, place) in enumerate(zip(sources, held))
        ]
        for c in copies:
            c.start()
        for c in copies:
            c.wait()
        length = lengths[0]
        slot = lax.broadcasted_iota(jnp.int32, (hist, HEAD_SIZE), 0)
        rows = group * STEPS
        place = lax.broadcasted_iota(jnp.int32, (rows, hist), 1)
        step = lax.broadcasted_iota(jnp.int32, (rows, hist), 0) % STEPS
        first = hist - STEPS
        seen = (place < length) | ((place >= first) & (place - first <= step))
        squares = jnp.zeros((STEPS, 1), jnp.float32)
        for h in range(heads):
            lanes = slice(h * HEAD_SIZE, (h + 1) * HEAD_SIZE)
            k, v = keys[h], values[h]
            for t in range(STEPS):
                k = jnp.where(slot == first + t, kv[t, 0:1, lanes], k)
                v = jnp.where(slot == first + t, kv[t, 1:2, lanes], v)
            cols = [(h * group + g) * HEAD_SIZE for g in range(group)]
            query = jnp.concatenate(
                [q[:, c : c + HEAD_SIZE].astype(jnp.float32) for c in cols], 0
            ).astype(jnp.bfloat16)
            scores = lax.dot_general(
                query, k, (((1,), (1,)), ((), ())), preferred_element_type=jnp.float32
            ) * (1.0 / HEAD_SIZE**0.5)
            scores = jnp.where(seen, scores, -1e30)
            top = jnp.max(scores, -1, keepdims=True)
            e = jnp.where(seen, jnp.exp(scores - top), 0.0)
            weights = (e / jnp.sum(e, -1, keepdims=True)).astype(jnp.bfloat16)
            out = jnp.dot(weights, v, preferred_element_type=jnp.float32)
            for g, c in enumerate(cols):
                here = slice(c, c + HEAD_SIZE)
                got = out[g * STEPS : (g + 1) * STEPS].astype(jnp.bfloat16)
                attended[:, here] = got
                mixed = residual[:, here].astype(jnp.float32) + got.astype(jnp.float32)
                squares += jnp.sum(mixed * mixed, -1, keepdims=True)
                sent[:, here] = (mixed * gain[:, here]).astype(jnp.bfloat16)
        sent[:, width:] = pair(squares)


def forward_kernel(blocks, workers, narrow, share, *refs):
    count = blocks * workers
    arrived, (held, gate, up), rest = refs[:blocks], refs[blocks : blocks + 3], refs[blocks + 3 :]
    outs, (x, sums, slots, sems) = rest[: -4], rest[-4:]
    me = lax.axis_index("wide") - count
    features = gate.shape[0]
    depth = held.shape[2]
    early, room = held.shape[0], slots.shape[0]
    total = features // depth
    half = features // narrow

    def stream(c):
        return fetches(share, c, (c - early) % room, gate, up, slots, sems)

    @pl.when(me >= 0)
    def _():
        for c in range(early, min(early + room, total)):
            for copy in stream(c):
                copy.start()
        lines, tails = [], []
        for d in range(share):
            part = lax.rem(lax.axis_index("parts") + d, share) if share > 1 else 0
            for block in arrived:
                for shift in range(workers):
                    owner = part * workers + lax.rem(me + shift, workers)
                    halves = [block[owner * narrow + n] for n in range(narrow)]
                    lines.append(
                        jnp.concatenate([h[:, :half] for h in halves], 1).astype(jnp.float32)
                    )
                    tails.append(sum(h[:, half:].astype(jnp.float32) for h in halves))
        pad = x.shape[0] - STEPS * count * share
        if pad:
            lines.append(jnp.zeros((pad, features), jnp.float32))
            tails.append(jnp.zeros((pad, TAIL), jnp.float32))
        x[...] = jnp.concatenate(lines, 0).astype(jnp.bfloat16)
        squares = jnp.sum(jnp.concatenate(tails, 0), -1, keepdims=True)
        r = lax.rsqrt(squares / D + EPS)
        for c in range(total):
            if c >= early:
                for copy in stream(c):
                    copy.wait()
            rows = x[:, c * depth : (c + 1) * depth]
            for m in range(2):
                block = held[c, m] if c < early else slots[(c - early) % room, m]
                product = jnp.dot(rows, block, preferred_element_type=jnp.float32)
                sums[m] = product if c == 0 else sums[m] + product
            if c >= early and c + room < total:
                for copy in stream(c + room):
                    copy.start()
        g, u = sums[0] * r, sums[1] * r
        hidden = (g / (1.0 + jnp.exp(-g)) * u).astype(jnp.bfloat16)
        for i, out in enumerate(outs):
            out[...] = hidden[i * STEPS : (i + 1) * STEPS]


def shards(queries, new_kv, keys, values, lengths, residual, gain, gate, up):
    wide = lax.axis_size("wide")
    narrow = lax.axis_size("narrow")
    serving = wide * 3 // 4
    workers = wide - serving
    blocks = serving // workers
    half = queries.shape[2]
    features, _, columns = gate.shape
    share = 1
    local = columns // share
    vmem = pl.BlockSpec(memory_space=pltpu.VMEM)
    hbm = pl.BlockSpec(memory_space=pltpu.HBM)
    owner = lax.axis_index("wide") < serving

    def in_hbm(a):
        return pltpu.with_memory_space_constraint(a, pltpu.HBM)

    gate = in_hbm(gate.reshape(features, columns))
    up = in_hbm(up.reshape(features, columns))
    operands = (
        queries.reshape(STEPS, half),
        new_kv.reshape(STEPS, 2, -1),
        keys.reshape(keys.shape[1:]),
        values.reshape(values.shape[1:]),
        residual.reshape(STEPS, half),
        gain.reshape(1, half),
    )
    attended, sent = pl.pallas_call(
        functools.partial(attend_kernel, serving),
        out_shape=(
            jax.ShapeDtypeStruct((STEPS, half), jnp.bfloat16),
            jax.ShapeDtypeStruct((STEPS, half + TAIL), jnp.bfloat16),
        ),
        in_specs=[pl.BlockSpec(memory_space=pltpu.SMEM)] + [hbm] * 6,
        out_specs=(vmem, vmem),
        scratch_shapes=[pltpu.VMEM(o.shape, o.dtype) for o in operands]
        + [pltpu.SemaphoreType.DMA((6,))],
        compiler_params=pltpu.CompilerParams(vmem_limit_bytes=8 << 20),
    )(lengths, *map(in_hbm, operands))

    groups = [
        [w * narrow + n for w in range(at, at + workers) for n in range(narrow)]
        for at in range(0, wide, workers)
    ]
    blank = pl.pallas_call(
        blank_kernel,
        out_shape=jax.ShapeDtypeStruct((workers * narrow, *sent.shape), jnp.bfloat16),
        out_specs=vmem,
        compiler_params=pltpu.CompilerParams(vmem_limit_bytes=8 << 20),
    )
    block = lax.cond(
        owner,
        lambda s: lax.all_gather(s, ("wide", "narrow"), axis=0, axis_index_groups=groups),
        lambda s: blank(),
        sent,
    )
    arrived = [
        lax.ppermute(block, "wide", [(b * workers + j, serving + j) for j in range(workers)])
        for b in range(blocks)
    ]
    early = min(EARLY, features // DEPTH - 1)
    held = pl.pallas_call(
        functools.partial(fetch_kernel, serving, share),
        out_shape=pltpu.VMEM((early, 2, DEPTH, local), jnp.bfloat16),
        in_specs=[pl.BlockSpec(memory_space=pl.ANY), hbm, hbm],
        out_specs=vmem,
        scratch_shapes=[pltpu.SemaphoreType.DMA((early, 2))],
        compiler_params=pltpu.CompilerParams(vmem_limit_bytes=4 << 20),
        cost_estimate=pl.CostEstimate(
            flops=0, bytes_accessed=early * 4 * DEPTH * local, transcendentals=0
        ),
    )(block, gate, up)
    padded = -(-STEPS * serving * share // 16) * 16
    hidden = pl.pallas_call(
        functools.partial(forward_kernel, blocks, workers, narrow, share),
        out_shape=[jax.ShapeDtypeStruct((STEPS, local), jnp.bfloat16)] * (serving * share),
        in_specs=[vmem] * (blocks + 1) + [hbm, hbm],
        out_specs=[vmem] * (serving * share),
        scratch_shapes=[
            pltpu.VMEM((padded, features), jnp.bfloat16),
            pltpu.VMEM((2, padded, local), jnp.float32),
            pltpu.VMEM((SLOTS, 2, DEPTH, local), jnp.bfloat16),
            pltpu.SemaphoreType.DMA((SLOTS, 2)),
        ],
        compiler_params=pltpu.CompilerParams(vmem_limit_bytes=32 << 20),
    )(*arrived, held, gate, up)
    back = [[None] * workers for _ in range(blocks)]
    for b in reversed(range(blocks)):
        for s in range(workers):
            pairs = [(serving + k, b * workers + (k + s) % workers) for k in range(workers)]
            back[b][s] = lax.ppermute(hidden[b * workers + s], "wide", pairs)
    me = lax.axis_index("wide")
    pieces = []
    for k in range(workers):
        piece = jnp.zeros((), jnp.bfloat16)
        for b in range(blocks):
            for s in range(workers):
                mine = me == b * workers + (k + s) % workers
                piece = jnp.where(mine, back[b][s], piece)
        pieces.append(piece)
    activated = jnp.concatenate(pieces, 1)
    return attended.reshape(STEPS, 1, half), activated.reshape(STEPS, 1, -1)


def solution(mesh):
    rows = P(None, ("parts", "wide"), "narrow")
    placed = (
        rows,
        P(None, ("parts", "wide"), None, "narrow"),
        P(("parts", "wide"), "narrow", None, None),
        P(("parts", "wide"), "narrow", None, None),
        P(("parts", "wide")),
        rows,
        P("narrow"),
        P(None, "narrow", "wide"),
        P(None, "narrow", "wide"),
    )
    return jax.shard_map(
        shards, mesh=mesh, in_specs=placed, out_specs=(rows, rows), check_vma=False
    )
```

```python
import functools

import jax
import jax.numpy as jnp
from jax import lax
from jax.experimental import pallas as pl
from jax.experimental.pallas import tpu as pltpu
from jax.sharding import PartitionSpec as P

D = 4096
HEAD_SIZE = 128
STEPS = 2
TAIL = 128
EPS = 1e-05
DEPTH = 256
EARLY = 7
SLOTS = 5


def pair(squares):
    high = squares.astype(jnp.bfloat16).astype(jnp.float32)
    lane = lax.broadcasted_iota(jnp.int32, (squares.shape[0], TAIL), 1)
    both = jnp.where(lane == 0, high, jnp.where(lane == 1, squares - high, 0.0))
    return both.astype(jnp.bfloat16)


def fetches(share, c, slot, gate, up, held, sems):
    depth, local = held.shape[2:]
    here = pl.ds(c * depth, depth)
    copies = []
    for m, matrix in enumerate((gate, up)):
        source = matrix.at[here]
        if share > 1:
            base = pl.multiple_of(lax.axis_index("parts") * local, 128)
            source = matrix.at[here, pl.ds(base, local)]
        copies.append(pltpu.make_async_copy(source, held.at[slot, m], sems.at[slot, m]))
    return copies


def fetch_kernel(serving, share, _, gate, up, held, sems):
    @pl.when(lax.axis_index("wide") >= serving)
    def _():
        copies = [fetches(share, c, c, gate, up, held, sems) for c in range(held.shape[0])]
        for some in copies:
            for c in some:
                c.start()
        for some in copies:
            for c in some:
                c.wait()


def blank_kernel(out):
    out[...] = jnp.zeros_like(out)


def attend_kernel(serving, *refs):
    sources, (attended, sent), held, sems = refs[:7], refs[7:9], refs[9:16], refs[16]
    lengths, q, kv, keys, values, residual, gain = held
    owner = lax.axis_index("wide") < serving
    heads, hist, _ = keys.shape
    width = q.shape[1]
    group = width // (heads * HEAD_SIZE)

    @pl.when(jnp.logical_not(owner))
    def _():
        attended[...] = jnp.zeros_like(attended)
        sent[...] = jnp.zeros_like(sent)

    @pl.when(owner)
    def _():
        copies = [
            pltpu.make_async_copy(source, place, sems.at[i])
            for i, (source, place) in enumerate(zip(sources, held))
        ]
        for c in copies:
            c.start()
        for c in copies:
            c.wait()
        length = lengths[0, 0]
        slot = lax.broadcasted_iota(jnp.int32, (hist, HEAD_SIZE), 0)
        rows = group * STEPS
        place = lax.broadcasted_iota(jnp.int32, (rows, hist), 1)
        step = lax.broadcasted_iota(jnp.int32, (rows, hist), 0) % STEPS
        first = hist - STEPS
        seen = (place < length) | ((place >= first) & (place - first <= step))
        squares = jnp.zeros((STEPS, 1), jnp.float32)
        for h in range(heads):
            lanes = slice(h * HEAD_SIZE, (h + 1) * HEAD_SIZE)
            k, v = keys[h], values[h]
            for t in range(STEPS):
                k = jnp.where(slot == first + t, kv[t, 0:1, lanes], k)
                v = jnp.where(slot == first + t, kv[t, 1:2, lanes], v)
            cols = [(h * group + g) * HEAD_SIZE for g in range(group)]
            query = jnp.concatenate(
                [q[:, c : c + HEAD_SIZE].astype(jnp.float32) for c in cols], 0
            ).astype(jnp.bfloat16)
            scores = lax.dot_general(
                query, k, (((1,), (1,)), ((), ())), preferred_element_type=jnp.float32
            ) * (1.0 / HEAD_SIZE**0.5)
            scores = jnp.where(seen, scores, -1e30)
            top = jnp.max(scores, -1, keepdims=True)
            e = jnp.where(seen, jnp.exp(scores - top), 0.0)
            weights = (e / jnp.sum(e, -1, keepdims=True)).astype(jnp.bfloat16)
            out = jnp.dot(weights, v, preferred_element_type=jnp.float32)
            for g, c in enumerate(cols):
                here = slice(c, c + HEAD_SIZE)
                got = out[g * STEPS : (g + 1) * STEPS].astype(jnp.bfloat16)
                attended[:, here] = got
                mixed = residual[:, here].astype(jnp.float32) + got.astype(jnp.float32)
                squares += jnp.sum(mixed * mixed, -1, keepdims=True)
                sent[:, here] = (mixed * gain[:, here]).astype(jnp.bfloat16)
        sent[:, width:] = pair(squares)


def forward_kernel(blocks, workers, narrow, share, *refs):
    count = blocks * workers
    arrived, (held, gate, up), rest = refs[:blocks], refs[blocks : blocks + 3], refs[blocks + 3 :]
    outs, (x, sums, slots, sems) = rest[: -4], rest[-4:]
    me = lax.axis_index("wide") - count
    features = gate.shape[0]
    depth = held.shape[2]
    early, room = held.shape[0], slots.shape[0]
    total = features // depth
    half = features // narrow

    def stream(c):
        return fetches(share, c, (c - early) % room, gate, up, slots, sems)

    @pl.when(me >= 0)
    def _():
        for c in range(early, min(early + room, total)):
            for copy in stream(c):
                copy.start()
        lines, tails = [], []
        for d in range(share):
            part = lax.rem(lax.axis_index("parts") + d, share) if share > 1 else 0
            for block in arrived:
                for shift in range(workers):
                    owner = part * workers + lax.rem(me + shift, workers)
                    halves = [block[owner * narrow + n] for n in range(narrow)]
                    lines.append(
                        jnp.concatenate([h[:, :half] for h in halves], 1).astype(jnp.float32)
                    )
                    tails.append(sum(h[:, half:].astype(jnp.float32) for h in halves))
        pad = x.shape[0] - STEPS * count * share
        if pad:
            lines.append(jnp.zeros((pad, features), jnp.float32))
            tails.append(jnp.zeros((pad, TAIL), jnp.float32))
        x[...] = jnp.concatenate(lines, 0).astype(jnp.bfloat16)
        squares = jnp.sum(jnp.concatenate(tails, 0), -1, keepdims=True)
        r = lax.rsqrt(squares / D + EPS)
        for c in range(total):
            rows = x[:, c * depth : (c + 1) * depth]
            for m in range(2):
                if c >= early:
                    stream(c)[m].wait()
                block = held[c, m] if c < early else slots[(c - early) % room, m]
                product = jnp.dot(rows, block, preferred_element_type=jnp.float32)
                sums[m] = product if c == 0 else sums[m] + product
            if c >= early and c + room < total:
                for copy in stream(c + room):
                    copy.start()
        g, u = sums[0] * r, sums[1] * r
        hidden = (g / (1.0 + jnp.exp(-g)) * u).astype(jnp.bfloat16)
        for i in range(count):
            out = outs[(blocks - 1 - i // workers) * workers + i % workers]
            out[...] = hidden[i * STEPS : (i + 1) * STEPS]


def finish_kernel(blocks, workers, attended, *refs):
    results, (attended_out, out) = refs[:-2], refs[-2:]
    attended_out[...] = attended[...]
    if len(results) == 1:
        out[...] = results[0][...]
        return
    me = lax.axis_index("wide")
    columns = results[0].shape[1]

    @pl.when(me >= blocks * workers)
    def _():
        out[...] = jnp.zeros_like(out)

    for i, result in enumerate(results):
        b, shift = divmod(i, workers)

        @pl.when((me >= b * workers) & (me < (b + 1) * workers))
        def _():
            k = lax.rem(me - b * workers + workers - shift, workers)
            out[:, pl.ds(pl.multiple_of(k * columns, 128), columns)] = result[...]


def shards(queries, new_kv, keys, values, lengths, residual, gain, gate, up):
    wide = lax.axis_size("wide")
    narrow = lax.axis_size("narrow")
    serving = wide * 3 // 4
    workers = wide - serving
    blocks = serving // workers
    half = queries.shape[2]
    features, _, columns = gate.shape
    share = 1
    local = columns // share
    vmem = pl.BlockSpec(memory_space=pltpu.VMEM)
    hbm = pl.BlockSpec(memory_space=pltpu.HBM)
    owner = lax.axis_index("wide") < serving

    def in_hbm(a):
        return pltpu.with_memory_space_constraint(a, pltpu.HBM)

    gate = in_hbm(gate.reshape(features, columns))
    up = in_hbm(up.reshape(features, columns))
    operands = (
        lengths.reshape(1, 1),
        queries.reshape(STEPS, half),
        new_kv.reshape(STEPS, 2, -1),
        keys.reshape(keys.shape[1:]),
        values.reshape(values.shape[1:]),
        residual.reshape(STEPS, half),
        gain.reshape(1, half),
    )
    attended, sent = pl.pallas_call(
        functools.partial(attend_kernel, serving),
        out_shape=(
            pltpu.VMEM((STEPS, half), jnp.bfloat16),
            jax.ShapeDtypeStruct((STEPS, half + TAIL), jnp.bfloat16),
        ),
        in_specs=[hbm] * 7,
        out_specs=(vmem, vmem),
        scratch_shapes=[]
        + [(pltpu.SMEM if o.dtype == jnp.int32 else pltpu.VMEM)(o.shape, o.dtype) for o in operands]
        + [pltpu.SemaphoreType.DMA((7,))],
        compiler_params=pltpu.CompilerParams(vmem_limit_bytes=8 << 20),
    )(operands[0], *map(in_hbm, operands[1:]))

    groups = [
        [w * narrow + n for w in range(at, at + workers) for n in range(narrow)]
        for at in range(0, wide, workers)
    ]
    blank = pl.pallas_call(
        blank_kernel,
        out_shape=jax.ShapeDtypeStruct((workers * narrow, *sent.shape), jnp.bfloat16),
        out_specs=vmem,
        compiler_params=pltpu.CompilerParams(vmem_limit_bytes=8 << 20),
    )
    block = lax.cond(
        owner,
        lambda s: lax.all_gather(s, ("wide", "narrow"), axis=0, axis_index_groups=groups),
        lambda s: blank(),
        sent,
    )
    arrived = [
        lax.ppermute(block, "wide", [(b * workers + j, serving + j) for j in range(workers)])
        for b in range(blocks)
    ]
    early = min(EARLY, features // DEPTH - 1)
    held = pl.pallas_call(
        functools.partial(fetch_kernel, serving, share),
        out_shape=pltpu.VMEM((early, 2, DEPTH, local), jnp.bfloat16),
        in_specs=[pl.BlockSpec(memory_space=pl.ANY), hbm, hbm],
        out_specs=vmem,
        scratch_shapes=[pltpu.SemaphoreType.DMA((early, 2))],
        compiler_params=pltpu.CompilerParams(vmem_limit_bytes=4 << 20),
        cost_estimate=pl.CostEstimate(
            flops=0, bytes_accessed=early * 4 * DEPTH * local, transcendentals=0
        ),
    )(block, gate, up)
    padded = -(-STEPS * serving * share // 16) * 16
    hidden = pl.pallas_call(
        functools.partial(forward_kernel, blocks, workers, narrow, share),
        out_shape=[jax.ShapeDtypeStruct((STEPS, local), jnp.bfloat16)] * (serving * share),
        in_specs=[vmem] * (blocks + 1) + [hbm, hbm],
        out_specs=[vmem] * (serving * share),
        scratch_shapes=[
            pltpu.VMEM((padded, features), jnp.bfloat16),
            pltpu.VMEM((2, padded, local), jnp.float32),
            pltpu.VMEM((SLOTS, 2, DEPTH, local), jnp.bfloat16),
            pltpu.SemaphoreType.DMA((SLOTS, 2)),
        ],
        compiler_params=pltpu.CompilerParams(vmem_limit_bytes=20 << 20),
    )(*arrived, held, gate, up)
    back = [[None] * workers for _ in range(blocks)]
    for b in range(blocks):
        for s in range(workers):
            pairs = [(serving + k, b * workers + (k + s) % workers) for k in range(workers)]
            back[b][s] = lax.ppermute(hidden[(blocks - 1 - b) * workers + s], "wide", pairs)
    aligned = columns % 128 == 0
    if aligned:
        results = [r for some in back for r in some]
    else:
        me = lax.axis_index("wide")
        pieces = []
        for k in range(workers):
            piece = jnp.zeros((), jnp.bfloat16)
            for b in range(blocks):
                for s in range(workers):
                    mine = me == b * workers + (k + s) % workers
                    piece = jnp.where(mine, back[b][s], piece)
            pieces.append(piece)
        results = [jnp.concatenate(pieces, 1)]
    attended, activated = pl.pallas_call(
        functools.partial(finish_kernel, blocks, workers),
        out_shape=(
            jax.ShapeDtypeStruct((STEPS, half), jnp.bfloat16),
            jax.ShapeDtypeStruct((STEPS, workers * columns), jnp.bfloat16),
        ),
        in_specs=[vmem] * (1 + len(results)),
        out_specs=(vmem, vmem),
        compiler_params=pltpu.CompilerParams(vmem_limit_bytes=8 << 20),
    )(attended, *results)
    return attended.reshape(STEPS, 1, half), activated.reshape(STEPS, 1, -1)


def solution(mesh):
    rows = P(None, ("parts", "wide"), "narrow")
    placed = (
        rows,
        P(None, ("parts", "wide"), None, "narrow"),
        P(("parts", "wide"), "narrow", None, None),
        P(("parts", "wide"), "narrow", None, None),
        P(("parts", "wide")),
        rows,
        P("narrow"),
        P(None, "narrow", "wide"),
        P(None, "narrow", "wide"),
    )
    return jax.shard_map(
        shards, mesh=mesh, in_specs=placed, out_specs=(rows, rows), check_vma=False
    )
```

```python
import functools

import jax
import jax.numpy as jnp
from jax import lax
from jax.experimental import pallas as pl
from jax.experimental.pallas import tpu as pltpu
from jax.sharding import PartitionSpec as P

D = 4096
HEAD_SIZE = 128
STEPS = 2
TAIL = 128
EPS = 1e-05
EARLY = 2048
TILE = 256
SLOTS = 5


def pair(squares):
    high = squares.astype(jnp.bfloat16).astype(jnp.float32)
    lane = lax.broadcasted_iota(jnp.int32, (squares.shape[0], TAIL), 1)
    both = jnp.where(lane == 0, high, jnp.where(lane == 1, squares - high, 0.0))
    return both.astype(jnp.bfloat16)


def fetch_kernel(serving, _, gate, up, gate_held, up_held, sems):
    @pl.when(lax.axis_index("wide") >= serving)
    def _():
        here = pl.ds(0, gate_held.shape[0])
        copies = [
            pltpu.make_async_copy(gate.at[here], gate_held, sems.at[0]),
            pltpu.make_async_copy(up.at[here], up_held, sems.at[1]),
        ]
        for c in copies:
            c.start()
        for c in copies:
            c.wait()


def blank_kernel(out):
    out[...] = jnp.zeros_like(out)


def attend_kernel(serving, *refs):
    sources, (attended, sent), held, sems = refs[:7], refs[7:9], refs[9:16], refs[16]
    lengths, q, kv, keys, values, residual, gain = held
    owner = lax.axis_index("wide") < serving
    heads, hist, _ = keys.shape
    width = q.shape[1]
    group = width // (heads * HEAD_SIZE)

    @pl.when(jnp.logical_not(owner))
    def _():
        attended[...] = jnp.zeros_like(attended)
        sent[...] = jnp.zeros_like(sent)

    @pl.when(owner)
    def _():
        copies = [
            pltpu.make_async_copy(source, place, sems.at[i])
            for i, (source, place) in enumerate(zip(sources, held))
        ]
        for c in copies:
            c.start()
        for c in copies:
            c.wait()
        length = lengths[0, 0]
        slot = lax.broadcasted_iota(jnp.int32, (hist, HEAD_SIZE), 0)
        rows = group * STEPS
        place = lax.broadcasted_iota(jnp.int32, (rows, hist), 1)
        step = lax.broadcasted_iota(jnp.int32, (rows, hist), 0) % STEPS
        first = hist - STEPS
        seen = (place < length) | ((place >= first) & (place - first <= step))
        squares = jnp.zeros((STEPS, 1), jnp.float32)
        for h in range(heads):
            lanes = slice(h * HEAD_SIZE, (h + 1) * HEAD_SIZE)
            k, v = keys[h], values[h]
            for t in range(STEPS):
                k = jnp.where(slot == first + t, kv[t, 0:1, lanes], k)
                v = jnp.where(slot == first + t, kv[t, 1:2, lanes], v)
            cols = [(h * group + g) * HEAD_SIZE for g in range(group)]
            query = jnp.concatenate(
                [q[:, c : c + HEAD_SIZE].astype(jnp.float32) for c in cols], 0
            ).astype(jnp.bfloat16)
            scores = lax.dot_general(
                query, k, (((1,), (1,)), ((), ())), preferred_element_type=jnp.float32
            ) * (1.0 / HEAD_SIZE**0.5)
            scores = jnp.where(seen, scores, -1e30)
            top = jnp.max(scores, -1, keepdims=True)
            e = jnp.where(seen, jnp.exp(scores - top), 0.0)
            weights = (e / jnp.sum(e, -1, keepdims=True)).astype(jnp.bfloat16)
            out = jnp.dot(weights, v, preferred_element_type=jnp.float32)
            for g, c in enumerate(cols):
                here = slice(c, c + HEAD_SIZE)
                got = out[g * STEPS : (g + 1) * STEPS].astype(jnp.bfloat16)
                attended[:, here] = got
                mixed = residual[:, here].astype(jnp.float32) + got.astype(jnp.float32)
                squares += jnp.sum(mixed * mixed, -1, keepdims=True)
                sent[:, here] = (mixed * gain[:, here]).astype(jnp.bfloat16)
        sent[:, width:] = pair(squares)


def forward_kernel(blocks, workers, narrow, *refs):
    count = blocks * workers
    arrived, (gate_held, up_held, gate, up), rest = refs[:blocks], refs[blocks:][:4], refs[blocks + 4 :]
    outs, (x, slots, sems) = rest[:-3], rest[-3:]
    me = lax.axis_index("wide") - count
    features, columns = gate.shape
    half = features // narrow
    early = gate_held.shape[0]
    room, _, late, tile = slots.shape
    total = columns // tile

    def stream(j):
        s = j % room
        here = (pl.ds(early, late), pl.ds(j * tile, tile))
        return [
            pltpu.make_async_copy(m.at[here], slots.at[s, i], sems.at[s, i])
            for i, m in enumerate((gate, up))
        ]

    @pl.when(me >= 0)
    def _():
        for j in range(min(room, total)):
            for copy in stream(j):
                copy.start()
        lines, tails = [], []
        for block in arrived:
            for shift in range(workers):
                owner = lax.rem(me + shift, workers)
                halves = [block[owner * narrow + n] for n in range(narrow)]
                lines.append(
                    jnp.concatenate([h[:, :half] for h in halves], 1).astype(jnp.float32)
                )
                tails.append(sum(h[:, half:].astype(jnp.float32) for h in halves))
        pad = x.shape[0] - STEPS * count
        if pad:
            lines.append(jnp.zeros((pad, features), jnp.float32))
            tails.append(jnp.zeros((pad, TAIL), jnp.float32))
        x[...] = jnp.concatenate(lines, 0).astype(jnp.bfloat16)
        squares = jnp.sum(jnp.concatenate(tails, 0), -1, keepdims=True)
        r = lax.rsqrt(squares / D + EPS)
        for j in range(total):
            here = slice(j * tile, (j + 1) * tile)
            sums = [
                jnp.dot(x[:, :early], held[:, here], preferred_element_type=jnp.float32)
                for held in (gate_held, up_held)
            ]
            for i, copy in enumerate(stream(j)):
                copy.wait()
                sums[i] += jnp.dot(
                    x[:, early:], slots[j % room, i], preferred_element_type=jnp.float32
                )
            if j + room < total:
                for copy in stream(j + room):
                    copy.start()
            g, u = sums[0] * r, sums[1] * r
            hidden = (g / (1.0 + jnp.exp(-g)) * u).astype(jnp.bfloat16)
            for i in range(count):
                out = outs[(blocks - 1 - i // workers) * workers + i % workers]
                out[:, here] = hidden[i * STEPS : (i + 1) * STEPS]


def finish_kernel(blocks, workers, attended, *refs):
    results, (attended_out, out) = refs[:-2], refs[-2:]
    attended_out[...] = attended[...]
    if len(results) == 1:
        out[...] = results[0][...]
        return
    me = lax.axis_index("wide")
    columns = results[0].shape[1]

    @pl.when(me >= blocks * workers)
    def _():
        out[...] = jnp.zeros_like(out)

    for i, result in enumerate(results):
        b, shift = divmod(i, workers)

        @pl.when((me >= b * workers) & (me < (b + 1) * workers))
        def _():
            k = lax.rem(me - b * workers + workers - shift, workers)
            out[:, pl.ds(pl.multiple_of(k * columns, 128), columns)] = result[...]


def shards(queries, new_kv, keys, values, lengths, residual, gain, gate, up):
    wide = lax.axis_size("wide")
    narrow = lax.axis_size("narrow")
    serving = wide * 3 // 4
    workers = wide - serving
    blocks = serving // workers
    half = queries.shape[2]
    features, _, columns = gate.shape
    vmem = pl.BlockSpec(memory_space=pltpu.VMEM)
    hbm = pl.BlockSpec(memory_space=pltpu.HBM)
    owner = lax.axis_index("wide") < serving

    def in_hbm(a):
        return pltpu.with_memory_space_constraint(a, pltpu.HBM)

    gate = in_hbm(gate.reshape(features, columns))
    up = in_hbm(up.reshape(features, columns))
    operands = (
        lengths.reshape(1, 1),
        queries.reshape(STEPS, half),
        new_kv.reshape(STEPS, 2, -1),
        keys.reshape(keys.shape[1:]),
        values.reshape(values.shape[1:]),
        residual.reshape(STEPS, half),
        gain.reshape(1, half),
    )
    attended, sent = pl.pallas_call(
        functools.partial(attend_kernel, serving),
        out_shape=(
            pltpu.VMEM((STEPS, half), jnp.bfloat16),
            jax.ShapeDtypeStruct((STEPS, half + TAIL), jnp.bfloat16),
        ),
        in_specs=[hbm] * 7,
        out_specs=(vmem, vmem),
        scratch_shapes=[]
        + [(pltpu.SMEM if o.dtype == jnp.int32 else pltpu.VMEM)(o.shape, o.dtype) for o in operands]
        + [pltpu.SemaphoreType.DMA((7,))],
        compiler_params=pltpu.CompilerParams(vmem_limit_bytes=8 << 20),
    )(operands[0], *map(in_hbm, operands[1:]))

    groups = [
        [w * narrow + n for w in range(at, at + workers) for n in range(narrow)]
        for at in range(0, wide, workers)
    ]
    blank = pl.pallas_call(
        blank_kernel,
        out_shape=jax.ShapeDtypeStruct((workers * narrow, *sent.shape), jnp.bfloat16),
        out_specs=vmem,
        compiler_params=pltpu.CompilerParams(vmem_limit_bytes=8 << 20),
    )
    block = lax.cond(
        owner,
        lambda s: lax.all_gather(s, ("wide", "narrow"), axis=0, axis_index_groups=groups),
        lambda s: blank(),
        sent,
    )
    arrived = [
        lax.ppermute(block, "wide", [(b * workers + j, serving + j) for j in range(workers)])
        for b in range(blocks)
    ]
    early = min(EARLY, features // 2)
    held = pl.pallas_call(
        functools.partial(fetch_kernel, serving),
        out_shape=[pltpu.VMEM((early, columns), jnp.bfloat16)] * 2,
        in_specs=[pl.BlockSpec(memory_space=pl.ANY), hbm, hbm],
        out_specs=[vmem] * 2,
        scratch_shapes=[pltpu.SemaphoreType.DMA((2,))],
        compiler_params=pltpu.CompilerParams(vmem_limit_bytes=4 << 20),
        cost_estimate=pl.CostEstimate(
            flops=0, bytes_accessed=early * 4 * columns, transcendentals=0
        ),
    )(block, gate, up)
    padded = -(-STEPS * serving // 16) * 16
    tile = TILE if columns % TILE == 0 else columns
    slots = min(SLOTS, columns // tile)
    hidden = pl.pallas_call(
        functools.partial(forward_kernel, blocks, workers, narrow),
        out_shape=[jax.ShapeDtypeStruct((STEPS, columns), jnp.bfloat16)] * serving,
        in_specs=[vmem] * (blocks + 2) + [hbm, hbm],
        out_specs=[vmem] * serving,
        scratch_shapes=[
            pltpu.VMEM((padded, features), jnp.bfloat16),
            pltpu.VMEM((slots, 2, features - early, tile), jnp.bfloat16),
            pltpu.SemaphoreType.DMA((slots, 2)),
        ],
        compiler_params=pltpu.CompilerParams(vmem_limit_bytes=20 << 20),
    )(*arrived, *held, gate, up)
    back = [[None] * workers for _ in range(blocks)]
    for b in range(blocks):
        for s in range(workers):
            pairs = [(serving + k, b * workers + (k + s) % workers) for k in range(workers)]
            back[b][s] = lax.ppermute(hidden[(blocks - 1 - b) * workers + s], "wide", pairs)
    aligned = columns % 128 == 0
    if aligned:
        results = [r for some in back for r in some]
    else:
        me = lax.axis_index("wide")
        pieces = []
        for k in range(workers):
            piece = jnp.zeros((), jnp.bfloat16)
            for b in range(blocks):
                for s in range(workers):
                    mine = me == b * workers + (k + s) % workers
                    piece = jnp.where(mine, back[b][s], piece)
            pieces.append(piece)
        results = [jnp.concatenate(pieces, 1)]
    attended, activated = pl.pallas_call(
        functools.partial(finish_kernel, blocks, workers),
        out_shape=(
            jax.ShapeDtypeStruct((STEPS, half), jnp.bfloat16),
            jax.ShapeDtypeStruct((STEPS, workers * columns), jnp.bfloat16),
        ),
        in_specs=[vmem] * (1 + len(results)),
        out_specs=(vmem, vmem),
        compiler_params=pltpu.CompilerParams(vmem_limit_bytes=8 << 20),
    )(attended, *results)
    return attended.reshape(STEPS, 1, half), activated.reshape(STEPS, 1, -1)


def solution(mesh):
    rows = P(None, ("parts", "wide"), "narrow")
    placed = (
        rows,
        P(None, ("parts", "wide"), None, "narrow"),
        P(("parts", "wide"), "narrow", None, None),
        P(("parts", "wide"), "narrow", None, None),
        P(("parts", "wide")),
        rows,
        P("narrow"),
        P(None, "narrow", "wide"),
        P(None, "narrow", "wide"),
    )
    return jax.shard_map(
        shards, mesh=mesh, in_specs=placed, out_specs=(rows, rows), check_vma=False
    )
```

```python
import functools

import jax
import jax.numpy as jnp
from jax import lax
from jax.experimental import pallas as pl
from jax.experimental.pallas import tpu as pltpu
from jax.sharding import PartitionSpec as P

D = 4096
HEAD_SIZE = 128
STEPS = 2
TAIL = 128
EPS = 1e-05
EARLY = 2048
DEPTH = 512
SLOTS = 2
WIDTH = 512
SHARES = (4, 2, 1, 0)


def pair(squares):
    high = squares.astype(jnp.bfloat16).astype(jnp.float32)
    lane = lax.broadcasted_iota(jnp.int32, (squares.shape[0], TAIL), 1)
    both = jnp.where(lane == 0, high, jnp.where(lane == 1, squares - high, 0.0))
    return both.astype(jnp.bfloat16)


def fetch_kernel(serving, _, gate, up, gate_held, up_held, sems):
    @pl.when(lax.axis_index("wide") >= serving)
    def _():
        here = pl.ds(0, gate_held.shape[0])
        copies = [
            pltpu.make_async_copy(gate.at[here], gate_held, sems.at[0]),
            pltpu.make_async_copy(up.at[here], up_held, sems.at[1]),
        ]
        for c in copies:
            c.start()
        for c in copies:
            c.wait()


def blank_kernel(out):
    out[...] = jnp.zeros_like(out)


def attend_kernel(serving, *refs):
    sources, (attended, sent), held, sems = refs[:7], refs[7:9], refs[9:16], refs[16]
    lengths, q, kv, keys, values, residual, gain = held
    owner = lax.axis_index("wide") < serving
    heads, hist, _ = keys.shape
    width = q.shape[1]
    group = width // (heads * HEAD_SIZE)

    @pl.when(jnp.logical_not(owner))
    def _():
        attended[...] = jnp.zeros_like(attended)
        sent[...] = jnp.zeros_like(sent)

    @pl.when(owner)
    def _():
        copies = [
            pltpu.make_async_copy(source, place, sems.at[i])
            for i, (source, place) in enumerate(zip(sources, held))
        ]
        for c in copies:
            c.start()
        for c in copies:
            c.wait()
        length = lengths[0, 0]
        slot = lax.broadcasted_iota(jnp.int32, (hist, HEAD_SIZE), 0)
        rows = group * STEPS
        place = lax.broadcasted_iota(jnp.int32, (rows, hist), 1)
        step = lax.broadcasted_iota(jnp.int32, (rows, hist), 0) % STEPS
        first = hist - STEPS
        seen = (place < length) | ((place >= first) & (place - first <= step))
        squares = jnp.zeros((STEPS, 1), jnp.float32)
        for h in range(heads):
            lanes = slice(h * HEAD_SIZE, (h + 1) * HEAD_SIZE)
            k, v = keys[h], values[h]
            for t in range(STEPS):
                k = jnp.where(slot == first + t, kv[t, 0:1, lanes], k)
                v = jnp.where(slot == first + t, kv[t, 1:2, lanes], v)
            cols = [(h * group + g) * HEAD_SIZE for g in range(group)]
            query = jnp.concatenate(
                [q[:, c : c + HEAD_SIZE].astype(jnp.float32) for c in cols], 0
            ).astype(jnp.bfloat16)
            scores = lax.dot_general(
                query, k, (((1,), (1,)), ((), ())), preferred_element_type=jnp.float32
            ) * (1.0 / HEAD_SIZE**0.5)
            scores = jnp.where(seen, scores, -1e30)
            top = jnp.max(scores, -1, keepdims=True)
            e = jnp.where(seen, jnp.exp(scores - top), 0.0)
            weights = (e / jnp.sum(e, -1, keepdims=True)).astype(jnp.bfloat16)
            out = jnp.dot(weights, v, preferred_element_type=jnp.float32)
            for g, c in enumerate(cols):
                here = slice(c, c + HEAD_SIZE)
                got = out[g * STEPS : (g + 1) * STEPS].astype(jnp.bfloat16)
                attended[:, here] = got
                mixed = residual[:, here].astype(jnp.float32) + got.astype(jnp.float32)
                squares += jnp.sum(mixed * mixed, -1, keepdims=True)
                sent[:, here] = (mixed * gain[:, here]).astype(jnp.bfloat16)
        sent[:, width:] = pair(squares)


def forward_kernel(blocks, workers, narrow, *refs):
    count = blocks * workers
    arrived, (gate_held, up_held, gate, up), rest = refs[:blocks], refs[blocks:][:4], refs[blocks + 4 :]
    outs, (x, sums, slots, sems) = rest[:-4], rest[-4:]
    me = lax.axis_index("wide") - count
    features, columns = gate.shape
    half = features // narrow
    early = gate_held.shape[0]
    room, _, depth, _ = slots.shape
    total = (features - early) // depth
    width = WIDTH if columns % WIDTH == 0 else columns
    spans = [slice(at, at + width) for at in range(0, columns, width)]

    def stream(j):
        s = j % room
        here = pl.ds(early + j * depth, depth)
        return [
            pltpu.make_async_copy(m.at[here], slots.at[s, i], sems.at[s, i])
            for i, m in enumerate((gate, up))
        ]

    @pl.when(me >= 0)
    def _():
        for j in range(min(room, total)):
            for copy in stream(j):
                copy.start()
        lines, tails = [], []
        for block in arrived:
            for shift in range(workers):
                owner = lax.rem(me + shift, workers)
                halves = [block[owner * narrow + n] for n in range(narrow)]
                lines.append(
                    jnp.concatenate([h[:, :half] for h in halves], 1).astype(jnp.float32)
                )
                tails.append(sum(h[:, half:].astype(jnp.float32) for h in halves))
        pad = x.shape[0] - STEPS * count
        if pad:
            lines.append(jnp.zeros((pad, features), jnp.float32))
            tails.append(jnp.zeros((pad, TAIL), jnp.float32))
        x[...] = jnp.concatenate(lines, 0).astype(jnp.bfloat16)
        squares = jnp.sum(jnp.concatenate(tails, 0), -1, keepdims=True)
        r = lax.rsqrt(squares / D + EPS)
        taken = set()

        def add(i, here, rows, block):
            product = jnp.dot(rows, block, preferred_element_type=jnp.float32)
            first = (i, here.start) not in taken
            taken.add((i, here.start))
            sums[i, :, here] = product if first else sums[i, :, here] + product

        waiting = list(spans)
        for j in range(total):
            for _ in range(-(-len(spans) * SHARES[min(j, len(SHARES) - 1)] // sum(SHARES))):
                if waiting:
                    here = waiting.pop(0)
                    for i, held in enumerate((gate_held, up_held)):
                        add(i, here, x[:, :early], held[:, here])
            if j == total - 1:
                for here in waiting:
                    for i, held in enumerate((gate_held, up_held)):
                        add(i, here, x[:, :early], held[:, here])
            for copy in stream(j):
                copy.wait()
            at = early + j * depth
            for here in spans:
                for i in range(2):
                    add(i, here, x[:, at : at + depth], slots[j % room, i, :, here])
            if j + room < total:
                for copy in stream(j + room):
                    copy.start()
        g, u = sums[0] * r, sums[1] * r
        hidden = (g / (1.0 + jnp.exp(-g)) * u).astype(jnp.bfloat16)
        for i in range(count):
            out = outs[(blocks - 1 - i // workers) * workers + i % workers]
            out[...] = hidden[i * STEPS : (i + 1) * STEPS]


def finish_kernel(blocks, workers, attended, *refs):
    results, (attended_out, out) = refs[:-2], refs[-2:]
    attended_out[...] = attended[...]
    if len(results) == 1:
        out[...] = results[0][...]
        return
    me = lax.axis_index("wide")
    columns = results[0].shape[1]

    @pl.when(me >= blocks * workers)
    def _():
        out[...] = jnp.zeros_like(out)

    for i, result in enumerate(results):
        b, shift = divmod(i, workers)

        @pl.when((me >= b * workers) & (me < (b + 1) * workers))
        def _():
            k = lax.rem(me - b * workers + workers - shift, workers)
            out[:, pl.ds(pl.multiple_of(k * columns, 128), columns)] = result[...]


def shards(queries, new_kv, keys, values, lengths, residual, gain, gate, up):
    wide = lax.axis_size("wide")
    narrow = lax.axis_size("narrow")
    serving = wide * 3 // 4
    workers = wide - serving
    blocks = serving // workers
    half = queries.shape[2]
    features, _, columns = gate.shape
    vmem = pl.BlockSpec(memory_space=pltpu.VMEM)
    hbm = pl.BlockSpec(memory_space=pltpu.HBM)
    owner = lax.axis_index("wide") < serving

    def in_hbm(a):
        return pltpu.with_memory_space_constraint(a, pltpu.HBM)

    gate = in_hbm(gate.reshape(features, columns))
    up = in_hbm(up.reshape(features, columns))
    operands = (
        lengths.reshape(1, 1),
        queries.reshape(STEPS, half),
        new_kv.reshape(STEPS, 2, -1),
        keys.reshape(keys.shape[1:]),
        values.reshape(values.shape[1:]),
        residual.reshape(STEPS, half),
        gain.reshape(1, half),
    )
    attended, sent = pl.pallas_call(
        functools.partial(attend_kernel, serving),
        out_shape=(
            pltpu.VMEM((STEPS, half), jnp.bfloat16),
            jax.ShapeDtypeStruct((STEPS, half + TAIL), jnp.bfloat16),
        ),
        in_specs=[hbm] * 7,
        out_specs=(vmem, vmem),
        scratch_shapes=[]
        + [(pltpu.SMEM if o.dtype == jnp.int32 else pltpu.VMEM)(o.shape, o.dtype) for o in operands]
        + [pltpu.SemaphoreType.DMA((7,))],
        compiler_params=pltpu.CompilerParams(vmem_limit_bytes=8 << 20),
    )(operands[0], *map(in_hbm, operands[1:]))

    groups = [
        [w * narrow + n for w in range(at, at + workers) for n in range(narrow)]
        for at in range(0, wide, workers)
    ]
    blank = pl.pallas_call(
        blank_kernel,
        out_shape=jax.ShapeDtypeStruct((workers * narrow, *sent.shape), jnp.bfloat16),
        out_specs=vmem,
        compiler_params=pltpu.CompilerParams(vmem_limit_bytes=8 << 20),
    )
    block = lax.cond(
        owner,
        lambda s: lax.all_gather(s, ("wide", "narrow"), axis=0, axis_index_groups=groups),
        lambda s: blank(),
        sent,
    )
    arrived = [
        lax.ppermute(block, "wide", [(b * workers + j, serving + j) for j in range(workers)])
        for b in range(blocks)
    ]
    early = min(EARLY, features // 2)
    held = pl.pallas_call(
        functools.partial(fetch_kernel, serving),
        out_shape=[pltpu.VMEM((early, columns), jnp.bfloat16)] * 2,
        in_specs=[pl.BlockSpec(memory_space=pl.ANY), hbm, hbm],
        out_specs=[vmem] * 2,
        scratch_shapes=[pltpu.SemaphoreType.DMA((2,))],
        compiler_params=pltpu.CompilerParams(vmem_limit_bytes=4 << 20),
        cost_estimate=pl.CostEstimate(
            flops=0, bytes_accessed=early * 4 * columns, transcendentals=0
        ),
    )(block, gate, up)
    padded = -(-STEPS * serving // 16) * 16
    depth = min(DEPTH, features - early)
    hidden = pl.pallas_call(
        functools.partial(forward_kernel, blocks, workers, narrow),
        out_shape=[jax.ShapeDtypeStruct((STEPS, columns), jnp.bfloat16)] * serving,
        in_specs=[vmem] * (blocks + 2) + [hbm, hbm],
        out_specs=[vmem] * serving,
        scratch_shapes=[
            pltpu.VMEM((padded, features), jnp.bfloat16),
            pltpu.VMEM((2, padded, columns), jnp.float32),
            pltpu.VMEM((SLOTS, 2, depth, columns), jnp.bfloat16),
            pltpu.SemaphoreType.DMA((SLOTS, 2)),
        ],
        compiler_params=pltpu.CompilerParams(vmem_limit_bytes=16 << 20),
    )(*arrived, *held, gate, up)
    back = [[None] * workers for _ in range(blocks)]
    for b in range(blocks):
        for s in range(workers):
            pairs = [(serving + k, b * workers + (k + s) % workers) for k in range(workers)]
            back[b][s] = lax.ppermute(hidden[(blocks - 1 - b) * workers + s], "wide", pairs)
    aligned = columns % 128 == 0
    if aligned:
        results = [r for some in back for r in some]
    else:
        me = lax.axis_index("wide")
        pieces = []
        for k in range(workers):
            piece = jnp.zeros((), jnp.bfloat16)
            for b in range(blocks):
                for s in range(workers):
                    mine = me == b * workers + (k + s) % workers
                    piece = jnp.where(mine, back[b][s], piece)
            pieces.append(piece)
        results = [jnp.concatenate(pieces, 1)]
    attended, activated = pl.pallas_call(
        functools.partial(finish_kernel, blocks, workers),
        out_shape=(
            jax.ShapeDtypeStruct((STEPS, half), jnp.bfloat16),
            jax.ShapeDtypeStruct((STEPS, workers * columns), jnp.bfloat16),
        ),
        in_specs=[vmem] * (1 + len(results)),
        out_specs=(vmem, vmem),
        compiler_params=pltpu.CompilerParams(vmem_limit_bytes=8 << 20),
    )(attended, *results)
    return attended.reshape(STEPS, 1, half), activated.reshape(STEPS, 1, -1)


def solution(mesh):
    rows = P(None, ("parts", "wide"), "narrow")
    placed = (
        rows,
        P(None, ("parts", "wide"), None, "narrow"),
        P(("parts", "wide"), "narrow", None, None),
        P(("parts", "wide"), "narrow", None, None),
        P(("parts", "wide")),
        rows,
        P("narrow"),
        P(None, "narrow", "wide"),
        P(None, "narrow", "wide"),
    )
    return jax.shard_map(
        shards, mesh=mesh, in_specs=placed, out_specs=(rows, rows), check_vma=False
    )
```

```python
import functools

import jax
import jax.numpy as jnp
from jax import lax
from jax.experimental import pallas as pl
from jax.experimental.pallas import tpu as pltpu
from jax.sharding import PartitionSpec as P

D = 4096
HEAD_SIZE = 128
STEPS = 2
TAIL = 128
EPS = 1e-05
EARLY = 1792
DEPTH = 512
SHORT = 256
SLOTS = 3
WIDTH = 512
SHARES = (3, 2, 1, 1)


def pair(squares):
    high = squares.astype(jnp.bfloat16).astype(jnp.float32)
    lane = lax.broadcasted_iota(jnp.int32, (squares.shape[0], TAIL), 1)
    both = jnp.where(lane == 0, high, jnp.where(lane == 1, squares - high, 0.0))
    return both.astype(jnp.bfloat16)


def fetch_kernel(serving, _, gate, up, gate_held, up_held, sems):
    @pl.when(lax.axis_index("wide") >= serving)
    def _():
        here = pl.ds(0, gate_held.shape[0])
        copies = [
            pltpu.make_async_copy(gate.at[here], gate_held, sems.at[0]),
            pltpu.make_async_copy(up.at[here], up_held, sems.at[1]),
        ]
        for c in copies:
            c.start()
        for c in copies:
            c.wait()


def blank_kernel(*outs):
    for out in outs:
        out[...] = jnp.zeros_like(out)


def attend_kernel(*refs):
    sources, (attended, sent), held, sems = refs[:7], refs[7:9], refs[9:16], refs[16]
    lengths, q, kv, keys, values, residual, gain = held
    heads, hist, _ = keys.shape
    width = q.shape[1]
    group = width // (heads * HEAD_SIZE)
    copies = [
        pltpu.make_async_copy(source, place, sems.at[i])
        for i, (source, place) in enumerate(zip(sources, held))
    ]
    for c in copies:
        c.start()
    for c in copies:
        c.wait()
    length = lengths[0, 0]
    slot = lax.broadcasted_iota(jnp.int32, (hist, HEAD_SIZE), 0)
    rows = group * STEPS
    place = lax.broadcasted_iota(jnp.int32, (rows, hist), 1)
    step = lax.broadcasted_iota(jnp.int32, (rows, hist), 0) % STEPS
    first = hist - STEPS
    seen = (place < length) | ((place >= first) & (place - first <= step))
    squares = jnp.zeros((STEPS, 1), jnp.float32)
    for h in range(heads):
        lanes = slice(h * HEAD_SIZE, (h + 1) * HEAD_SIZE)
        k, v = keys[h], values[h]
        for t in range(STEPS):
            k = jnp.where(slot == first + t, kv[t, 0:1, lanes], k)
            v = jnp.where(slot == first + t, kv[t, 1:2, lanes], v)
        cols = [(h * group + g) * HEAD_SIZE for g in range(group)]
        query = jnp.concatenate(
            [q[:, c : c + HEAD_SIZE].astype(jnp.float32) for c in cols], 0
        ).astype(jnp.bfloat16)
        scores = lax.dot_general(
            query, k, (((1,), (1,)), ((), ())), preferred_element_type=jnp.float32
        ) * (1.0 / HEAD_SIZE**0.5)
        scores = jnp.where(seen, scores, -1e30)
        top = jnp.max(scores, -1, keepdims=True)
        e = jnp.where(seen, jnp.exp(scores - top), 0.0)
        weights = (e / jnp.sum(e, -1, keepdims=True)).astype(jnp.bfloat16)
        out = jnp.dot(weights, v, preferred_element_type=jnp.float32)
        for g, c in enumerate(cols):
            here = slice(c, c + HEAD_SIZE)
            got = out[g * STEPS : (g + 1) * STEPS].astype(jnp.bfloat16)
            attended[:, here] = got
            mixed = residual[:, here].astype(jnp.float32) + got.astype(jnp.float32)
            squares += jnp.sum(mixed * mixed, -1, keepdims=True)
            sent[:, here] = (mixed * gain[:, here]).astype(jnp.bfloat16)
    sent[:, width:] = pair(squares)


def forward_kernel(blocks, workers, narrow, *refs):
    count = blocks * workers
    arrived, (gate_held, up_held, gate, up), rest = refs[:blocks], refs[blocks:][:4], refs[blocks + 4 :]
    outs, (x, sums, slots, sems) = rest[:-4], rest[-4:]
    me = lax.axis_index("wide") - count
    features, columns = gate.shape
    half = features // narrow
    early = gate_held.shape[0]
    room, _, depth, _ = slots.shape
    blocks_at = [early]
    while features - blocks_at[-1] > 2 * depth:
        blocks_at.append(blocks_at[-1] + depth)
    blocks_at += range(blocks_at[-1] + SHORT, features + 1, SHORT)
    total = len(blocks_at) - 1
    width = WIDTH if columns % WIDTH == 0 else columns
    spans = [slice(at, at + width) for at in range(0, columns, width)]

    def stream(j):
        s = j % room
        at, size = blocks_at[j], blocks_at[j + 1] - blocks_at[j]
        here, there = pl.ds(at, size), pl.ds(0, size)
        return [
            pltpu.make_async_copy(m.at[here], slots.at[s, i, there], sems.at[s, i])
            for i, m in enumerate((gate, up))
        ]

    @pl.when(me >= 0)
    def _():
        for j in range(min(room, total)):
            for copy in stream(j):
                copy.start()
        lines, tails = [], []
        for block in arrived:
            for shift in range(workers):
                owner = lax.rem(me + shift, workers)
                halves = [block[owner * narrow + n] for n in range(narrow)]
                lines.append(
                    jnp.concatenate([h[:, :half] for h in halves], 1).astype(jnp.float32)
                )
                tails.append(sum(h[:, half:].astype(jnp.float32) for h in halves))
        pad = x.shape[0] - STEPS * count
        if pad:
            lines.append(jnp.zeros((pad, features), jnp.float32))
            tails.append(jnp.zeros((pad, TAIL), jnp.float32))
        x[...] = jnp.concatenate(lines, 0).astype(jnp.bfloat16)
        squares = jnp.sum(jnp.concatenate(tails, 0), -1, keepdims=True)
        r = lax.rsqrt(squares / D + EPS)
        taken = set()

        def add(i, here, rows, block):
            product = jnp.dot(rows, block, preferred_element_type=jnp.float32)
            first = (i, here.start) not in taken
            taken.add((i, here.start))
            sums[i, :, here] = product if first else sums[i, :, here] + product

        waiting = list(spans)
        for j in range(total):
            share = SHARES[j] if j < len(SHARES) else 0
            for _ in range(-(-len(spans) * share // sum(SHARES))):
                if waiting:
                    here = waiting.pop(0)
                    for i, held in enumerate((gate_held, up_held)):
                        add(i, here, x[:, :early], held[:, here])
            if j == total - 1:
                for here in waiting:
                    for i, held in enumerate((gate_held, up_held)):
                        add(i, here, x[:, :early], held[:, here])
            for copy in stream(j):
                copy.wait()
            at, end = blocks_at[j], blocks_at[j + 1]
            for here in spans:
                for i in range(2):
                    add(i, here, x[:, at:end], slots[j % room, i, : end - at, here])
            if j + room < total:
                for copy in stream(j + room):
                    copy.start()
        g, u = sums[0] * r, sums[1] * r
        hidden = (g / (1.0 + jnp.exp(-g)) * u).astype(jnp.bfloat16)
        for i in range(count):
            out = outs[(blocks - 1 - i // workers) * workers + i % workers]
            out[...] = hidden[i * STEPS : (i + 1) * STEPS]


def finish_kernel(blocks, workers, attended, *refs):
    results, (attended_out, out) = refs[:-2], refs[-2:]
    attended_out[...] = attended[...]
    if len(results) == 1:
        out[...] = results[0][...]
        return
    me = lax.axis_index("wide")
    columns = results[0].shape[1]

    @pl.when(me >= blocks * workers)
    def _():
        out[...] = jnp.zeros_like(out)

    for i, result in enumerate(results):
        b, shift = divmod(i, workers)

        @pl.when((me >= b * workers) & (me < (b + 1) * workers))
        def _():
            k = lax.rem(me - b * workers + workers - shift, workers)
            out[:, pl.ds(pl.multiple_of(k * columns, 128), columns)] = result[...]


def shards(queries, new_kv, keys, values, lengths, residual, gain, gate, up):
    wide = lax.axis_size("wide")
    narrow = lax.axis_size("narrow")
    serving = wide * 3 // 4
    workers = wide - serving
    blocks = serving // workers
    half = queries.shape[2]
    features, _, columns = gate.shape
    vmem = pl.BlockSpec(memory_space=pltpu.VMEM)
    hbm = pl.BlockSpec(memory_space=pltpu.HBM)
    owner = lax.axis_index("wide") < serving

    def in_hbm(a):
        return pltpu.with_memory_space_constraint(a, pltpu.HBM)

    gate = in_hbm(gate.reshape(features, columns))
    up = in_hbm(up.reshape(features, columns))
    operands = (
        lengths.reshape(1, 1),
        queries.reshape(STEPS, half),
        new_kv.reshape(STEPS, 2, -1),
        keys.reshape(keys.shape[1:]),
        values.reshape(values.shape[1:]),
        residual.reshape(STEPS, half),
        gain.reshape(1, half),
    )
    groups = [
        [w * narrow + n for w in range(at, at + workers) for n in range(narrow)]
        for at in range(0, wide, workers)
    ]
    shapes = (
        jax.ShapeDtypeStruct((STEPS, half), jnp.bfloat16),
        jax.ShapeDtypeStruct((workers * narrow, STEPS, half + TAIL), jnp.bfloat16),
    )

    def serve(*operands):
        attended, sent = pl.pallas_call(
            attend_kernel,
            out_shape=(shapes[0], jax.ShapeDtypeStruct(shapes[1].shape[1:], jnp.bfloat16)),
            in_specs=[hbm] * 7,
            out_specs=(vmem, vmem),
            scratch_shapes=[
                (pltpu.SMEM if o.dtype == jnp.int32 else pltpu.VMEM)(o.shape, o.dtype)
                for o in operands
            ]
            + [pltpu.SemaphoreType.DMA((7,))],
            compiler_params=pltpu.CompilerParams(vmem_limit_bytes=8 << 20),
        )(operands[0], *map(in_hbm, operands[1:]))
        gathered = lax.all_gather(sent, ("wide", "narrow"), axis=0, axis_index_groups=groups)
        return attended, gathered

    def rest(*operands):
        return pl.pallas_call(
            blank_kernel,
            out_shape=shapes,
            out_specs=(vmem, vmem),
            compiler_params=pltpu.CompilerParams(vmem_limit_bytes=8 << 20),
        )()

    attended, block = lax.cond(owner, serve, rest, *operands)
    arrived = [
        lax.ppermute(block, "wide", [(b * workers + j, serving + j) for j in range(workers)])
        for b in range(blocks)
    ]
    early = min(EARLY, features // 2)
    held = pl.pallas_call(
        functools.partial(fetch_kernel, serving),
        out_shape=[pltpu.VMEM((early, columns), jnp.bfloat16)] * 2,
        in_specs=[pl.BlockSpec(memory_space=pl.ANY), hbm, hbm],
        out_specs=[vmem] * 2,
        scratch_shapes=[pltpu.SemaphoreType.DMA((2,))],
        compiler_params=pltpu.CompilerParams(vmem_limit_bytes=4 << 20),
        cost_estimate=pl.CostEstimate(
            flops=0, bytes_accessed=early * 4 * columns, transcendentals=0
        ),
    )(block, gate, up)
    padded = -(-STEPS * serving // 16) * 16
    depth = min(DEPTH, features - early)
    hidden = pl.pallas_call(
        functools.partial(forward_kernel, blocks, workers, narrow),
        out_shape=[jax.ShapeDtypeStruct((STEPS, columns), jnp.bfloat16)] * serving,
        in_specs=[vmem] * (blocks + 2) + [hbm, hbm],
        out_specs=[vmem] * serving,
        scratch_shapes=[
            pltpu.VMEM((padded, features), jnp.bfloat16),
            pltpu.VMEM((2, padded, columns), jnp.float32),
            pltpu.VMEM((SLOTS, 2, depth, columns), jnp.bfloat16),
            pltpu.SemaphoreType.DMA((SLOTS, 2)),
        ],
        compiler_params=pltpu.CompilerParams(vmem_limit_bytes=22 << 20),
    )(*arrived, *held, gate, up)
    back = [[None] * workers for _ in range(blocks)]
    for b in range(blocks):
        for s in range(workers):
            pairs = [(serving + k, b * workers + (k + s) % workers) for k in range(workers)]
            back[b][s] = lax.ppermute(hidden[(blocks - 1 - b) * workers + s], "wide", pairs)
    aligned = columns % 128 == 0
    if aligned:
        results = [r for some in back for r in some]
    else:
        me = lax.axis_index("wide")
        pieces = []
        for k in range(workers):
            piece = jnp.zeros((), jnp.bfloat16)
            for b in range(blocks):
                for s in range(workers):
                    mine = me == b * workers + (k + s) % workers
                    piece = jnp.where(mine, back[b][s], piece)
            pieces.append(piece)
        results = [jnp.concatenate(pieces, 1)]
    attended, activated = pl.pallas_call(
        functools.partial(finish_kernel, blocks, workers),
        out_shape=(
            jax.ShapeDtypeStruct((STEPS, half), jnp.bfloat16),
            jax.ShapeDtypeStruct((STEPS, workers * columns), jnp.bfloat16),
        ),
        in_specs=[vmem] * (1 + len(results)),
        out_specs=(vmem, vmem),
        compiler_params=pltpu.CompilerParams(vmem_limit_bytes=8 << 20),
    )(attended, *results)
    return attended.reshape(STEPS, 1, half), activated.reshape(STEPS, 1, -1)


def solution(mesh):
    rows = P(None, ("parts", "wide"), "narrow")
    placed = (
        rows,
        P(None, ("parts", "wide"), None, "narrow"),
        P(("parts", "wide"), "narrow", None, None),
        P(("parts", "wide"), "narrow", None, None),
        P(("parts", "wide")),
        rows,
        P("narrow"),
        P(None, "narrow", "wide"),
        P(None, "narrow", "wide"),
    )
    return jax.shard_map(
        shards, mesh=mesh, in_specs=placed, out_specs=(rows, rows), check_vma=False
    )
```

```python
import functools

import jax
import jax.numpy as jnp
from jax import lax
from jax.experimental import pallas as pl
from jax.experimental.pallas import tpu as pltpu
from jax.sharding import PartitionSpec as P

D = 4096
HEAD_SIZE = 128
STEPS = 2
TAIL = 128
EPS = 1e-05
EARLY = 2048
DEPTH = 512
SLOTS = 4
AHEAD = (2, 0, 1, 0, 1)


def pair(squares):
    high = squares.astype(jnp.bfloat16).astype(jnp.float32)
    lane = lax.broadcasted_iota(jnp.int32, (squares.shape[0], TAIL), 1)
    both = jnp.where(lane == 0, high, jnp.where(lane == 1, squares - high, 0.0))
    return both.astype(jnp.bfloat16)


def fetch_kernel(serving, _, gate, up, gate_held, up_held, sems):
    @pl.when(lax.axis_index("wide") >= serving)
    def _():
        here = pl.ds(0, gate_held.shape[0])
        copies = [
            pltpu.make_async_copy(gate.at[here], gate_held, sems.at[0]),
            pltpu.make_async_copy(up.at[here], up_held, sems.at[1]),
        ]
        for c in copies:
            c.start()
        for c in copies:
            c.wait()


def blank_kernel(*outs):
    for out in outs:
        out[...] = jnp.zeros_like(out)


def attend_kernel(*refs):
    sources, (attended, sent), held, sems = refs[:7], refs[7:9], refs[9:16], refs[16]
    lengths, q, kv, keys, values, residual, gain = held
    heads, hist, _ = keys.shape
    width = q.shape[1]
    group = width // (heads * HEAD_SIZE)
    copies = [
        pltpu.make_async_copy(source, place, sems.at[i])
        for i, (source, place) in enumerate(zip(sources, held))
    ]
    for c in copies:
        c.start()
    for c in copies:
        c.wait()
    length = lengths[0, 0]
    slot = lax.broadcasted_iota(jnp.int32, (hist, HEAD_SIZE), 0)
    rows = group * STEPS
    place = lax.broadcasted_iota(jnp.int32, (rows, hist), 1)
    step = lax.broadcasted_iota(jnp.int32, (rows, hist), 0) % STEPS
    first = hist - STEPS
    seen = (place < length) | ((place >= first) & (place - first <= step))
    squares = jnp.zeros((STEPS, 1), jnp.float32)
    for h in range(heads):
        lanes = slice(h * HEAD_SIZE, (h + 1) * HEAD_SIZE)
        k, v = keys[h], values[h]
        for t in range(STEPS):
            k = jnp.where(slot == first + t, kv[t, 0:1, lanes], k)
            v = jnp.where(slot == first + t, kv[t, 1:2, lanes], v)
        cols = [(h * group + g) * HEAD_SIZE for g in range(group)]
        query = jnp.concatenate(
            [q[:, c : c + HEAD_SIZE].astype(jnp.float32) for c in cols], 0
        ).astype(jnp.bfloat16)
        scores = lax.dot_general(
            query, k, (((1,), (1,)), ((), ())), preferred_element_type=jnp.float32
        ) * (1.0 / HEAD_SIZE**0.5)
        scores = jnp.where(seen, scores, -1e30)
        top = jnp.max(scores, -1, keepdims=True)
        e = jnp.where(seen, jnp.exp(scores - top), 0.0)
        weights = (e / jnp.sum(e, -1, keepdims=True)).astype(jnp.bfloat16)
        out = jnp.dot(weights, v, preferred_element_type=jnp.float32)
        for g, c in enumerate(cols):
            here = slice(c, c + HEAD_SIZE)
            got = out[g * STEPS : (g + 1) * STEPS].astype(jnp.bfloat16)
            attended[:, here] = got
            mixed = residual[:, here].astype(jnp.float32) + got.astype(jnp.float32)
            squares += jnp.sum(mixed * mixed, -1, keepdims=True)
            sent[:, here] = (mixed * gain[:, here]).astype(jnp.bfloat16)
    sent[:, width:] = pair(squares)


def forward_kernel(blocks, workers, narrow, *refs):
    count = blocks * workers
    arrived, (gate_held, up_held, gate, up), rest = refs[:blocks], refs[blocks:][:4], refs[blocks + 4 :]
    outs, (x, sums, slots, sems) = rest[:-4], rest[-4:]
    me = lax.axis_index("wide") - count
    features, columns = gate.shape
    half = features // narrow
    early = gate_held.shape[0]
    room, _, depth, across = slots.shape
    units = [(at, c) for at in range(early, features, depth) for c in range(0, columns, across)]
    cut = across // 512 * 256
    spans = {
        c: [slice(p, q) for p, q in ((c, c + cut), (c + cut, c + across)) if p < q]
        for c in range(0, columns, across)
    }

    def stream(j):
        s = j % room
        here = (pl.ds(units[j][0], depth), pl.ds(units[j][1], across))
        return [
            pltpu.make_async_copy(m.at[here], slots.at[s, i], sems.at[s, i])
            for i, m in enumerate((gate, up))
        ]

    @pl.when(me >= 0)
    def _():
        for j in range(min(room, len(units))):
            for copy in stream(j):
                copy.start()
        lines, tails = [], []
        for block in arrived:
            for shift in range(workers):
                owner = lax.rem(me + shift, workers)
                halves = [block[owner * narrow + n] for n in range(narrow)]
                lines.append(
                    jnp.concatenate([h[:, :half] for h in halves], 1).astype(jnp.float32)
                )
                tails.append(sum(h[:, half:].astype(jnp.float32) for h in halves))
        pad = x.shape[0] - STEPS * count
        if pad:
            lines.append(jnp.zeros((pad, features), jnp.float32))
            tails.append(jnp.zeros((pad, TAIL), jnp.float32))
        x[...] = jnp.concatenate(lines, 0).astype(jnp.bfloat16)
        squares = jnp.sum(jnp.concatenate(tails, 0), -1, keepdims=True)
        r = lax.rsqrt(squares / D + EPS)
        taken = set()

        def add(i, here, rows, block):
            product = jnp.dot(rows, block, preferred_element_type=jnp.float32)
            first = (i, here.start) not in taken
            taken.add((i, here.start))
            sums[i, :, here] = product if first else sums[i, :, here] + product

        waiting = [here for some in spans.values() for here in some]

        def resident(count):
            for here in waiting[:count]:
                for i, held in enumerate((gate_held, up_held)):
                    add(i, here, x[:, :early], held[:, here])
            del waiting[:count]

        for j, (at, c) in enumerate(units):
            resident(AHEAD[j] if j < len(AHEAD) else 0)
            if j == len(units) - 1:
                resident(len(waiting))
            for copy in stream(j):
                copy.wait()
            for here in spans[c]:
                there = slice(here.start - c, here.stop - c)
                for i in range(2):
                    add(i, here, x[:, at : at + depth], slots[j % room, i, :, there])
            if j + room < len(units):
                for copy in stream(j + room):
                    copy.start()
        g, u = sums[0] * r, sums[1] * r
        hidden = (g / (1.0 + jnp.exp(-g)) * u).astype(jnp.bfloat16)
        for i in range(count):
            out = outs[(blocks - 1 - i // workers) * workers + i % workers]
            out[...] = hidden[i * STEPS : (i + 1) * STEPS]


def finish_kernel(blocks, workers, attended, *refs):
    results, (attended_out, out) = refs[:-2], refs[-2:]
    attended_out[...] = attended[...]
    if len(results) == 1:
        out[...] = results[0][...]
        return
    me = lax.axis_index("wide")
    columns = results[0].shape[1]

    @pl.when(me >= blocks * workers)
    def _():
        out[...] = jnp.zeros_like(out)

    for i, result in enumerate(results):
        b, shift = divmod(i, workers)

        @pl.when((me >= b * workers) & (me < (b + 1) * workers))
        def _():
            k = lax.rem(me - b * workers + workers - shift, workers)
            out[:, pl.ds(pl.multiple_of(k * columns, 128), columns)] = result[...]


def shards(queries, new_kv, keys, values, lengths, residual, gain, gate, up):
    wide = lax.axis_size("wide")
    narrow = lax.axis_size("narrow")
    serving = wide * 3 // 4
    workers = wide - serving
    blocks = serving // workers
    half = queries.shape[2]
    features, _, columns = gate.shape
    vmem = pl.BlockSpec(memory_space=pltpu.VMEM)
    hbm = pl.BlockSpec(memory_space=pltpu.HBM)
    owner = lax.axis_index("wide") < serving

    def in_hbm(a):
        return pltpu.with_memory_space_constraint(a, pltpu.HBM)

    gate = in_hbm(gate.reshape(features, columns))
    up = in_hbm(up.reshape(features, columns))
    operands = (
        lengths.reshape(1, 1),
        queries.reshape(STEPS, half),
        new_kv.reshape(STEPS, 2, -1),
        keys.reshape(keys.shape[1:]),
        values.reshape(values.shape[1:]),
        residual.reshape(STEPS, half),
        gain.reshape(1, half),
    )
    groups = [
        [w * narrow + n for w in range(at, at + workers) for n in range(narrow)]
        for at in range(0, wide, workers)
    ]
    shapes = (
        jax.ShapeDtypeStruct((STEPS, half), jnp.bfloat16),
        jax.ShapeDtypeStruct((workers * narrow, STEPS, half + TAIL), jnp.bfloat16),
    )

    def serve(*operands):
        attended, sent = pl.pallas_call(
            attend_kernel,
            out_shape=(
                pltpu.VMEM(shapes[0].shape, jnp.bfloat16),
                jax.ShapeDtypeStruct(shapes[1].shape[1:], jnp.bfloat16),
            ),
            in_specs=[hbm] * 7,
            out_specs=(vmem, vmem),
            scratch_shapes=[
                (pltpu.SMEM if o.dtype == jnp.int32 else pltpu.VMEM)(o.shape, o.dtype)
                for o in operands
            ]
            + [pltpu.SemaphoreType.DMA((7,))],
            compiler_params=pltpu.CompilerParams(vmem_limit_bytes=8 << 20),
        )(operands[0], *map(in_hbm, operands[1:]))
        gathered = lax.all_gather(sent, ("wide", "narrow"), axis=0, axis_index_groups=groups)
        return attended, gathered

    def rest(*operands):
        return pl.pallas_call(
            blank_kernel,
            out_shape=(pltpu.VMEM(shapes[0].shape, jnp.bfloat16), shapes[1]),
            out_specs=(vmem, vmem),
            compiler_params=pltpu.CompilerParams(vmem_limit_bytes=8 << 20),
        )()

    attended, block = lax.cond(owner, serve, rest, *operands)
    arrived = [
        lax.ppermute(block, "wide", [(b * workers + j, serving + j) for j in range(workers)])
        for b in range(blocks)
    ]
    early = min(EARLY, features // 2)
    held = pl.pallas_call(
        functools.partial(fetch_kernel, serving),
        out_shape=[pltpu.VMEM((early, columns), jnp.bfloat16)] * 2,
        in_specs=[pl.BlockSpec(memory_space=pl.ANY), hbm, hbm],
        out_specs=[vmem] * 2,
        scratch_shapes=[pltpu.SemaphoreType.DMA((2,))],
        compiler_params=pltpu.CompilerParams(vmem_limit_bytes=4 << 20),
        cost_estimate=pl.CostEstimate(
            flops=0, bytes_accessed=early * 4 * columns, transcendentals=0
        ),
    )(block, gate, up)
    padded = -(-STEPS * serving // 16) * 16
    depth = min(DEPTH, features - early)
    across = columns // 2 if columns % 512 == 0 else columns
    hidden = pl.pallas_call(
        functools.partial(forward_kernel, blocks, workers, narrow),
        out_shape=[jax.ShapeDtypeStruct((STEPS, columns), jnp.bfloat16)] * serving,
        in_specs=[vmem] * (blocks + 2) + [hbm, hbm],
        out_specs=[vmem] * serving,
        scratch_shapes=[
            pltpu.VMEM((padded, features), jnp.bfloat16),
            pltpu.VMEM((2, padded, columns), jnp.float32),
            pltpu.VMEM((SLOTS, 2, depth, across), jnp.bfloat16),
            pltpu.SemaphoreType.DMA((SLOTS, 2)),
        ],
        compiler_params=pltpu.CompilerParams(vmem_limit_bytes=16 << 20),
    )(*arrived, *held, gate, up)
    back = [[None] * workers for _ in range(blocks)]
    for b in range(blocks):
        for s in range(workers):
            pairs = [(serving + k, b * workers + (k + s) % workers) for k in range(workers)]
            back[b][s] = lax.ppermute(hidden[(blocks - 1 - b) * workers + s], "wide", pairs)
    aligned = columns % 128 == 0
    if aligned:
        results = [r for some in back for r in some]
    else:
        me = lax.axis_index("wide")
        pieces = []
        for k in range(workers):
            piece = jnp.zeros((), jnp.bfloat16)
            for b in range(blocks):
                for s in range(workers):
                    mine = me == b * workers + (k + s) % workers
                    piece = jnp.where(mine, back[b][s], piece)
            pieces.append(piece)
        results = [jnp.concatenate(pieces, 1)]
    attended, activated = pl.pallas_call(
        functools.partial(finish_kernel, blocks, workers),
        out_shape=(
            jax.ShapeDtypeStruct((STEPS, half), jnp.bfloat16),
            jax.ShapeDtypeStruct((STEPS, workers * columns), jnp.bfloat16),
        ),
        in_specs=[vmem] * (1 + len(results)),
        out_specs=(vmem, vmem),
        compiler_params=pltpu.CompilerParams(vmem_limit_bytes=8 << 20),
    )(attended, *results)
    return attended.reshape(STEPS, 1, half), activated.reshape(STEPS, 1, -1)


def solution(mesh):
    rows = P(None, ("parts", "wide"), "narrow")
    placed = (
        rows,
        P(None, ("parts", "wide"), None, "narrow"),
        P(("parts", "wide"), "narrow", None, None),
        P(("parts", "wide"), "narrow", None, None),
        P(("parts", "wide")),
        rows,
        P("narrow"),
        P(None, "narrow", "wide"),
        P(None, "narrow", "wide"),
    )
    return jax.shard_map(
        shards, mesh=mesh, in_specs=placed, out_specs=(rows, rows), check_vma=False
    )
```

```python
import functools

import jax
import jax.numpy as jnp
from jax import lax
from jax.experimental import pallas as pl
from jax.experimental.pallas import tpu as pltpu
from jax.sharding import PartitionSpec as P

D = 4096
HEAD_SIZE = 128
STEPS = 2
TAIL = 128
EPS = 1e-05
TILE = 256
SLOTS = 4
AHEAD = (3, 1, 1, 1, 1)


def pair(squares):
    high = squares.astype(jnp.bfloat16).astype(jnp.float32)
    lane = lax.broadcasted_iota(jnp.int32, (squares.shape[0], TAIL), 1)
    both = jnp.where(lane == 0, high, jnp.where(lane == 1, squares - high, 0.0))
    return both.astype(jnp.bfloat16)


def fetch_kernel(serving, _, gate, up, gate_held, up_held, sems):
    @pl.when(lax.axis_index("wide") >= serving)
    def _():
        here = pl.ds(0, gate_held.shape[1])
        copies = [
            pltpu.make_async_copy(gate.at[:, here], gate_held, sems.at[0]),
            pltpu.make_async_copy(up.at[:, here], up_held, sems.at[1]),
        ]
        for c in copies:
            c.start()
        for c in copies:
            c.wait()


def blank_kernel(*outs):
    for out in outs:
        out[...] = jnp.zeros_like(out)


def attend_kernel(*refs):
    sources, (attended, sent), held, sems = refs[:7], refs[7:9], refs[9:16], refs[16]
    lengths, q, kv, keys, values, residual, gain = held
    heads, hist, _ = keys.shape
    width = q.shape[1]
    group = width // (heads * HEAD_SIZE)
    copies = [
        pltpu.make_async_copy(source, place, sems.at[i])
        for i, (source, place) in enumerate(zip(sources, held))
    ]
    for c in copies:
        c.start()
    for c in copies:
        c.wait()
    length = lengths[0, 0]
    slot = lax.broadcasted_iota(jnp.int32, (hist, HEAD_SIZE), 0)
    rows = group * STEPS
    place = lax.broadcasted_iota(jnp.int32, (rows, hist), 1)
    step = lax.broadcasted_iota(jnp.int32, (rows, hist), 0) % STEPS
    first = hist - STEPS
    seen = (place < length) | ((place >= first) & (place - first <= step))
    squares = jnp.zeros((STEPS, 1), jnp.float32)
    for h in range(heads):
        lanes = slice(h * HEAD_SIZE, (h + 1) * HEAD_SIZE)
        k, v = keys[h], values[h]
        for t in range(STEPS):
            k = jnp.where(slot == first + t, kv[t, 0:1, lanes], k)
            v = jnp.where(slot == first + t, kv[t, 1:2, lanes], v)
        cols = [(h * group + g) * HEAD_SIZE for g in range(group)]
        query = jnp.concatenate(
            [q[:, c : c + HEAD_SIZE].astype(jnp.float32) for c in cols], 0
        ).astype(jnp.bfloat16)
        scores = lax.dot_general(
            query, k, (((1,), (1,)), ((), ())), preferred_element_type=jnp.float32
        ) * (1.0 / HEAD_SIZE**0.5)
        scores = jnp.where(seen, scores, -1e30)
        top = jnp.max(scores, -1, keepdims=True)
        e = jnp.where(seen, jnp.exp(scores - top), 0.0)
        weights = (e / jnp.sum(e, -1, keepdims=True)).astype(jnp.bfloat16)
        out = jnp.dot(weights, v, preferred_element_type=jnp.float32)
        for g, c in enumerate(cols):
            here = slice(c, c + HEAD_SIZE)
            got = out[g * STEPS : (g + 1) * STEPS].astype(jnp.bfloat16)
            attended[:, here] = got
            mixed = residual[:, here].astype(jnp.float32) + got.astype(jnp.float32)
            squares += jnp.sum(mixed * mixed, -1, keepdims=True)
            sent[:, here] = (mixed * gain[:, here]).astype(jnp.bfloat16)
    sent[:, width:] = pair(squares)


def forward_kernel(blocks, workers, narrow, *refs):
    count = blocks * workers
    arrived, (gate_held, up_held, gate, up), rest = refs[:blocks], refs[blocks:][:4], refs[blocks + 4 :]
    outs, (x, slots, sems) = rest[:-3], rest[-3:]
    me = lax.axis_index("wide") - count
    features, columns = gate.shape
    half = features // narrow
    early = gate_held.shape[1]
    room, _, _, tile = slots.shape
    units = list(range(early, columns, tile))

    def stream(j):
        s = j % room
        here = pl.ds(units[j], tile)
        return [
            pltpu.make_async_copy(m.at[:, here], slots.at[s, i], sems.at[s, i])
            for i, m in enumerate((gate, up))
        ]

    @pl.when(me >= 0)
    def _():
        for j in range(min(room, len(units))):
            for copy in stream(j):
                copy.start()
        lines, tails = [], []
        for block in arrived:
            for shift in range(workers):
                owner = lax.rem(me + shift, workers)
                halves = [block[owner * narrow + n] for n in range(narrow)]
                lines.append(
                    jnp.concatenate([h[:, :half] for h in halves], 1).astype(jnp.float32)
                )
                tails.append(sum(h[:, half:].astype(jnp.float32) for h in halves))
        pad = x.shape[0] - STEPS * count
        if pad:
            lines.append(jnp.zeros((pad, features), jnp.float32))
            tails.append(jnp.zeros((pad, TAIL), jnp.float32))
        x[...] = jnp.concatenate(lines, 0).astype(jnp.bfloat16)
        squares = jnp.sum(jnp.concatenate(tails, 0), -1, keepdims=True)
        r = lax.rsqrt(squares / D + EPS)

        def produce(at, gate_tile, up_tile):
            g = jnp.dot(x[...], gate_tile, preferred_element_type=jnp.float32) * r
            u = jnp.dot(x[...], up_tile, preferred_element_type=jnp.float32) * r
            hidden = (g / (1.0 + jnp.exp(-g)) * u).astype(jnp.bfloat16)
            for i in range(count):
                out = outs[(blocks - 1 - i // workers) * workers + i % workers]
                out[:, at : at + tile] = hidden[i * STEPS : (i + 1) * STEPS]

        waiting = list(range(0, early, tile))

        def resident(some):
            for at in waiting[:some]:
                produce(at, gate_held[:, at : at + tile], up_held[:, at : at + tile])
            del waiting[:some]

        for j, at in enumerate(units):
            resident(AHEAD[j] if j < len(AHEAD) else 0)
            if j == len(units) - 1:
                resident(len(waiting))
            for copy in stream(j):
                copy.wait()
            produce(at, slots[j % room, 0], slots[j % room, 1])
            if j + room < len(units):
                for copy in stream(j + room):
                    copy.start()
        if not units:
            resident(len(waiting))


def finish_kernel(blocks, workers, attended, *refs):
    results, (attended_out, out) = refs[:-2], refs[-2:]
    attended_out[...] = attended[...]
    if len(results) == 1:
        out[...] = results[0][...]
        return
    me = lax.axis_index("wide")
    columns = results[0].shape[1]

    @pl.when(me >= blocks * workers)
    def _():
        out[...] = jnp.zeros_like(out)

    for i, result in enumerate(results):
        b, shift = divmod(i, workers)

        @pl.when((me >= b * workers) & (me < (b + 1) * workers))
        def _():
            k = lax.rem(me - b * workers + workers - shift, workers)
            out[:, pl.ds(pl.multiple_of(k * columns, 128), columns)] = result[...]


def shards(queries, new_kv, keys, values, lengths, residual, gain, gate, up):
    wide = lax.axis_size("wide")
    narrow = lax.axis_size("narrow")
    serving = wide * 3 // 4
    workers = wide - serving
    blocks = serving // workers
    half = queries.shape[2]
    features, _, columns = gate.shape
    vmem = pl.BlockSpec(memory_space=pltpu.VMEM)
    hbm = pl.BlockSpec(memory_space=pltpu.HBM)
    owner = lax.axis_index("wide") < serving

    def in_hbm(a):
        return pltpu.with_memory_space_constraint(a, pltpu.HBM)

    gate = in_hbm(gate.reshape(features, columns))
    up = in_hbm(up.reshape(features, columns))
    operands = (
        lengths.reshape(1, 1),
        queries.reshape(STEPS, half),
        new_kv.reshape(STEPS, 2, -1),
        keys.reshape(keys.shape[1:]),
        values.reshape(values.shape[1:]),
        residual.reshape(STEPS, half),
        gain.reshape(1, half),
    )
    groups = [
        [w * narrow + n for w in range(at, at + workers) for n in range(narrow)]
        for at in range(0, wide, workers)
    ]
    shapes = (
        jax.ShapeDtypeStruct((STEPS, half), jnp.bfloat16),
        jax.ShapeDtypeStruct((workers * narrow, STEPS, half + TAIL), jnp.bfloat16),
    )

    def serve(*operands):
        attended, sent = pl.pallas_call(
            attend_kernel,
            out_shape=(
                pltpu.VMEM(shapes[0].shape, jnp.bfloat16),
                jax.ShapeDtypeStruct(shapes[1].shape[1:], jnp.bfloat16),
            ),
            in_specs=[hbm] * 7,
            out_specs=(vmem, vmem),
            scratch_shapes=[
                (pltpu.SMEM if o.dtype == jnp.int32 else pltpu.VMEM)(o.shape, o.dtype)
                for o in operands
            ]
            + [pltpu.SemaphoreType.DMA((7,))],
            compiler_params=pltpu.CompilerParams(vmem_limit_bytes=8 << 20),
        )(operands[0], *map(in_hbm, operands[1:]))
        gathered = lax.all_gather(sent, ("wide", "narrow"), axis=0, axis_index_groups=groups)
        return attended, gathered

    def rest(*operands):
        return pl.pallas_call(
            blank_kernel,
            out_shape=(pltpu.VMEM(shapes[0].shape, jnp.bfloat16), shapes[1]),
            out_specs=(vmem, vmem),
            compiler_params=pltpu.CompilerParams(vmem_limit_bytes=8 << 20),
        )()

    attended, block = lax.cond(owner, serve, rest, *operands)
    arrived = [
        lax.ppermute(block, "wide", [(b * workers + j, serving + j) for j in range(workers)])
        for b in range(blocks)
    ]
    tile = TILE if columns % (2 * TILE) == 0 else columns
    early = columns // 2 // tile * tile or columns
    held = pl.pallas_call(
        functools.partial(fetch_kernel, serving),
        out_shape=[pltpu.VMEM((features, early), jnp.bfloat16)] * 2,
        in_specs=[pl.BlockSpec(memory_space=pl.ANY), hbm, hbm],
        out_specs=[vmem] * 2,
        scratch_shapes=[pltpu.SemaphoreType.DMA((2,))],
        compiler_params=pltpu.CompilerParams(vmem_limit_bytes=4 << 20),
        cost_estimate=pl.CostEstimate(
            flops=0, bytes_accessed=early * 4 * features, transcendentals=0
        ),
    )(block, gate, up)
    padded = -(-STEPS * serving // 16) * 16
    hidden = pl.pallas_call(
        functools.partial(forward_kernel, blocks, workers, narrow),
        out_shape=[jax.ShapeDtypeStruct((STEPS, columns), jnp.bfloat16)] * serving,
        in_specs=[vmem] * (blocks + 2) + [hbm, hbm],
        out_specs=[vmem] * serving,
        scratch_shapes=[
            pltpu.VMEM((padded, features), jnp.bfloat16),
            pltpu.VMEM((SLOTS, 2, features, tile), jnp.bfloat16),
            pltpu.SemaphoreType.DMA((SLOTS, 2)),
        ],
        compiler_params=pltpu.CompilerParams(vmem_limit_bytes=18 << 20),
    )(*arrived, *held, gate, up)
    back = [[None] * workers for _ in range(blocks)]
    for b in range(blocks):
        for s in range(workers):
            pairs = [(serving + k, b * workers + (k + s) % workers) for k in range(workers)]
            back[b][s] = lax.ppermute(hidden[(blocks - 1 - b) * workers + s], "wide", pairs)
    aligned = columns % 128 == 0
    if aligned:
        results = [r for some in back for r in some]
    else:
        me = lax.axis_index("wide")
        pieces = []
        for k in range(workers):
            piece = jnp.zeros((), jnp.bfloat16)
            for b in range(blocks):
                for s in range(workers):
                    mine = me == b * workers + (k + s) % workers
                    piece = jnp.where(mine, back[b][s], piece)
            pieces.append(piece)
        results = [jnp.concatenate(pieces, 1)]
    attended, activated = pl.pallas_call(
        functools.partial(finish_kernel, blocks, workers),
        out_shape=(
            jax.ShapeDtypeStruct((STEPS, half), jnp.bfloat16),
            jax.ShapeDtypeStruct((STEPS, workers * columns), jnp.bfloat16),
        ),
        in_specs=[vmem] * (1 + len(results)),
        out_specs=(vmem, vmem),
        compiler_params=pltpu.CompilerParams(vmem_limit_bytes=8 << 20),
    )(attended, *results)
    return attended.reshape(STEPS, 1, half), activated.reshape(STEPS, 1, -1)


def solution(mesh):
    rows = P(None, ("parts", "wide"), "narrow")
    placed = (
        rows,
        P(None, ("parts", "wide"), None, "narrow"),
        P(("parts", "wide"), "narrow", None, None),
        P(("parts", "wide"), "narrow", None, None),
        P(("parts", "wide")),
        rows,
        P("narrow"),
        P(None, "narrow", "wide"),
        P(None, "narrow", "wide"),
    )
    return jax.shard_map(
        shards, mesh=mesh, in_specs=placed, out_specs=(rows, rows), check_vma=False
    )
```

```python
import functools

import jax
import jax.numpy as jnp
from jax import lax
from jax.experimental import pallas as pl
from jax.experimental.pallas import tpu as pltpu
from jax.sharding import PartitionSpec as P

D = 4096
HEAD_SIZE = 128
STEPS = 2
TAIL = 128
EPS = 1e-05
TILE = 256
SLOTS = 4
AHEAD = (3, 1, 1, 1, 1)


def pair(squares):
    high = squares.astype(jnp.bfloat16).astype(jnp.float32)
    lane = lax.broadcasted_iota(jnp.int32, (squares.shape[0], TAIL), 1)
    both = jnp.where(lane == 0, high, jnp.where(lane == 1, squares - high, 0.0))
    return both.astype(jnp.bfloat16)


def fetch_kernel(serving, _, gate, up, gate_held, up_held, sems):
    @pl.when(lax.axis_index("wide") >= serving)
    def _():
        here = pl.ds(0, gate_held.shape[1])
        copies = [
            pltpu.make_async_copy(gate.at[:, here], gate_held, sems.at[0]),
            pltpu.make_async_copy(up.at[:, here], up_held, sems.at[1]),
        ]
        for c in copies:
            c.start()
        for c in copies:
            c.wait()


def blank_kernel(*outs):
    for out in outs:
        out[...] = jnp.zeros_like(out)


def attend_kernel(*refs):
    sources, (attended, sent), held, sems = refs[:7], refs[7:9], refs[9:16], refs[16]
    lengths, q, kv, keys, values, residual, gain = held
    heads, hist, _ = keys.shape
    width = q.shape[1]
    group = width // (heads * HEAD_SIZE)
    copies = [
        pltpu.make_async_copy(source, place, sems.at[i])
        for i, (source, place) in enumerate(zip(sources, held))
    ]
    for c in copies:
        c.start()
    for c in copies:
        c.wait()
    length = lengths[0, 0]
    slot = lax.broadcasted_iota(jnp.int32, (hist, HEAD_SIZE), 0)
    rows = group * STEPS
    place = lax.broadcasted_iota(jnp.int32, (rows, hist), 1)
    step = lax.broadcasted_iota(jnp.int32, (rows, hist), 0) % STEPS
    first = hist - STEPS
    seen = (place < length) | ((place >= first) & (place - first <= step))
    squares = jnp.zeros((STEPS, 1), jnp.float32)
    for h in range(heads):
        lanes = slice(h * HEAD_SIZE, (h + 1) * HEAD_SIZE)
        k, v = keys[h], values[h]
        for t in range(STEPS):
            k = jnp.where(slot == first + t, kv[t, 0:1, lanes], k)
            v = jnp.where(slot == first + t, kv[t, 1:2, lanes], v)
        cols = [(h * group + g) * HEAD_SIZE for g in range(group)]
        query = jnp.concatenate(
            [q[:, c : c + HEAD_SIZE].astype(jnp.float32) for c in cols], 0
        ).astype(jnp.bfloat16)
        scores = lax.dot_general(
            query, k, (((1,), (1,)), ((), ())), preferred_element_type=jnp.float32
        ) * (1.0 / HEAD_SIZE**0.5)
        scores = jnp.where(seen, scores, -1e30)
        top = jnp.max(scores, -1, keepdims=True)
        e = jnp.where(seen, jnp.exp(scores - top), 0.0)
        weights = (e / jnp.sum(e, -1, keepdims=True)).astype(jnp.bfloat16)
        out = jnp.dot(weights, v, preferred_element_type=jnp.float32)
        for g, c in enumerate(cols):
            here = slice(c, c + HEAD_SIZE)
            got = out[g * STEPS : (g + 1) * STEPS].astype(jnp.bfloat16)
            attended[:, here] = got
            mixed = residual[:, here].astype(jnp.float32) + got.astype(jnp.float32)
            squares += jnp.sum(mixed * mixed, -1, keepdims=True)
            sent[:, here] = (mixed * gain[:, here]).astype(jnp.bfloat16)
    sent[:, width:] = pair(squares)


def forward_kernel(blocks, workers, narrow, *refs):
    count = blocks * workers
    arrived, (gate_held, up_held, gate, up), rest = refs[:blocks], refs[blocks:][:4], refs[blocks + 4 :]
    outs, (x, slots, sems) = rest[:-3], rest[-3:]
    me = lax.axis_index("wide") - count
    features, columns = gate.shape
    half = features // narrow
    early = gate_held.shape[1]
    room, _, _, tile = slots.shape
    units = list(range(early, columns, tile))

    def stream(j):
        s = j % room
        here = pl.ds(units[j], tile)
        return [
            pltpu.make_async_copy(m.at[:, here], slots.at[s, i], sems.at[s, i])
            for i, m in enumerate((gate, up))
        ]

    @pl.when(me >= 0)
    def _():
        for j in range(min(room, len(units))):
            for copy in stream(j):
                copy.start()
        lines, tails = [], []
        for block in arrived:
            for shift in range(workers):
                owner = lax.rem(me + shift, workers)
                halves = [block[owner * narrow + n] for n in range(narrow)]
                lines.append(
                    jnp.concatenate([h[:, :half] for h in halves], 1).astype(jnp.float32)
                )
                tails.append(sum(h[:, half:].astype(jnp.float32) for h in halves))
        pad = x.shape[0] - STEPS * count
        if pad:
            lines.append(jnp.zeros((pad, features), jnp.float32))
            tails.append(jnp.zeros((pad, TAIL), jnp.float32))
        x[...] = jnp.concatenate(lines, 0).astype(jnp.bfloat16)
        squares = jnp.sum(jnp.concatenate(tails, 0), -1, keepdims=True)
        r = lax.rsqrt(squares / D + EPS)

        def produce(at, gate_tile, up_tile):
            g = jnp.dot(x[...], gate_tile, preferred_element_type=jnp.float32) * r
            u = jnp.dot(x[...], up_tile, preferred_element_type=jnp.float32) * r
            hidden = (g / (1.0 + jnp.exp(-g)) * u).astype(jnp.bfloat16)
            for i in range(count):
                out = outs[blocks - 1 - i // workers]
                out[i % workers, :, at : at + tile] = hidden[i * STEPS : (i + 1) * STEPS]

        waiting = list(range(0, early, tile))

        def resident(some):
            for at in waiting[:some]:
                produce(at, gate_held[:, at : at + tile], up_held[:, at : at + tile])
            del waiting[:some]

        for j, at in enumerate(units):
            resident(AHEAD[j] if j < len(AHEAD) else 0)
            if j == len(units) - 1:
                resident(len(waiting))
            for copy in stream(j):
                copy.wait()
            produce(at, slots[j % room, 0], slots[j % room, 1])
            if j + room < len(units):
                for copy in stream(j + room):
                    copy.start()
        if not units:
            resident(len(waiting))


def choose_kernel(workers, *refs):
    results, out = refs[:-1], refs[-1]
    for b, result in enumerate(results):

        @pl.when(lax.axis_index("wide") // workers == b)
        def _():
            out[...] = result[...]


def finish_kernel(workers, attended, gathered, attended_out, out):
    me = lax.axis_index("wide")
    columns = gathered.shape[3]
    attended_out[...] = attended[...]
    for k in range(workers):
        shift = lax.rem(lax.rem(me, workers) + workers - k, workers)
        out[:, k * columns : (k + 1) * columns] = gathered[k, shift]


def shards(queries, new_kv, keys, values, lengths, residual, gain, gate, up):
    wide = lax.axis_size("wide")
    narrow = lax.axis_size("narrow")
    serving = wide * 3 // 4
    workers = wide - serving
    blocks = serving // workers
    half = queries.shape[2]
    features, _, columns = gate.shape
    vmem = pl.BlockSpec(memory_space=pltpu.VMEM)
    hbm = pl.BlockSpec(memory_space=pltpu.HBM)
    owner = lax.axis_index("wide") < serving

    def in_hbm(a):
        return pltpu.with_memory_space_constraint(a, pltpu.HBM)

    gate = in_hbm(gate.reshape(features, columns))
    up = in_hbm(up.reshape(features, columns))
    operands = (
        lengths.reshape(1, 1),
        queries.reshape(STEPS, half),
        new_kv.reshape(STEPS, 2, -1),
        keys.reshape(keys.shape[1:]),
        values.reshape(values.shape[1:]),
        residual.reshape(STEPS, half),
        gain.reshape(1, half),
    )
    groups = [
        [w * narrow + n for w in range(at, at + workers) for n in range(narrow)]
        for at in range(0, wide, workers)
    ]
    shapes = (
        jax.ShapeDtypeStruct((STEPS, half), jnp.bfloat16),
        jax.ShapeDtypeStruct((workers * narrow, STEPS, half + TAIL), jnp.bfloat16),
    )

    def serve(*operands):
        attended, sent = pl.pallas_call(
            attend_kernel,
            out_shape=(
                pltpu.VMEM(shapes[0].shape, jnp.bfloat16),
                jax.ShapeDtypeStruct(shapes[1].shape[1:], jnp.bfloat16),
            ),
            in_specs=[hbm] * 7,
            out_specs=(vmem, vmem),
            scratch_shapes=[
                (pltpu.SMEM if o.dtype == jnp.int32 else pltpu.VMEM)(o.shape, o.dtype)
                for o in operands
            ]
            + [pltpu.SemaphoreType.DMA((7,))],
            compiler_params=pltpu.CompilerParams(vmem_limit_bytes=8 << 20),
        )(operands[0], *map(in_hbm, operands[1:]))
        gathered = lax.all_gather(sent, ("wide", "narrow"), axis=0, axis_index_groups=groups)
        return attended, gathered

    def rest(*operands):
        return pl.pallas_call(
            blank_kernel,
            out_shape=(pltpu.VMEM(shapes[0].shape, jnp.bfloat16), shapes[1]),
            out_specs=(vmem, vmem),
            compiler_params=pltpu.CompilerParams(vmem_limit_bytes=8 << 20),
        )()

    attended, block = lax.cond(owner, serve, rest, *operands)
    arrived = [
        lax.ppermute(block, "wide", [(b * workers + j, serving + j) for j in range(workers)])
        for b in range(blocks)
    ]
    tile = TILE if columns % (2 * TILE) == 0 else columns
    early = columns // 2 // tile * tile or columns
    held = pl.pallas_call(
        functools.partial(fetch_kernel, serving),
        out_shape=[pltpu.VMEM((features, early), jnp.bfloat16)] * 2,
        in_specs=[pl.BlockSpec(memory_space=pl.ANY), hbm, hbm],
        out_specs=[vmem] * 2,
        scratch_shapes=[pltpu.SemaphoreType.DMA((2,))],
        compiler_params=pltpu.CompilerParams(vmem_limit_bytes=4 << 20),
        cost_estimate=pl.CostEstimate(
            flops=0, bytes_accessed=early * 4 * features, transcendentals=0
        ),
    )(block, gate, up)
    padded = -(-STEPS * serving // 16) * 16
    hidden = pl.pallas_call(
        functools.partial(forward_kernel, blocks, workers, narrow),
        out_shape=[jax.ShapeDtypeStruct((workers, STEPS, columns), jnp.bfloat16)] * blocks,
        in_specs=[vmem] * (blocks + 2) + [hbm, hbm],
        out_specs=[vmem] * blocks,
        scratch_shapes=[
            pltpu.VMEM((padded, features), jnp.bfloat16),
            pltpu.VMEM((SLOTS, 2, features, tile), jnp.bfloat16),
            pltpu.SemaphoreType.DMA((SLOTS, 2)),
        ],
        compiler_params=pltpu.CompilerParams(vmem_limit_bytes=18 << 20),
    )(*arrived, *held, gate, up)
    back = [
        lax.ppermute(
            hidden[blocks - 1 - b], "wide", [(serving + k, b * workers + k) for k in range(workers)]
        )
        for b in range(blocks)
    ]
    peers = [list(range(at, at + workers)) for at in range(0, wide, workers)]
    shape = jax.ShapeDtypeStruct((workers, STEPS, columns), jnp.bfloat16)

    def collect(*back):
        mine = pl.pallas_call(
            functools.partial(choose_kernel, workers),
            out_shape=shape,
            in_specs=[vmem] * blocks,
            out_specs=vmem,
            compiler_params=pltpu.CompilerParams(vmem_limit_bytes=8 << 20),
        )(*back)
        return lax.all_gather(mine, "wide", axis=0, axis_index_groups=peers)

    def skip(*back):
        return pl.pallas_call(
            blank_kernel,
            out_shape=jax.ShapeDtypeStruct((workers, *shape.shape), jnp.bfloat16),
            out_specs=vmem,
            compiler_params=pltpu.CompilerParams(vmem_limit_bytes=8 << 20),
        )()

    gathered = lax.cond(owner, collect, skip, *back)
    attended, activated = pl.pallas_call(
        functools.partial(finish_kernel, workers),
        out_shape=(
            jax.ShapeDtypeStruct((STEPS, half), jnp.bfloat16),
            jax.ShapeDtypeStruct((STEPS, workers * columns), jnp.bfloat16),
        ),
        in_specs=[vmem] * 2,
        out_specs=(vmem, vmem),
        compiler_params=pltpu.CompilerParams(vmem_limit_bytes=8 << 20),
    )(attended, gathered)
    return attended.reshape(STEPS, 1, half), activated.reshape(STEPS, 1, -1)


def solution(mesh):
    rows = P(None, ("parts", "wide"), "narrow")
    placed = (
        rows,
        P(None, ("parts", "wide"), None, "narrow"),
        P(("parts", "wide"), "narrow", None, None),
        P(("parts", "wide"), "narrow", None, None),
        P(("parts", "wide")),
        rows,
        P("narrow"),
        P(None, "narrow", "wide"),
        P(None, "narrow", "wide"),
    )
    return jax.shard_map(
        shards, mesh=mesh, in_specs=placed, out_specs=(rows, rows), check_vma=False
    )
```

```python
import functools

import jax
import jax.numpy as jnp
from jax import lax
from jax.experimental import pallas as pl
from jax.experimental.pallas import tpu as pltpu
from jax.sharding import PartitionSpec as P

D = 4096
HEAD_SIZE = 128
STEPS = 2
TAIL = 128
EPS = 1e-05
TILE = 256
SLOTS = 4
AHEAD = (3, 1, 1, 1, 1)


def pair(squares):
    high = squares.astype(jnp.bfloat16).astype(jnp.float32)
    lane = lax.broadcasted_iota(jnp.int32, (squares.shape[0], TAIL), 1)
    both = jnp.where(lane == 0, high, jnp.where(lane == 1, squares - high, 0.0))
    return both.astype(jnp.bfloat16)


def blank_kernel(*outs):
    for out in outs:
        out[...] = jnp.zeros_like(out)


def attend_kernel(*refs):
    sources, (attended, sent), held, sems = refs[:7], refs[7:9], refs[9:16], refs[16]
    lengths, q, kv, keys, values, residual, gain = held
    heads, hist, _ = keys.shape
    width = q.shape[1]
    group = width // (heads * HEAD_SIZE)
    copies = [
        pltpu.make_async_copy(source, place, sems.at[i])
        for i, (source, place) in enumerate(zip(sources, held))
    ]
    for c in copies:
        c.start()
    for c in copies:
        c.wait()
    length = lengths[0, 0]
    slot = lax.broadcasted_iota(jnp.int32, (hist, HEAD_SIZE), 0)
    rows = group * STEPS
    place = lax.broadcasted_iota(jnp.int32, (rows, hist), 1)
    step = lax.broadcasted_iota(jnp.int32, (rows, hist), 0) % STEPS
    first = hist - STEPS
    seen = (place < length) | ((place >= first) & (place - first <= step))
    squares = jnp.zeros((STEPS, 1), jnp.float32)
    for h in range(heads):
        lanes = slice(h * HEAD_SIZE, (h + 1) * HEAD_SIZE)
        k, v = keys[h], values[h]
        for t in range(STEPS):
            k = jnp.where(slot == first + t, kv[t, 0:1, lanes], k)
            v = jnp.where(slot == first + t, kv[t, 1:2, lanes], v)
        cols = [(h * group + g) * HEAD_SIZE for g in range(group)]
        query = jnp.concatenate(
            [q[:, c : c + HEAD_SIZE].astype(jnp.float32) for c in cols], 0
        ).astype(jnp.bfloat16)
        scores = lax.dot_general(
            query, k, (((1,), (1,)), ((), ())), preferred_element_type=jnp.float32
        ) * (1.0 / HEAD_SIZE**0.5)
        scores = jnp.where(seen, scores, -1e30)
        top = jnp.max(scores, -1, keepdims=True)
        e = jnp.where(seen, jnp.exp(scores - top), 0.0)
        weights = (e / jnp.sum(e, -1, keepdims=True)).astype(jnp.bfloat16)
        out = jnp.dot(weights, v, preferred_element_type=jnp.float32)
        for g, c in enumerate(cols):
            here = slice(c, c + HEAD_SIZE)
            got = out[g * STEPS : (g + 1) * STEPS].astype(jnp.bfloat16)
            attended[:, here] = got
            mixed = residual[:, here].astype(jnp.float32) + got.astype(jnp.float32)
            squares += jnp.sum(mixed * mixed, -1, keepdims=True)
            sent[:, here] = (mixed * gain[:, here]).astype(jnp.bfloat16)
    sent[:, width:] = pair(squares)


def forward_kernel(blocks, workers, narrow, *refs):
    count = blocks * workers
    arrived, (gate_held, up_held, gate, up), rest = refs[:blocks], refs[blocks:][:4], refs[blocks + 4 :]
    outs, (x, slots, sems) = rest[:-3], rest[-3:]
    me = lax.axis_index("wide") - count
    features, columns = gate.shape
    half = features // narrow
    early = gate_held.shape[1]
    room, _, _, tile = slots.shape
    units = list(range(early, columns, tile))

    def stream(j):
        s = j % room
        here = pl.ds(units[j], tile)
        return [
            pltpu.make_async_copy(m.at[:, here], slots.at[s, i], sems.at[s, i])
            for i, m in enumerate((gate, up))
        ]

    @pl.when(me >= 0)
    def _():
        for j in range(min(room, len(units))):
            for copy in stream(j):
                copy.start()
        lines, tails = [], []
        for block in arrived:
            for shift in range(workers):
                owner = lax.rem(me + shift, workers)
                halves = [block[owner * narrow + n] for n in range(narrow)]
                lines.append(
                    jnp.concatenate([h[:, :half] for h in halves], 1).astype(jnp.float32)
                )
                tails.append(sum(h[:, half:].astype(jnp.float32) for h in halves))
        pad = x.shape[0] - STEPS * count
        if pad:
            lines.append(jnp.zeros((pad, features), jnp.float32))
            tails.append(jnp.zeros((pad, TAIL), jnp.float32))
        x[...] = jnp.concatenate(lines, 0).astype(jnp.bfloat16)
        squares = jnp.sum(jnp.concatenate(tails, 0), -1, keepdims=True)
        r = lax.rsqrt(squares / D + EPS)

        def produce(at, gate_tile, up_tile):
            g = jnp.dot(x[...], gate_tile, preferred_element_type=jnp.float32) * r
            u = jnp.dot(x[...], up_tile, preferred_element_type=jnp.float32) * r
            hidden = (g / (1.0 + jnp.exp(-g)) * u).astype(jnp.bfloat16)
            for i in range(count):
                out = outs[(blocks - 1 - i // workers) * workers + i % workers]
                out[:, at : at + tile] = hidden[i * STEPS : (i + 1) * STEPS]

        waiting = list(range(0, early, tile))

        def resident(some):
            for at in waiting[:some]:
                produce(at, gate_held[:, at : at + tile], up_held[:, at : at + tile])
            del waiting[:some]

        for j, at in enumerate(units):
            resident(AHEAD[j] if j < len(AHEAD) else 0)
            if j == len(units) - 1:
                resident(len(waiting))
            for copy in stream(j):
                copy.wait()
            produce(at, slots[j % room, 0], slots[j % room, 1])
            if j + room < len(units):
                for copy in stream(j + room):
                    copy.start()
        if not units:
            resident(len(waiting))


def finish_kernel(blocks, workers, attended, *refs):
    results, (attended_out, out) = refs[:-2], refs[-2:]
    attended_out[...] = attended[...]
    if len(results) == 1:
        out[...] = results[0][...]
        return
    me = lax.axis_index("wide")
    columns = results[0].shape[1]

    @pl.when(me >= blocks * workers)
    def _():
        out[...] = jnp.zeros_like(out)

    for i, result in enumerate(results):
        b, shift = divmod(i, workers)

        @pl.when((me >= b * workers) & (me < (b + 1) * workers))
        def _():
            k = lax.rem(me - b * workers + workers - shift, workers)
            out[:, pl.ds(pl.multiple_of(k * columns, 128), columns)] = result[...]


def shards(queries, new_kv, keys, values, lengths, residual, gain, gate, up):
    wide = lax.axis_size("wide")
    narrow = lax.axis_size("narrow")
    serving = wide * 3 // 4
    workers = wide - serving
    blocks = serving // workers
    half = queries.shape[2]
    features, _, columns = gate.shape
    vmem = pl.BlockSpec(memory_space=pltpu.VMEM)
    hbm = pl.BlockSpec(memory_space=pltpu.HBM)
    owner = lax.axis_index("wide") < serving

    def in_hbm(a):
        return pltpu.with_memory_space_constraint(a, pltpu.HBM)

    gate = gate.reshape(features, columns)
    up = up.reshape(features, columns)
    operands = (
        lengths.reshape(1, 1),
        queries.reshape(STEPS, half),
        new_kv.reshape(STEPS, 2, -1),
        keys.reshape(keys.shape[1:]),
        values.reshape(values.shape[1:]),
        residual.reshape(STEPS, half),
        gain.reshape(1, half),
    )
    groups = [
        [w * narrow + n for w in range(at, at + workers) for n in range(narrow)]
        for at in range(0, wide, workers)
    ]
    shapes = (
        jax.ShapeDtypeStruct((STEPS, half), jnp.bfloat16),
        jax.ShapeDtypeStruct((workers * narrow, STEPS, half + TAIL), jnp.bfloat16),
    )

    def serve(*operands):
        attended, sent = pl.pallas_call(
            attend_kernel,
            out_shape=(
                pltpu.VMEM(shapes[0].shape, jnp.bfloat16),
                jax.ShapeDtypeStruct(shapes[1].shape[1:], jnp.bfloat16),
            ),
            in_specs=[hbm] * 7,
            out_specs=(vmem, vmem),
            scratch_shapes=[
                (pltpu.SMEM if o.dtype == jnp.int32 else pltpu.VMEM)(o.shape, o.dtype)
                for o in operands
            ]
            + [pltpu.SemaphoreType.DMA((7,))],
            compiler_params=pltpu.CompilerParams(vmem_limit_bytes=8 << 20),
        )(operands[0], *map(in_hbm, operands[1:]))
        gathered = lax.all_gather(sent, ("wide", "narrow"), axis=0, axis_index_groups=groups)
        return attended, gathered

    def rest(*operands):
        return pl.pallas_call(
            blank_kernel,
            out_shape=(pltpu.VMEM(shapes[0].shape, jnp.bfloat16), shapes[1]),
            out_specs=(vmem, vmem),
            compiler_params=pltpu.CompilerParams(vmem_limit_bytes=8 << 20),
        )()

    attended, block = lax.cond(owner, serve, rest, *operands)
    arrived = [
        lax.ppermute(block, "wide", [(b * workers + j, serving + j) for j in range(workers)])
        for b in range(blocks)
    ]
    tile = TILE if columns % (2 * TILE) == 0 else columns
    early = columns // 2 // tile * tile or columns
    held = [m[:, :early] for m in (gate, up)]
    padded = -(-STEPS * serving // 16) * 16
    hidden = pl.pallas_call(
        functools.partial(forward_kernel, blocks, workers, narrow),
        out_shape=[jax.ShapeDtypeStruct((STEPS, columns), jnp.bfloat16)] * serving,
        in_specs=[vmem] * (blocks + 2) + [hbm, hbm],
        out_specs=[vmem] * serving,
        scratch_shapes=[
            pltpu.VMEM((padded, features), jnp.bfloat16),
            pltpu.VMEM((SLOTS, 2, features, tile), jnp.bfloat16),
            pltpu.SemaphoreType.DMA((SLOTS, 2)),
        ],
        compiler_params=pltpu.CompilerParams(vmem_limit_bytes=18 << 20),
    )(*arrived, *held, in_hbm(gate), in_hbm(up))
    back = [[None] * workers for _ in range(blocks)]
    for b in range(blocks):
        for s in range(workers):
            pairs = [(serving + k, b * workers + (k + s) % workers) for k in range(workers)]
            back[b][s] = lax.ppermute(hidden[(blocks - 1 - b) * workers + s], "wide", pairs)
    aligned = columns % 128 == 0
    if aligned:
        results = [r for some in back for r in some]
    else:
        me = lax.axis_index("wide")
        pieces = []
        for k in range(workers):
            piece = jnp.zeros((), jnp.bfloat16)
            for b in range(blocks):
                for s in range(workers):
                    mine = me == b * workers + (k + s) % workers
                    piece = jnp.where(mine, back[b][s], piece)
            pieces.append(piece)
        results = [jnp.concatenate(pieces, 1)]
    attended, activated = pl.pallas_call(
        functools.partial(finish_kernel, blocks, workers),
        out_shape=(
            jax.ShapeDtypeStruct((STEPS, half), jnp.bfloat16),
            jax.ShapeDtypeStruct((STEPS, workers * columns), jnp.bfloat16),
        ),
        in_specs=[vmem] * (1 + len(results)),
        out_specs=(vmem, vmem),
        compiler_params=pltpu.CompilerParams(vmem_limit_bytes=8 << 20),
    )(attended, *results)
    return attended.reshape(STEPS, 1, half), activated.reshape(STEPS, 1, -1)


def solution(mesh):
    rows = P(None, ("parts", "wide"), "narrow")
    placed = (
        rows,
        P(None, ("parts", "wide"), None, "narrow"),
        P(("parts", "wide"), "narrow", None, None),
        P(("parts", "wide"), "narrow", None, None),
        P(("parts", "wide")),
        rows,
        P("narrow"),
        P(None, "narrow", "wide"),
        P(None, "narrow", "wide"),
    )
    return jax.shard_map(
        shards, mesh=mesh, in_specs=placed, out_specs=(rows, rows), check_vma=False
    )
```

```python
import functools

import jax
import jax.numpy as jnp
from jax import lax
from jax.experimental import pallas as pl
from jax.experimental.pallas import tpu as pltpu
from jax.sharding import PartitionSpec as P

D = 4096
HEAD_SIZE = 128
STEPS = 2
TAIL = 128
EPS = 1e-05
TILE = 256
SLOTS = 4
AHEAD = (3, 1, 1, 1, 1)


def pair(squares):
    high = squares.astype(jnp.bfloat16).astype(jnp.float32)
    lane = lax.broadcasted_iota(jnp.int32, (squares.shape[0], TAIL), 1)
    both = jnp.where(lane == 0, high, jnp.where(lane == 1, squares - high, 0.0))
    return both.astype(jnp.bfloat16)


def fetch_kernel(serving, _, gate, up, gate_held, up_held, sems):
    @pl.when(lax.axis_index("wide") >= serving)
    def _():
        here = pl.ds(0, gate_held.shape[1])
        copies = [
            pltpu.make_async_copy(gate.at[:, here], gate_held, sems.at[0]),
            pltpu.make_async_copy(up.at[:, here], up_held, sems.at[1]),
        ]
        for c in copies:
            c.start()
        for c in copies:
            c.wait()


def blank_kernel(*outs):
    for out in outs:
        out[...] = jnp.zeros_like(out)


def attend_kernel(*refs):
    sources, (attended, sent), held, sems = refs[:7], refs[7:9], refs[9:16], refs[16]
    lengths, q, kv, keys, values, residual, gain = held
    heads, hist, _ = keys.shape
    width = q.shape[1]
    group = width // (heads * HEAD_SIZE)
    copies = [
        pltpu.make_async_copy(source, place, sems.at[i])
        for i, (source, place) in enumerate(zip(sources, held))
    ]
    for c in copies:
        c.start()
    for c in copies:
        c.wait()
    length = lengths[0, 0]
    slot = lax.broadcasted_iota(jnp.int32, (hist, HEAD_SIZE), 0)
    rows = group * STEPS
    place = lax.broadcasted_iota(jnp.int32, (rows, hist), 1)
    step = lax.broadcasted_iota(jnp.int32, (rows, hist), 0) % STEPS
    first = hist - STEPS
    seen = (place < length) | ((place >= first) & (place - first <= step))
    squares = jnp.zeros((STEPS, 1), jnp.float32)
    for h in range(heads):
        lanes = slice(h * HEAD_SIZE, (h + 1) * HEAD_SIZE)
        k, v = keys[h], values[h]
        for t in range(STEPS):
            k = jnp.where(slot == first + t, kv[t, 0:1, lanes], k)
            v = jnp.where(slot == first + t, kv[t, 1:2, lanes], v)
        cols = [(h * group + g) * HEAD_SIZE for g in range(group)]
        query = jnp.concatenate(
            [q[:, c : c + HEAD_SIZE].astype(jnp.float32) for c in cols], 0
        ).astype(jnp.bfloat16)
        scores = lax.dot_general(
            query, k, (((1,), (1,)), ((), ())), preferred_element_type=jnp.float32
        ) * (1.0 / HEAD_SIZE**0.5)
        scores = jnp.where(seen, scores, -1e30)
        top = jnp.max(scores, -1, keepdims=True)
        e = jnp.where(seen, jnp.exp(scores - top), 0.0)
        weights = (e / jnp.sum(e, -1, keepdims=True)).astype(jnp.bfloat16)
        out = jnp.dot(weights, v, preferred_element_type=jnp.float32)
        for g, c in enumerate(cols):
            here = slice(c, c + HEAD_SIZE)
            got = out[g * STEPS : (g + 1) * STEPS].astype(jnp.bfloat16)
            attended[:, here] = got
            mixed = residual[:, here].astype(jnp.float32) + got.astype(jnp.float32)
            squares += jnp.sum(mixed * mixed, -1, keepdims=True)
            sent[:, here] = (mixed * gain[:, here]).astype(jnp.bfloat16)
    sent[:, width:] = pair(squares)


def places(blocks, workers):
    middle = blocks // 2
    leaving = [b for b in range(blocks) if b != middle]
    found = []
    for b in range(blocks):
        for shift in range(workers):
            nth = leaving.index(b) * workers + shift if b != middle else None
            found.append(nth)
    return found


def forward_kernel(blocks, workers, narrow, *refs):
    count = blocks * workers
    arrived, (gate_held, up_held, gate, up), rest = refs[:blocks], refs[blocks:][:4], refs[blocks + 4 :]
    outs, (x, slots, sems) = rest[:-3], rest[-3:]
    me = lax.axis_index("wide") - count
    features, columns = gate.shape
    half = features // narrow
    early = gate_held.shape[1]
    room, _, _, tile = slots.shape
    units = list(range(early, columns, tile))

    def stream(j):
        s = j % room
        here = pl.ds(units[j], tile)
        return [
            pltpu.make_async_copy(m.at[:, here], slots.at[s, i], sems.at[s, i])
            for i, m in enumerate((gate, up))
        ]

    @pl.when(me >= 0)
    def _():
        for j in range(min(room, len(units))):
            for copy in stream(j):
                copy.start()
        lines, tails = [], []
        for block in arrived:
            for shift in range(workers):
                owner = lax.rem(me + shift, workers)
                halves = [block[owner * narrow + n] for n in range(narrow)]
                lines.append(
                    jnp.concatenate([h[:, :half] for h in halves], 1).astype(jnp.float32)
                )
                tails.append(sum(h[:, half:].astype(jnp.float32) for h in halves))
        pad = x.shape[0] - STEPS * count
        if pad:
            lines.append(jnp.zeros((pad, features), jnp.float32))
            tails.append(jnp.zeros((pad, TAIL), jnp.float32))
        x[...] = jnp.concatenate(lines, 0).astype(jnp.bfloat16)
        squares = jnp.sum(jnp.concatenate(tails, 0), -1, keepdims=True)
        r = lax.rsqrt(squares / D + EPS)

        def produce(at, gate_tile, up_tile):
            g = jnp.dot(x[...], gate_tile, preferred_element_type=jnp.float32) * r
            u = jnp.dot(x[...], up_tile, preferred_element_type=jnp.float32) * r
            hidden = (g / (1.0 + jnp.exp(-g)) * u).astype(jnp.bfloat16)
            for i, place in enumerate(places(blocks, workers)):
                rows = hidden[i * STEPS : (i + 1) * STEPS]
                if place is None:
                    outs[-1][i % workers, :, at : at + tile] = rows
                else:
                    outs[place][:, at : at + tile] = rows

        waiting = list(range(0, early, tile))

        def resident(some):
            for at in waiting[:some]:
                produce(at, gate_held[:, at : at + tile], up_held[:, at : at + tile])
            del waiting[:some]

        for j, at in enumerate(units):
            resident(AHEAD[j] if j < len(AHEAD) else 0)
            if j == len(units) - 1:
                resident(len(waiting))
            for copy in stream(j):
                copy.wait()
            produce(at, slots[j % room, 0], slots[j % room, 1])
            if j + room < len(units):
                for copy in stream(j + room):
                    copy.start()
        if not units:
            resident(len(waiting))


def finish_kernel(blocks, workers, attended, gathered, *refs):
    results, (attended_out, out) = refs[:-2], refs[-2:]
    me = lax.axis_index("wide")
    block, place = me // workers, lax.rem(me, workers)
    columns = gathered.shape[3]
    attended_out[...] = attended[...]

    @pl.when(block >= blocks)
    def _():
        out[...] = jnp.zeros_like(out)

    @pl.when(block == blocks // 2)
    def _():
        for k in range(workers):
            shift = lax.rem(place + workers - k, workers)
            out[:, k * columns : (k + 1) * columns] = gathered[k, shift]

    if not results:
        return

    for i, nth in enumerate(places(blocks, workers)):
        if nth is not None:

            @pl.when(block == i // workers)
            def _(i=i, nth=nth):
                k = lax.rem(place + workers - i % workers, workers)
                out[:, pl.ds(pl.multiple_of(k * columns, 128), columns)] = results[nth][...]


def shards(queries, new_kv, keys, values, lengths, residual, gain, gate, up):
    wide = lax.axis_size("wide")
    narrow = lax.axis_size("narrow")
    serving = wide * 3 // 4
    workers = wide - serving
    blocks = serving // workers
    half = queries.shape[2]
    features, _, columns = gate.shape
    vmem = pl.BlockSpec(memory_space=pltpu.VMEM)
    hbm = pl.BlockSpec(memory_space=pltpu.HBM)
    owner = lax.axis_index("wide") < serving

    def in_hbm(a):
        return pltpu.with_memory_space_constraint(a, pltpu.HBM)

    gate = in_hbm(gate.reshape(features, columns))
    up = in_hbm(up.reshape(features, columns))
    operands = (
        lengths.reshape(1, 1),
        queries.reshape(STEPS, half),
        new_kv.reshape(STEPS, 2, -1),
        keys.reshape(keys.shape[1:]),
        values.reshape(values.shape[1:]),
        residual.reshape(STEPS, half),
        gain.reshape(1, half),
    )
    groups = [
        [w * narrow + n for w in range(at, at + workers) for n in range(narrow)]
        for at in range(0, wide, workers)
    ]
    shapes = (
        jax.ShapeDtypeStruct((STEPS, half), jnp.bfloat16),
        jax.ShapeDtypeStruct((workers * narrow, STEPS, half + TAIL), jnp.bfloat16),
    )

    def serve(*operands):
        attended, sent = pl.pallas_call(
            attend_kernel,
            out_shape=(
                pltpu.VMEM(shapes[0].shape, jnp.bfloat16),
                jax.ShapeDtypeStruct(shapes[1].shape[1:], jnp.bfloat16),
            ),
            in_specs=[hbm] * 7,
            out_specs=(vmem, vmem),
            scratch_shapes=[
                (pltpu.SMEM if o.dtype == jnp.int32 else pltpu.VMEM)(o.shape, o.dtype)
                for o in operands
            ]
            + [pltpu.SemaphoreType.DMA((7,))],
            compiler_params=pltpu.CompilerParams(vmem_limit_bytes=8 << 20),
        )(operands[0], *map(in_hbm, operands[1:]))
        gathered = lax.all_gather(sent, ("wide", "narrow"), axis=0, axis_index_groups=groups)
        return attended, gathered

    def rest(*operands):
        return pl.pallas_call(
            blank_kernel,
            out_shape=(pltpu.VMEM(shapes[0].shape, jnp.bfloat16), shapes[1]),
            out_specs=(vmem, vmem),
            compiler_params=pltpu.CompilerParams(vmem_limit_bytes=8 << 20),
        )()

    attended, block = lax.cond(owner, serve, rest, *operands)
    arrived = [
        lax.ppermute(block, "wide", [(b * workers + j, serving + j) for j in range(workers)])
        for b in range(blocks)
    ]
    tile = TILE if columns % (2 * TILE) == 0 else columns
    early = columns // 2 // tile * tile or columns
    held = pl.pallas_call(
        functools.partial(fetch_kernel, serving),
        out_shape=[pltpu.VMEM((features, early), jnp.bfloat16)] * 2,
        in_specs=[pl.BlockSpec(memory_space=pl.ANY), hbm, hbm],
        out_specs=[vmem] * 2,
        scratch_shapes=[pltpu.SemaphoreType.DMA((2,))],
        compiler_params=pltpu.CompilerParams(vmem_limit_bytes=4 << 20),
        cost_estimate=pl.CostEstimate(
            flops=0, bytes_accessed=early * 4 * features, transcendentals=0
        ),
    )(block, gate, up)
    padded = -(-STEPS * serving // 16) * 16
    together = jax.ShapeDtypeStruct((workers, STEPS, columns), jnp.bfloat16)
    *hidden, shared = pl.pallas_call(
        functools.partial(forward_kernel, blocks, workers, narrow),
        out_shape=[jax.ShapeDtypeStruct((STEPS, columns), jnp.bfloat16)] * (serving - workers)
        + [together],
        in_specs=[vmem] * (blocks + 2) + [hbm, hbm],
        out_specs=[vmem] * (serving - workers + 1),
        scratch_shapes=[
            pltpu.VMEM((padded, features), jnp.bfloat16),
            pltpu.VMEM((SLOTS, 2, features, tile), jnp.bfloat16),
            pltpu.SemaphoreType.DMA((SLOTS, 2)),
        ],
        compiler_params=pltpu.CompilerParams(vmem_limit_bytes=18 << 20),
    )(*arrived, *held, gate, up)
    middle = blocks // 2
    shared = lax.ppermute(
        shared, "wide", [(serving + k, middle * workers + k) for k in range(workers)]
    )
    peers = [list(range(at, at + workers)) for at in range(0, wide, workers)]

    def skip(shared):
        return pl.pallas_call(
            blank_kernel,
            out_shape=jax.ShapeDtypeStruct((workers, *shared.shape), jnp.bfloat16),
            out_specs=vmem,
            compiler_params=pltpu.CompilerParams(vmem_limit_bytes=8 << 20),
        )()

    gathered = lax.cond(
        lax.axis_index("wide") // workers == middle,
        lambda shared: lax.all_gather(shared, "wide", axis=0, axis_index_groups=peers),
        skip,
        shared,
    )
    results = list(hidden)
    for i, nth in enumerate(places(blocks, workers)):
        if nth is not None:
            b, s = divmod(i, workers)
            pairs = [(serving + k, b * workers + (k + s) % workers) for k in range(workers)]
            results[nth] = lax.ppermute(hidden[nth], "wide", pairs)
    aligned = columns % 128 == 0
    attended, activated = pl.pallas_call(
        functools.partial(finish_kernel, blocks, workers),
        out_shape=(
            jax.ShapeDtypeStruct((STEPS, half), jnp.bfloat16),
            jax.ShapeDtypeStruct((STEPS, workers * columns), jnp.bfloat16),
        ),
        in_specs=[vmem] * (2 + (len(results) if aligned else 0)),
        out_specs=(vmem, vmem),
        compiler_params=pltpu.CompilerParams(vmem_limit_bytes=8 << 20),
    )(attended, gathered, *(results if aligned else []))
    if not aligned:
        me = lax.axis_index("wide")
        pieces = []
        for k in range(workers):
            piece = activated[:, k * columns : (k + 1) * columns]
            for i, nth in enumerate(places(blocks, workers)):
                if nth is not None:
                    mine = me == i // workers * workers + (k + i) % workers
                    piece = jnp.where(mine, results[nth], piece)
            pieces.append(piece)
        activated = jnp.concatenate(pieces, 1)
    return attended.reshape(STEPS, 1, half), activated.reshape(STEPS, 1, -1)


def solution(mesh):
    rows = P(None, ("parts", "wide"), "narrow")
    placed = (
        rows,
        P(None, ("parts", "wide"), None, "narrow"),
        P(("parts", "wide"), "narrow", None, None),
        P(("parts", "wide"), "narrow", None, None),
        P(("parts", "wide")),
        rows,
        P("narrow"),
        P(None, "narrow", "wide"),
        P(None, "narrow", "wide"),
    )
    return jax.shard_map(
        shards, mesh=mesh, in_specs=placed, out_specs=(rows, rows), check_vma=False
    )
```

```python
import functools

import jax
import jax.numpy as jnp
from jax import lax
from jax.experimental import pallas as pl
from jax.experimental.pallas import tpu as pltpu
from jax.sharding import PartitionSpec as P

D = 4096
HEAD_SIZE = 128
STEPS = 2
TAIL = 128
EPS = 1e-05
TILE = 256
SLOTS = 4
SPAN = 512
AHEAD = (1, 1, 1, 1)


def pair(squares):
    high = squares.astype(jnp.bfloat16).astype(jnp.float32)
    lane = lax.broadcasted_iota(jnp.int32, (squares.shape[0], TAIL), 1)
    both = jnp.where(lane == 0, high, jnp.where(lane == 1, squares - high, 0.0))
    return both.astype(jnp.bfloat16)


def fetch_kernel(serving, _, gate, up, gate_held, up_held, sems):
    @pl.when(lax.axis_index("wide") >= serving)
    def _():
        here = pl.ds(0, gate_held.shape[1])
        copies = [
            pltpu.make_async_copy(gate.at[:, here], gate_held, sems.at[0]),
            pltpu.make_async_copy(up.at[:, here], up_held, sems.at[1]),
        ]
        for c in copies:
            c.start()
        for c in copies:
            c.wait()


def blank_kernel(*outs):
    for out in outs:
        out[...] = jnp.zeros_like(out)


def attend_kernel(*refs):
    sources, (attended, sent), held, sems = refs[:7], refs[7:9], refs[9:16], refs[16]
    lengths, q, kv, keys, values, residual, gain = held
    heads, hist, _ = keys.shape
    width = q.shape[1]
    group = width // (heads * HEAD_SIZE)
    copies = [
        pltpu.make_async_copy(source, place, sems.at[i])
        for i, (source, place) in enumerate(zip(sources, held))
    ]
    for c in copies:
        c.start()
    for c in copies:
        c.wait()
    length = lengths[0, 0]
    first = hist - STEPS
    for h in range(heads):
        lanes = slice(h * HEAD_SIZE, (h + 1) * HEAD_SIZE)
        for t in range(STEPS):
            keys[h, first + t : first + t + 1, :] = kv[t, 0:1, lanes]
            values[h, first + t : first + t + 1, :] = kv[t, 1:2, lanes]
    rows = heads * group * STEPS
    place = lax.broadcasted_iota(jnp.int32, (rows, hist), 1)
    step = lax.broadcasted_iota(jnp.int32, (rows, hist), 0) % STEPS
    seen = (place < length) | ((place >= first) & (place - first <= step))
    cols = [c * HEAD_SIZE for c in range(heads * group)]
    query = jnp.concatenate([q[:, c : c + HEAD_SIZE].astype(jnp.float32) for c in cols], 0)
    query = query.astype(jnp.bfloat16).reshape(heads, group * STEPS, HEAD_SIZE)
    scores = jnp.concatenate(
        [
            lax.dot_general(
                query[h], keys[h], (((1,), (1,)), ((), ())), preferred_element_type=jnp.float32
            )
            for h in range(heads)
        ],
        0,
    ) * (1.0 / HEAD_SIZE**0.5)
    scores = jnp.where(seen, scores, -1e30)
    top = jnp.max(scores, -1, keepdims=True)
    e = jnp.where(seen, jnp.exp(scores - top), 0.0)
    weights = (e / jnp.sum(e, -1, keepdims=True)).astype(jnp.bfloat16)
    weights = weights.reshape(heads, group * STEPS, hist)
    outs = [
        jnp.dot(weights[h], values[h], preferred_element_type=jnp.float32) for h in range(heads)
    ]
    squares = jnp.zeros((STEPS, HEAD_SIZE), jnp.float32)
    for i, c in enumerate(cols):
        here = slice(c, c + HEAD_SIZE)
        g = i % group * STEPS
        got = outs[i // group][g : g + STEPS].astype(jnp.bfloat16)
        attended[:, here] = got
        mixed = residual[:, here].astype(jnp.float32) + got.astype(jnp.float32)
        squares += mixed * mixed
        sent[:, here] = (mixed * gain[:, here]).astype(jnp.bfloat16)
    squares = jnp.sum(squares, -1, keepdims=True)
    sent[:, width:] = pair(squares)


def places(blocks, workers):
    middle = blocks // 2
    leaving = [b for b in range(blocks) if b != middle]
    found = []
    for b in range(blocks):
        for shift in range(workers):
            nth = leaving.index(b) * workers + shift if b != middle else None
            found.append(nth)
    return found


def forward_kernel(blocks, workers, narrow, *refs):
    count = blocks * workers
    arrived, (gate_held, up_held, gate, up), rest = refs[:blocks], refs[blocks:][:4], refs[blocks + 4 :]
    outs, (x, slots, sems) = rest[:-3], rest[-3:]
    me = lax.axis_index("wide") - count
    features, columns = gate.shape
    half = features // narrow
    early = gate_held.shape[1]
    room, _, _, tile = slots.shape
    units = list(range(early, columns, tile))

    def stream(j):
        s = j % room
        here = pl.ds(units[j], tile)
        return [
            pltpu.make_async_copy(m.at[:, here], slots.at[s, i], sems.at[s, i])
            for i, m in enumerate((gate, up))
        ]

    @pl.when(me >= 0)
    def _():
        for j in range(min(room, len(units))):
            for copy in stream(j):
                copy.start()
        lines, tails = [], []
        for block in arrived:
            for shift in range(workers):
                owner = lax.rem(me + shift, workers)
                halves = [block[owner * narrow + n] for n in range(narrow)]
                lines.append(
                    jnp.concatenate([h[:, :half] for h in halves], 1).astype(jnp.float32)
                )
                tails.append(sum(h[:, half:].astype(jnp.float32) for h in halves))
        pad = x.shape[0] - STEPS * count
        if pad:
            lines.append(jnp.zeros((pad, features), jnp.float32))
            tails.append(jnp.zeros((pad, TAIL), jnp.float32))
        x[...] = jnp.concatenate(lines, 0).astype(jnp.bfloat16)
        squares = jnp.sum(jnp.concatenate(tails, 0), -1, keepdims=True)
        r = lax.rsqrt(squares / D + EPS)

        def produce(at, gate_tile, up_tile):
            g = jnp.dot(x[...], gate_tile, preferred_element_type=jnp.float32) * r
            u = jnp.dot(x[...], up_tile, preferred_element_type=jnp.float32) * r
            hidden = (g / (1.0 + jnp.exp(-g)) * u).astype(jnp.bfloat16)
            for i, place in enumerate(places(blocks, workers)):
                rows = hidden[i * STEPS : (i + 1) * STEPS]
                if place is None:
                    outs[-1][i % workers, :, at : at + rows.shape[1]] = rows
                else:
                    outs[place][:, at : at + rows.shape[1]] = rows

        waiting = list(range(0, early, SPAN))

        def resident(some):
            for at in waiting[:some]:
                end = min(at + SPAN, early)
                produce(at, gate_held[:, at:end], up_held[:, at:end])
            del waiting[:some]

        for j, at in enumerate(units):
            resident(AHEAD[j] if j < len(AHEAD) else 0)
            if j == len(units) - 1:
                resident(len(waiting))
            for copy in stream(j):
                copy.wait()
            produce(at, slots[j % room, 0], slots[j % room, 1])
            if j + room < len(units):
                for copy in stream(j + room):
                    copy.start()
        if not units:
            resident(len(waiting))


def finish_kernel(blocks, workers, attended, gathered, *refs):
    results, (attended_out, out) = refs[:-2], refs[-2:]
    me = lax.axis_index("wide")
    block, place = me // workers, lax.rem(me, workers)
    columns = gathered.shape[3]
    attended_out[...] = attended[...]

    @pl.when(block >= blocks)
    def _():
        out[...] = jnp.zeros_like(out)

    @pl.when(block == blocks // 2)
    def _():
        for k in range(workers):
            shift = lax.rem(place + workers - k, workers)
            out[:, k * columns : (k + 1) * columns] = gathered[k, shift]

    if not results:
        return

    for i, nth in enumerate(places(blocks, workers)):
        if nth is not None:

            @pl.when(block == i // workers)
            def _(i=i, nth=nth):
                k = lax.rem(place + workers - i % workers, workers)
                out[:, pl.ds(pl.multiple_of(k * columns, 128), columns)] = results[nth][...]


def shards(queries, new_kv, keys, values, lengths, residual, gain, gate, up):
    wide = lax.axis_size("wide")
    narrow = lax.axis_size("narrow")
    serving = wide * 3 // 4
    workers = wide - serving
    blocks = serving // workers
    half = queries.shape[2]
    features, _, columns = gate.shape
    vmem = pl.BlockSpec(memory_space=pltpu.VMEM)
    hbm = pl.BlockSpec(memory_space=pltpu.HBM)
    owner = lax.axis_index("wide") < serving

    def in_hbm(a):
        return pltpu.with_memory_space_constraint(a, pltpu.HBM)

    gate = in_hbm(gate.reshape(features, columns))
    up = in_hbm(up.reshape(features, columns))
    operands = (
        lengths.reshape(1, 1),
        queries.reshape(STEPS, half),
        new_kv.reshape(STEPS, 2, -1),
        keys.reshape(keys.shape[1:]),
        values.reshape(values.shape[1:]),
        residual.reshape(STEPS, half),
        gain.reshape(1, half),
    )
    groups = [
        [w * narrow + n for w in range(at, at + workers) for n in range(narrow)]
        for at in range(0, wide, workers)
    ]
    shapes = (
        jax.ShapeDtypeStruct((STEPS, half), jnp.bfloat16),
        jax.ShapeDtypeStruct((workers * narrow, STEPS, half + TAIL), jnp.bfloat16),
    )

    def serve(*operands):
        attended, sent = pl.pallas_call(
            attend_kernel,
            out_shape=(
                pltpu.VMEM(shapes[0].shape, jnp.bfloat16),
                jax.ShapeDtypeStruct(shapes[1].shape[1:], jnp.bfloat16),
            ),
            in_specs=[hbm] * 7,
            out_specs=(vmem, vmem),
            scratch_shapes=[
                (pltpu.SMEM if o.dtype == jnp.int32 else pltpu.VMEM)(o.shape, o.dtype)
                for o in operands
            ]
            + [pltpu.SemaphoreType.DMA((7,))],
            compiler_params=pltpu.CompilerParams(vmem_limit_bytes=8 << 20),
        )(operands[0], *map(in_hbm, operands[1:]))
        gathered = lax.all_gather(sent, ("wide", "narrow"), axis=0, axis_index_groups=groups)
        return attended, gathered

    def rest(*operands):
        return pl.pallas_call(
            blank_kernel,
            out_shape=(pltpu.VMEM(shapes[0].shape, jnp.bfloat16), shapes[1]),
            out_specs=(vmem, vmem),
            compiler_params=pltpu.CompilerParams(vmem_limit_bytes=8 << 20),
        )()

    attended, block = lax.cond(owner, serve, rest, *operands)
    arrived = [
        lax.ppermute(block, "wide", [(b * workers + j, serving + j) for j in range(workers)])
        for b in range(blocks)
    ]
    tile = TILE if columns % (2 * TILE) == 0 else columns
    early = columns // 2 // tile * tile or columns
    held = pl.pallas_call(
        functools.partial(fetch_kernel, serving),
        out_shape=[pltpu.VMEM((features, early), jnp.bfloat16)] * 2,
        in_specs=[pl.BlockSpec(memory_space=pl.ANY), hbm, hbm],
        out_specs=[vmem] * 2,
        scratch_shapes=[pltpu.SemaphoreType.DMA((2,))],
        compiler_params=pltpu.CompilerParams(vmem_limit_bytes=4 << 20),
        cost_estimate=pl.CostEstimate(
            flops=0, bytes_accessed=early * 4 * features, transcendentals=0
        ),
    )(block, gate, up)
    padded = -(-STEPS * serving // 16) * 16
    together = jax.ShapeDtypeStruct((workers, STEPS, columns), jnp.bfloat16)
    *hidden, shared = pl.pallas_call(
        functools.partial(forward_kernel, blocks, workers, narrow),
        out_shape=[jax.ShapeDtypeStruct((STEPS, columns), jnp.bfloat16)] * (serving - workers)
        + [together],
        in_specs=[vmem] * (blocks + 2) + [hbm, hbm],
        out_specs=[vmem] * (serving - workers + 1),
        scratch_shapes=[
            pltpu.VMEM((padded, features), jnp.bfloat16),
            pltpu.VMEM((SLOTS, 2, features, tile), jnp.bfloat16),
            pltpu.SemaphoreType.DMA((SLOTS, 2)),
        ],
        compiler_params=pltpu.CompilerParams(vmem_limit_bytes=18 << 20),
    )(*arrived, *held, gate, up)
    middle = blocks // 2
    shared = lax.ppermute(
        shared, "wide", [(serving + k, middle * workers + k) for k in range(workers)]
    )
    peers = [list(range(at, at + workers)) for at in range(0, wide, workers)]

    def skip(shared):
        return pl.pallas_call(
            blank_kernel,
            out_shape=jax.ShapeDtypeStruct((workers, *shared.shape), jnp.bfloat16),
            out_specs=vmem,
            compiler_params=pltpu.CompilerParams(vmem_limit_bytes=8 << 20),
        )()

    gathered = lax.cond(
        lax.axis_index("wide") // workers == middle,
        lambda shared: lax.all_gather(shared, "wide", axis=0, axis_index_groups=peers),
        skip,
        shared,
    )
    results = list(hidden)
    for i, nth in enumerate(places(blocks, workers)):
        if nth is not None:
            b, s = divmod(i, workers)
            pairs = [(serving + k, b * workers + (k + s) % workers) for k in range(workers)]
            results[nth] = lax.ppermute(hidden[nth], "wide", pairs)
    aligned = columns % 128 == 0
    attended, activated = pl.pallas_call(
        functools.partial(finish_kernel, blocks, workers),
        out_shape=(
            jax.ShapeDtypeStruct((STEPS, half), jnp.bfloat16),
            jax.ShapeDtypeStruct((STEPS, workers * columns), jnp.bfloat16),
        ),
        in_specs=[vmem] * (2 + (len(results) if aligned else 0)),
        out_specs=(vmem, vmem),
        compiler_params=pltpu.CompilerParams(vmem_limit_bytes=8 << 20),
    )(attended, gathered, *(results if aligned else []))
    if not aligned:
        me = lax.axis_index("wide")
        pieces = []
        for k in range(workers):
            piece = activated[:, k * columns : (k + 1) * columns]
            for i, nth in enumerate(places(blocks, workers)):
                if nth is not None:
                    mine = me == i // workers * workers + (k + i) % workers
                    piece = jnp.where(mine, results[nth], piece)
            pieces.append(piece)
        activated = jnp.concatenate(pieces, 1)
    return attended.reshape(STEPS, 1, half), activated.reshape(STEPS, 1, -1)


def solution(mesh):
    rows = P(None, ("parts", "wide"), "narrow")
    placed = (
        rows,
        P(None, ("parts", "wide"), None, "narrow"),
        P(("parts", "wide"), "narrow", None, None),
        P(("parts", "wide"), "narrow", None, None),
        P(("parts", "wide")),
        rows,
        P("narrow"),
        P(None, "narrow", "wide"),
        P(None, "narrow", "wide"),
    )
    return jax.shard_map(
        shards, mesh=mesh, in_specs=placed, out_specs=(rows, rows), check_vma=False
    )
```

```python
import functools

import jax
import jax.numpy as jnp
from jax import lax
from jax.experimental import pallas as pl
from jax.experimental.pallas import tpu as pltpu
from jax.sharding import PartitionSpec as P

D = 4096
HEAD_SIZE = 128
STEPS = 2
TAIL = 128
EPS = 1e-05
TILE = 256
SLOTS = 4
AHEAD = (3, 1, 1, 1, 1)


def pair(squares):
    high = squares.astype(jnp.bfloat16).astype(jnp.float32)
    lane = lax.broadcasted_iota(jnp.int32, (squares.shape[0], TAIL), 1)
    both = jnp.where(lane == 0, high, jnp.where(lane == 1, squares - high, 0.0))
    return both.astype(jnp.bfloat16)


def fetch_kernel(serving, _, gate, up, gate_held, up_held, sems):
    @pl.when(lax.axis_index("wide") >= serving)
    def _():
        here = pl.ds(0, gate_held.shape[1])
        copies = [
            pltpu.make_async_copy(gate.at[:, here], gate_held, sems.at[0]),
            pltpu.make_async_copy(up.at[:, here], up_held, sems.at[1]),
        ]
        for c in copies:
            c.start()
        for c in copies:
            c.wait()


def blank_kernel(*outs):
    for out in outs:
        out[...] = jnp.zeros_like(out)


def attend_kernel(*refs):
    sources, (attended, sent), held, sems = refs[:7], refs[7:9], refs[9:16], refs[16]
    lengths, q, kv, keys, values, residual, gain = held
    heads, hist, _ = keys.shape
    width = q.shape[1]
    group = width // (heads * HEAD_SIZE)
    copies = [
        pltpu.make_async_copy(source, place, sems.at[i])
        for i, (source, place) in enumerate(zip(sources, held))
    ]
    for c in copies:
        c.start()
    for c in copies:
        c.wait()
    length = lengths[0, 0]
    first = hist - STEPS
    for h in range(heads):
        lanes = slice(h * HEAD_SIZE, (h + 1) * HEAD_SIZE)
        for t in range(STEPS):
            keys[h, first + t : first + t + 1, :] = kv[t, 0:1, lanes]
            values[h, first + t : first + t + 1, :] = kv[t, 1:2, lanes]
    rows = heads * group * STEPS
    place = lax.broadcasted_iota(jnp.int32, (rows, hist), 1)
    step = lax.broadcasted_iota(jnp.int32, (rows, hist), 0) % STEPS
    seen = (place < length) | ((place >= first) & (place - first <= step))
    cols = [c * HEAD_SIZE for c in range(heads * group)]
    query = jnp.concatenate([q[:, c : c + HEAD_SIZE].astype(jnp.float32) for c in cols], 0)
    query = query.astype(jnp.bfloat16).reshape(heads, group * STEPS, HEAD_SIZE)
    scores = jnp.concatenate(
        [
            lax.dot_general(
                query[h], keys[h], (((1,), (1,)), ((), ())), preferred_element_type=jnp.float32
            )
            for h in range(heads)
        ],
        0,
    ) * (1.0 / HEAD_SIZE**0.5)
    scores = jnp.where(seen, scores, -1e30)
    top = jnp.max(scores, -1, keepdims=True)
    e = jnp.where(seen, jnp.exp(scores - top), 0.0)
    weights = (e / jnp.sum(e, -1, keepdims=True)).astype(jnp.bfloat16)
    weights = weights.reshape(heads, group * STEPS, hist)
    outs = [
        jnp.dot(weights[h], values[h], preferred_element_type=jnp.float32) for h in range(heads)
    ]
    squares = jnp.zeros((STEPS, HEAD_SIZE), jnp.float32)
    for i, c in enumerate(cols):
        here = slice(c, c + HEAD_SIZE)
        g = i % group * STEPS
        got = outs[i // group][g : g + STEPS].astype(jnp.bfloat16)
        attended[:, here] = got
        mixed = residual[:, here].astype(jnp.float32) + got.astype(jnp.float32)
        squares += mixed * mixed
        sent[:, here] = (mixed * gain[:, here]).astype(jnp.bfloat16)
    squares = jnp.sum(squares, -1, keepdims=True)
    sent[:, width:] = pair(squares)


def places(blocks, workers):
    middle = blocks // 2
    leaving = [b for b in range(blocks) if b != middle]
    found = []
    for b in range(blocks):
        for shift in range(workers):
            nth = leaving.index(b) * workers + shift if b != middle else None
            found.append(nth)
    return found


def forward_kernel(blocks, workers, narrow, *refs):
    count = blocks * workers
    arrived, (gate_held, up_held, gate, up), rest = refs[:blocks], refs[blocks:][:4], refs[blocks + 4 :]
    outs, (x, slots, sems) = rest[:-3], rest[-3:]
    me = lax.axis_index("wide") - count
    features, columns = gate.shape
    half = features // narrow
    early = gate_held.shape[1]
    room, _, _, tile = slots.shape
    units = list(range(early, columns, tile))
    depths = [pl.ds(0, features // 2), pl.ds(features // 2, features // 2)]

    def stream(j):
        s = j % room
        here = pl.ds(units[j], tile)
        return [
            pltpu.make_async_copy(m.at[k, here], slots.at[s, i, k], sems.at[s, i, part])
            for part, k in enumerate(depths)
            for i, m in enumerate((gate, up))
        ]

    @pl.when(me >= 0)
    def _():
        for j in range(min(room, len(units))):
            for copy in stream(j):
                copy.start()
        tails = []
        for b, block in enumerate(arrived):
            for shift in range(workers):
                owner = lax.rem(me + shift, workers)
                at = (b * workers + shift) * STEPS
                tail = jnp.zeros((STEPS, TAIL), jnp.float32)
                for n in range(narrow):
                    piece = block[owner * narrow + n]
                    x[at : at + STEPS, n * half : (n + 1) * half] = piece[:, :half]
                    tail += piece[:, half:].astype(jnp.float32)
                tails.append(tail)
        pad = x.shape[0] - STEPS * count
        if pad:
            x[STEPS * count :, :] = jnp.zeros((pad, features), jnp.bfloat16)
            tails.append(jnp.zeros((pad, TAIL), jnp.float32))
        squares = jnp.sum(jnp.concatenate(tails, 0), -1, keepdims=True)
        r = lax.rsqrt(squares / D + EPS)

        def product(rows, block):
            return jnp.dot(rows, block, preferred_element_type=jnp.float32)

        def produce(at, g, u):
            g, u = g * r, u * r
            hidden = (g / (1.0 + jnp.exp(-g)) * u).astype(jnp.bfloat16)
            for i, place in enumerate(places(blocks, workers)):
                rows = hidden[i * STEPS : (i + 1) * STEPS]
                if place is None:
                    outs[-1][i % workers, :, at : at + rows.shape[1]] = rows
                else:
                    outs[place][:, at : at + rows.shape[1]] = rows

        waiting = list(range(0, early, tile))

        def resident(some):
            for at in waiting[:some]:
                here = slice(at, at + tile)
                produce(at, *[product(x[...], held[:, here]) for held in (gate_held, up_held)])
            del waiting[:some]

        for j, at in enumerate(units):
            resident(AHEAD[j] if j < len(AHEAD) else 0)
            if j == len(units) - 1:
                resident(len(waiting))
            s = j % room
            if j < len(units) - 1:
                for copy in stream(j):
                    copy.wait()
                produce(at, *[product(x[...], slots[s, i]) for i in range(2)])
            else:
                sums = [0.0, 0.0]
                for part in range(2):
                    k = slice(part * features // 2, (part + 1) * features // 2)
                    for copy in stream(j)[part * 2 : part * 2 + 2]:
                        copy.wait()
                    for i in range(2):
                        sums[i] += product(x[:, k], slots[s, i, k])
                produce(at, *sums)
            if j + room < len(units):
                for copy in stream(j + room):
                    copy.start()
        if not units:
            resident(len(waiting))


def finish_kernel(blocks, workers, attended, gathered, *refs):
    results, (attended_out, out) = refs[:-2], refs[-2:]
    me = lax.axis_index("wide")
    block, place = me // workers, lax.rem(me, workers)
    columns = gathered.shape[3]
    attended_out[...] = attended[...]

    @pl.when(block >= blocks)
    def _():
        out[...] = jnp.zeros_like(out)

    @pl.when(block == blocks // 2)
    def _():
        for k in range(workers):
            shift = lax.rem(place + workers - k, workers)
            out[:, k * columns : (k + 1) * columns] = gathered[k, shift]

    if not results:
        return

    for i, nth in enumerate(places(blocks, workers)):
        if nth is not None:

            @pl.when(block == i // workers)
            def _(i=i, nth=nth):
                k = lax.rem(place + workers - i % workers, workers)
                out[:, pl.ds(pl.multiple_of(k * columns, 128), columns)] = results[nth][...]


def shards(queries, new_kv, keys, values, lengths, residual, gain, gate, up):
    wide = lax.axis_size("wide")
    narrow = lax.axis_size("narrow")
    serving = wide * 3 // 4
    workers = wide - serving
    blocks = serving // workers
    half = queries.shape[2]
    features, _, columns = gate.shape
    vmem = pl.BlockSpec(memory_space=pltpu.VMEM)
    hbm = pl.BlockSpec(memory_space=pltpu.HBM)
    owner = lax.axis_index("wide") < serving

    def in_hbm(a):
        return pltpu.with_memory_space_constraint(a, pltpu.HBM)

    gate = in_hbm(gate.reshape(features, columns))
    up = in_hbm(up.reshape(features, columns))
    operands = (
        lengths.reshape(1, 1),
        queries.reshape(STEPS, half),
        new_kv.reshape(STEPS, 2, -1),
        keys.reshape(keys.shape[1:]),
        values.reshape(values.shape[1:]),
        residual.reshape(STEPS, half),
        gain.reshape(1, half),
    )
    groups = [
        [w * narrow + n for w in range(at, at + workers) for n in range(narrow)]
        for at in range(0, wide, workers)
    ]
    shapes = (
        jax.ShapeDtypeStruct((STEPS, half), jnp.bfloat16),
        jax.ShapeDtypeStruct((workers * narrow, STEPS, half + TAIL), jnp.bfloat16),
    )

    def serve(*operands):
        attended, sent = pl.pallas_call(
            attend_kernel,
            out_shape=(
                pltpu.VMEM(shapes[0].shape, jnp.bfloat16),
                jax.ShapeDtypeStruct(shapes[1].shape[1:], jnp.bfloat16),
            ),
            in_specs=[hbm] * 7,
            out_specs=(vmem, vmem),
            scratch_shapes=[
                (pltpu.SMEM if o.dtype == jnp.int32 else pltpu.VMEM)(o.shape, o.dtype)
                for o in operands
            ]
            + [pltpu.SemaphoreType.DMA((7,))],
            compiler_params=pltpu.CompilerParams(vmem_limit_bytes=8 << 20),
        )(operands[0], *map(in_hbm, operands[1:]))
        gathered = lax.all_gather(sent, ("wide", "narrow"), axis=0, axis_index_groups=groups)
        return attended, gathered

    def rest(*operands):
        return pl.pallas_call(
            blank_kernel,
            out_shape=(pltpu.VMEM(shapes[0].shape, jnp.bfloat16), shapes[1]),
            out_specs=(vmem, vmem),
            compiler_params=pltpu.CompilerParams(vmem_limit_bytes=8 << 20),
        )()

    attended, block = lax.cond(owner, serve, rest, *operands)
    arrived = [
        lax.ppermute(block, "wide", [(b * workers + j, serving + j) for j in range(workers)])
        for b in range(blocks)
    ]
    tile = TILE if columns % (2 * TILE) == 0 else columns
    early = columns // 2 // tile * tile or columns
    held = pl.pallas_call(
        functools.partial(fetch_kernel, serving),
        out_shape=[pltpu.VMEM((features, early), jnp.bfloat16)] * 2,
        in_specs=[pl.BlockSpec(memory_space=pl.ANY), hbm, hbm],
        out_specs=[vmem] * 2,
        scratch_shapes=[pltpu.SemaphoreType.DMA((2,))],
        compiler_params=pltpu.CompilerParams(vmem_limit_bytes=4 << 20),
        cost_estimate=pl.CostEstimate(
            flops=0, bytes_accessed=early * 4 * features, transcendentals=0
        ),
    )(block, gate, up)
    padded = -(-STEPS * serving // 16) * 16
    together = jax.ShapeDtypeStruct((workers, STEPS, columns), jnp.bfloat16)
    *hidden, shared = pl.pallas_call(
        functools.partial(forward_kernel, blocks, workers, narrow),
        out_shape=[jax.ShapeDtypeStruct((STEPS, columns), jnp.bfloat16)] * (serving - workers)
        + [together],
        in_specs=[vmem] * (blocks + 2) + [hbm, hbm],
        out_specs=[vmem] * (serving - workers + 1),
        scratch_shapes=[
            pltpu.VMEM((padded, features), jnp.bfloat16),
            pltpu.VMEM((SLOTS, 2, features, tile), jnp.bfloat16),
            pltpu.SemaphoreType.DMA((SLOTS, 2, 2)),
        ],
        compiler_params=pltpu.CompilerParams(vmem_limit_bytes=19 << 20),
    )(*arrived, *held, gate, up)
    middle = blocks // 2
    shared = lax.ppermute(
        shared, "wide", [(serving + k, middle * workers + k) for k in range(workers)]
    )
    peers = [list(range(at, at + workers)) for at in range(0, wide, workers)]

    def skip(shared):
        return pl.pallas_call(
            blank_kernel,
            out_shape=jax.ShapeDtypeStruct((workers, *shared.shape), jnp.bfloat16),
            out_specs=vmem,
            compiler_params=pltpu.CompilerParams(vmem_limit_bytes=8 << 20),
        )()

    gathered = lax.cond(
        lax.axis_index("wide") // workers == middle,
        lambda shared: lax.all_gather(shared, "wide", axis=0, axis_index_groups=peers),
        skip,
        shared,
    )
    results = list(hidden)
    for i, nth in enumerate(places(blocks, workers)):
        if nth is not None:
            b, s = divmod(i, workers)
            pairs = [(serving + k, b * workers + (k + s) % workers) for k in range(workers)]
            results[nth] = lax.ppermute(hidden[nth], "wide", pairs)
    aligned = columns % 128 == 0
    attended, activated = pl.pallas_call(
        functools.partial(finish_kernel, blocks, workers),
        out_shape=(
            jax.ShapeDtypeStruct((STEPS, half), jnp.bfloat16),
            jax.ShapeDtypeStruct((STEPS, workers * columns), jnp.bfloat16),
        ),
        in_specs=[vmem] * (2 + (len(results) if aligned else 0)),
        out_specs=(vmem, vmem),
        compiler_params=pltpu.CompilerParams(vmem_limit_bytes=8 << 20),
    )(attended, gathered, *(results if aligned else []))
    if not aligned:
        me = lax.axis_index("wide")
        pieces = []
        for k in range(workers):
            piece = activated[:, k * columns : (k + 1) * columns]
            for i, nth in enumerate(places(blocks, workers)):
                if nth is not None:
                    mine = me == i // workers * workers + (k + i) % workers
                    piece = jnp.where(mine, results[nth], piece)
            pieces.append(piece)
        activated = jnp.concatenate(pieces, 1)
    return attended.reshape(STEPS, 1, half), activated.reshape(STEPS, 1, -1)


def solution(mesh):
    rows = P(None, ("parts", "wide"), "narrow")
    placed = (
        rows,
        P(None, ("parts", "wide"), None, "narrow"),
        P(("parts", "wide"), "narrow", None, None),
        P(("parts", "wide"), "narrow", None, None),
        P(("parts", "wide")),
        rows,
        P("narrow"),
        P(None, "narrow", "wide"),
        P(None, "narrow", "wide"),
    )
    return jax.shard_map(
        shards, mesh=mesh, in_specs=placed, out_specs=(rows, rows), check_vma=False
    )
```

```python
import functools

import jax
import jax.numpy as jnp
from jax import lax
from jax.experimental import pallas as pl
from jax.experimental.pallas import tpu as pltpu
from jax.sharding import PartitionSpec as P

D = 4096
HEAD_SIZE = 128
STEPS = 2
TAIL = 128
EPS = 1e-05
TILE = 256
SLOTS = 4
AHEAD = (3, 1, 1, 1, 1)
CHUNK = 1024


def pair(squares):
    high = squares.astype(jnp.bfloat16).astype(jnp.float32)
    lane = lax.broadcasted_iota(jnp.int32, (squares.shape[0], TAIL), 1)
    both = jnp.where(lane == 0, high, jnp.where(lane == 1, squares - high, 0.0))
    return both.astype(jnp.bfloat16)


def fetch_kernel(serving, _, gate, up, gate_held, up_held, sems):
    @pl.when(lax.axis_index("wide") >= serving)
    def _():
        here = pl.ds(0, gate_held.shape[1])
        copies = [
            pltpu.make_async_copy(gate.at[:, here], gate_held, sems.at[0]),
            pltpu.make_async_copy(up.at[:, here], up_held, sems.at[1]),
        ]
        for c in copies:
            c.start()
        for c in copies:
            c.wait()


def blank_kernel(*outs):
    for out in outs:
        out[...] = jnp.zeros_like(out)


def attend_kernel(*refs):
    sources, (attended, sent), held, sems = refs[:7], refs[7:9], refs[9:16], refs[16]
    lengths, q, kv, keys, values, residual, gain = held
    heads, hist, _ = keys.shape
    width = q.shape[1]
    group = width // (heads * HEAD_SIZE)
    copies = [
        pltpu.make_async_copy(source, place, sems.at[i])
        for i, (source, place) in enumerate(zip(sources, held))
    ]
    for c in copies:
        c.start()
    for c in copies:
        c.wait()
    length = lengths[0, 0]
    first = hist - STEPS
    for h in range(heads):
        lanes = slice(h * HEAD_SIZE, (h + 1) * HEAD_SIZE)
        for t in range(STEPS):
            keys[h, first + t : first + t + 1, :] = kv[t, 0:1, lanes]
            values[h, first + t : first + t + 1, :] = kv[t, 1:2, lanes]
    rows = heads * group * STEPS
    place = lax.broadcasted_iota(jnp.int32, (rows, hist), 1)
    step = lax.broadcasted_iota(jnp.int32, (rows, hist), 0) % STEPS
    seen = (place < length) | ((place >= first) & (place - first <= step))
    cols = [c * HEAD_SIZE for c in range(heads * group)]
    query = jnp.concatenate([q[:, c : c + HEAD_SIZE].astype(jnp.float32) for c in cols], 0)
    query = query.astype(jnp.bfloat16).reshape(heads, group * STEPS, HEAD_SIZE)
    scores = jnp.concatenate(
        [
            lax.dot_general(
                query[h], keys[h], (((1,), (1,)), ((), ())), preferred_element_type=jnp.float32
            )
            for h in range(heads)
        ],
        0,
    ) * (1.0 / HEAD_SIZE**0.5)
    scores = jnp.where(seen, scores, -1e30)
    top = jnp.max(scores, -1, keepdims=True)
    e = jnp.where(seen, jnp.exp(scores - top), 0.0)
    weights = (e / jnp.sum(e, -1, keepdims=True)).astype(jnp.bfloat16)
    weights = weights.reshape(heads, group * STEPS, hist)
    outs = [
        jnp.dot(weights[h], values[h], preferred_element_type=jnp.float32) for h in range(heads)
    ]
    squares = jnp.zeros((STEPS, HEAD_SIZE), jnp.float32)
    for i, c in enumerate(cols):
        here = slice(c, c + HEAD_SIZE)
        g = i % group * STEPS
        got = outs[i // group][g : g + STEPS].astype(jnp.bfloat16)
        attended[:, here] = got
        mixed = residual[:, here].astype(jnp.float32) + got.astype(jnp.float32)
        squares += mixed * mixed
        sent[:, here] = (mixed * gain[:, here]).astype(jnp.bfloat16)
    squares = jnp.sum(squares, -1, keepdims=True)
    sent[:, width:] = pair(squares)


def places(blocks, workers):
    middle = blocks // 2
    leaving = [b for b in range(blocks) if b != middle]
    found = []
    for b in range(blocks):
        for shift in range(workers):
            nth = leaving.index(b) * workers + shift if b != middle else None
            found.append(nth)
    return found


def forward_kernel(blocks, workers, narrow, *refs):
    count = blocks * workers
    arrived, (gate_held, up_held, gate, up), rest = refs[:blocks], refs[blocks:][:4], refs[blocks + 4 :]
    outs, (x, slots, sems) = rest[:-3], rest[-3:]
    me = lax.axis_index("wide") - count
    features, columns = gate.shape
    half = features // narrow
    early = gate_held.shape[1]
    room, _, _, tile = slots.shape
    units = list(range(early, columns, tile))

    def stream(j):
        s = j % room
        here = pl.ds(units[j], tile)
        size = features // 2 if j == len(units) - 1 else features
        depths = [pl.ds(at, size) for at in range(0, features, size)]
        return [
            pltpu.make_async_copy(m.at[k, here], slots.at[s, i, k], sems.at[s, i, part])
            for part, k in enumerate(depths)
            for i, m in enumerate((gate, up))
        ]

    @pl.when(me >= 0)
    def _():
        for j in range(min(room, len(units))):
            for copy in stream(j):
                copy.start()
        lines, tails = [], []
        for block in arrived:
            for shift in range(workers):
                owner = lax.rem(me + shift, workers)
                halves = [block[owner * narrow + n] for n in range(narrow)]
                lines.append(
                    jnp.concatenate([h[:, :half] for h in halves], 1).astype(jnp.float32)
                )
                tails.append(sum(h[:, half:].astype(jnp.float32) for h in halves))
        pad = x.shape[0] - STEPS * count
        if pad:
            lines.append(jnp.zeros((pad, features), jnp.float32))
            tails.append(jnp.zeros((pad, TAIL), jnp.float32))
        x[...] = jnp.concatenate(lines, 0).astype(jnp.bfloat16)
        squares = jnp.sum(jnp.concatenate(tails, 0), -1, keepdims=True)
        r = lax.rsqrt(squares / D + EPS)

        def multiply(depth, sums, tiles):
            for at in range(depth.start, depth.stop, CHUNK):
                k = slice(at, min(at + CHUNK, depth.stop))
                for i, some in enumerate(tiles):
                    more = jnp.dot(x[:, k], some(k), preferred_element_type=jnp.float32)
                    sums[i] = more if sums[i] is None else sums[i] + more
            return sums

        def produce(at, g, u):
            g, u = g * r, u * r
            hidden = (g / (1.0 + jnp.exp(-g)) * u).astype(jnp.bfloat16)
            for i, place in enumerate(places(blocks, workers)):
                rows = hidden[i * STEPS : (i + 1) * STEPS]
                if place is None:
                    outs[-1][i % workers, :, at : at + tile] = rows
                else:
                    outs[place][:, at : at + tile] = rows

        waiting = list(range(0, early, tile))

        def resident(some):
            for at in waiting[:some]:
                here = slice(at, at + tile)
                tiles = [lambda k, m=m: m[k, here] for m in (gate_held, up_held)]
                produce(at, *multiply(slice(0, features), [None] * 2, tiles))
            del waiting[:some]

        for j, at in enumerate(units):
            resident(AHEAD[j] if j < len(AHEAD) else 0)
            if j == len(units) - 1:
                resident(len(waiting))
            copies, sums = stream(j), [None] * 2
            tiles = [lambda k, i=i, s=j % room: slots[s, i, k, :] for i in range(2)]
            size = features * 2 // len(copies)
            for part in range(len(copies) // 2):
                for copy in copies[part * 2 : part * 2 + 2]:
                    copy.wait()
                multiply(slice(part * size, (part + 1) * size), sums, tiles)
            produce(at, *sums)
            if j + room < len(units):
                for copy in stream(j + room):
                    copy.start()
        if not units:
            resident(len(waiting))


def finish_kernel(blocks, workers, attended, gathered, *refs):
    results, (attended_out, out) = refs[:-2], refs[-2:]
    me = lax.axis_index("wide")
    block, place = me // workers, lax.rem(me, workers)
    columns = gathered.shape[3]
    attended_out[...] = attended[...]

    @pl.when(block >= blocks)
    def _():
        out[...] = jnp.zeros_like(out)

    @pl.when(block == blocks // 2)
    def _():
        for k in range(workers):
            shift = lax.rem(place + workers - k, workers)
            out[:, k * columns : (k + 1) * columns] = gathered[k, shift]

    if not results:
        return

    for i, nth in enumerate(places(blocks, workers)):
        if nth is not None:

            @pl.when(block == i // workers)
            def _(i=i, nth=nth):
                k = lax.rem(place + workers - i % workers, workers)
                out[:, pl.ds(pl.multiple_of(k * columns, 128), columns)] = results[nth][...]


def shards(queries, new_kv, keys, values, lengths, residual, gain, gate, up):
    wide = lax.axis_size("wide")
    narrow = lax.axis_size("narrow")
    serving = wide * 3 // 4
    workers = wide - serving
    blocks = serving // workers
    half = queries.shape[2]
    features, _, columns = gate.shape
    vmem = pl.BlockSpec(memory_space=pltpu.VMEM)
    hbm = pl.BlockSpec(memory_space=pltpu.HBM)
    owner = lax.axis_index("wide") < serving

    def in_hbm(a):
        return pltpu.with_memory_space_constraint(a, pltpu.HBM)

    gate = in_hbm(gate.reshape(features, columns))
    up = in_hbm(up.reshape(features, columns))
    operands = (
        lengths.reshape(1, 1),
        queries.reshape(STEPS, half),
        new_kv.reshape(STEPS, 2, -1),
        keys.reshape(keys.shape[1:]),
        values.reshape(values.shape[1:]),
        residual.reshape(STEPS, half),
        gain.reshape(1, half),
    )
    groups = [
        [w * narrow + n for w in range(at, at + workers) for n in range(narrow)]
        for at in range(0, wide, workers)
    ]
    shapes = (
        jax.ShapeDtypeStruct((STEPS, half), jnp.bfloat16),
        jax.ShapeDtypeStruct((workers * narrow, STEPS, half + TAIL), jnp.bfloat16),
    )

    def serve(*operands):
        attended, sent = pl.pallas_call(
            attend_kernel,
            out_shape=(
                pltpu.VMEM(shapes[0].shape, jnp.bfloat16),
                jax.ShapeDtypeStruct(shapes[1].shape[1:], jnp.bfloat16),
            ),
            in_specs=[hbm] * 7,
            out_specs=(vmem, vmem),
            scratch_shapes=[
                (pltpu.SMEM if o.dtype == jnp.int32 else pltpu.VMEM)(o.shape, o.dtype)
                for o in operands
            ]
            + [pltpu.SemaphoreType.DMA((7,))],
            compiler_params=pltpu.CompilerParams(vmem_limit_bytes=8 << 20),
        )(operands[0], *map(in_hbm, operands[1:]))
        gathered = lax.all_gather(sent, ("wide", "narrow"), axis=0, axis_index_groups=groups)
        return attended, gathered

    def rest(*operands):
        return pl.pallas_call(
            blank_kernel,
            out_shape=(pltpu.VMEM(shapes[0].shape, jnp.bfloat16), shapes[1]),
            out_specs=(vmem, vmem),
            compiler_params=pltpu.CompilerParams(vmem_limit_bytes=8 << 20),
        )()

    attended, block = lax.cond(owner, serve, rest, *operands)
    arrived = [
        lax.ppermute(block, "wide", [(b * workers + j, serving + j) for j in range(workers)])
        for b in range(blocks)
    ]
    tile = TILE if columns % (2 * TILE) == 0 else columns
    early = columns // 2 // tile * tile or columns
    held = pl.pallas_call(
        functools.partial(fetch_kernel, serving),
        out_shape=[pltpu.VMEM((features, early), jnp.bfloat16)] * 2,
        in_specs=[pl.BlockSpec(memory_space=pl.ANY), hbm, hbm],
        out_specs=[vmem] * 2,
        scratch_shapes=[pltpu.SemaphoreType.DMA((2,))],
        compiler_params=pltpu.CompilerParams(vmem_limit_bytes=4 << 20),
        cost_estimate=pl.CostEstimate(
            flops=0, bytes_accessed=early * 4 * features, transcendentals=0
        ),
    )(block, gate, up)
    padded = -(-STEPS * serving // 16) * 16
    together = jax.ShapeDtypeStruct((workers, STEPS, columns), jnp.bfloat16)
    *hidden, shared = pl.pallas_call(
        functools.partial(forward_kernel, blocks, workers, narrow),
        out_shape=[jax.ShapeDtypeStruct((STEPS, columns), jnp.bfloat16)] * (serving - workers)
        + [together],
        in_specs=[vmem] * (blocks + 2) + [hbm, hbm],
        out_specs=[vmem] * (serving - workers + 1),
        scratch_shapes=[
            pltpu.VMEM((padded, features), jnp.bfloat16),
            pltpu.VMEM((SLOTS, 2, features, tile), jnp.bfloat16),
            pltpu.SemaphoreType.DMA((SLOTS, 2, 2)),
        ],
        compiler_params=pltpu.CompilerParams(vmem_limit_bytes=19 << 20),
    )(*arrived, *held, gate, up)
    middle = blocks // 2
    shared = lax.ppermute(
        shared, "wide", [(serving + k, middle * workers + k) for k in range(workers)]
    )
    peers = [list(range(at, at + workers)) for at in range(0, wide, workers)]

    def skip(shared):
        return pl.pallas_call(
            blank_kernel,
            out_shape=jax.ShapeDtypeStruct((workers, *shared.shape), jnp.bfloat16),
            out_specs=vmem,
            compiler_params=pltpu.CompilerParams(vmem_limit_bytes=8 << 20),
        )()

    gathered = lax.cond(
        lax.axis_index("wide") // workers == middle,
        lambda shared: lax.all_gather(shared, "wide", axis=0, axis_index_groups=peers),
        skip,
        shared,
    )
    results = list(hidden)
    for i, nth in enumerate(places(blocks, workers)):
        if nth is not None:
            b, s = divmod(i, workers)
            pairs = [(serving + k, b * workers + (k + s) % workers) for k in range(workers)]
            results[nth] = lax.ppermute(hidden[nth], "wide", pairs)
    aligned = columns % 128 == 0
    attended, activated = pl.pallas_call(
        functools.partial(finish_kernel, blocks, workers),
        out_shape=(
            jax.ShapeDtypeStruct((STEPS, half), jnp.bfloat16),
            jax.ShapeDtypeStruct((STEPS, workers * columns), jnp.bfloat16),
        ),
        in_specs=[vmem] * (2 + (len(results) if aligned else 0)),
        out_specs=(vmem, vmem),
        compiler_params=pltpu.CompilerParams(vmem_limit_bytes=8 << 20),
    )(attended, gathered, *(results if aligned else []))
    if not aligned:
        me = lax.axis_index("wide")
        pieces = []
        for k in range(workers):
            piece = activated[:, k * columns : (k + 1) * columns]
            for i, nth in enumerate(places(blocks, workers)):
                if nth is not None:
                    mine = me == i // workers * workers + (k + i) % workers
                    piece = jnp.where(mine, results[nth], piece)
            pieces.append(piece)
        activated = jnp.concatenate(pieces, 1)
    return attended.reshape(STEPS, 1, half), activated.reshape(STEPS, 1, -1)


def solution(mesh):
    rows = P(None, ("parts", "wide"), "narrow")
    placed = (
        rows,
        P(None, ("parts", "wide"), None, "narrow"),
        P(("parts", "wide"), "narrow", None, None),
        P(("parts", "wide"), "narrow", None, None),
        P(("parts", "wide")),
        rows,
        P("narrow"),
        P(None, "narrow", "wide"),
        P(None, "narrow", "wide"),
    )
    return jax.shard_map(
        shards, mesh=mesh, in_specs=placed, out_specs=(rows, rows), check_vma=False
    )
```

```python
import functools

import jax
import jax.numpy as jnp
from jax import lax
from jax.experimental import pallas as pl
from jax.experimental.pallas import tpu as pltpu
from jax.sharding import PartitionSpec as P

D = 4096
HEAD_SIZE = 128
STEPS = 2
TAIL = 128
EPS = 1e-05
TILE = 256
SLOTS = 4
AHEAD = (3, 1, 1, 1, 1)
CHUNK = 1024
PARTS = 4


def pair(squares):
    high = squares.astype(jnp.bfloat16).astype(jnp.float32)
    lane = lax.broadcasted_iota(jnp.int32, (squares.shape[0], TAIL), 1)
    both = jnp.where(lane == 0, high, jnp.where(lane == 1, squares - high, 0.0))
    return both.astype(jnp.bfloat16)


def fetch_kernel(serving, _, gate, up, gate_held, up_held, sems):
    @pl.when(lax.axis_index("wide") >= serving)
    def _():
        features, early = gate_held.shape
        copies = []
        for part in range(PARTS):
            k = pl.ds(part * features // PARTS, features // PARTS)
            for i, (m, held) in enumerate(((gate, gate_held), (up, up_held))):
                copies.append(
                    pltpu.make_async_copy(m.at[k, pl.ds(0, early)], held.at[k], sems.at[i, part])
                )
        for c in copies:
            c.start()
        for c in copies:
            c.wait()


def blank_kernel(*outs):
    for out in outs:
        out[...] = jnp.zeros_like(out)


def attend_kernel(*refs):
    sources, (attended, sent), held, sems = refs[:7], refs[7:9], refs[9:16], refs[16]
    lengths, q, kv, keys, values, residual, gain = held
    heads, hist, _ = keys.shape
    width = q.shape[1]
    group = width // (heads * HEAD_SIZE)
    copies = [
        pltpu.make_async_copy(source, place, sems.at[i])
        for i, (source, place) in enumerate(zip(sources, held))
    ]
    for c in copies:
        c.start()
    for c in copies:
        c.wait()
    length = lengths[0, 0]
    first = hist - STEPS
    for h in range(heads):
        lanes = slice(h * HEAD_SIZE, (h + 1) * HEAD_SIZE)
        for t in range(STEPS):
            keys[h, first + t : first + t + 1, :] = kv[t, 0:1, lanes]
            values[h, first + t : first + t + 1, :] = kv[t, 1:2, lanes]
    rows = heads * group * STEPS
    place = lax.broadcasted_iota(jnp.int32, (rows, hist), 1)
    step = lax.broadcasted_iota(jnp.int32, (rows, hist), 0) % STEPS
    seen = (place < length) | ((place >= first) & (place - first <= step))
    cols = [c * HEAD_SIZE for c in range(heads * group)]
    query = jnp.concatenate([q[:, c : c + HEAD_SIZE].astype(jnp.float32) for c in cols], 0)
    query = query.astype(jnp.bfloat16).reshape(heads, group * STEPS, HEAD_SIZE)
    scores = jnp.concatenate(
        [
            lax.dot_general(
                query[h], keys[h], (((1,), (1,)), ((), ())), preferred_element_type=jnp.float32
            )
            for h in range(heads)
        ],
        0,
    ) * (1.0 / HEAD_SIZE**0.5)
    scores = jnp.where(seen, scores, -1e30)
    top = jnp.max(scores, -1, keepdims=True)
    e = jnp.where(seen, jnp.exp(scores - top), 0.0)
    weights = (e / jnp.sum(e, -1, keepdims=True)).astype(jnp.bfloat16)
    weights = weights.reshape(heads, group * STEPS, hist)
    outs = [
        jnp.dot(weights[h], values[h], preferred_element_type=jnp.float32) for h in range(heads)
    ]
    squares = jnp.zeros((STEPS, HEAD_SIZE), jnp.float32)
    for i, c in enumerate(cols):
        here = slice(c, c + HEAD_SIZE)
        g = i % group * STEPS
        got = outs[i // group][g : g + STEPS].astype(jnp.bfloat16)
        attended[:, here] = got
        mixed = residual[:, here].astype(jnp.float32) + got.astype(jnp.float32)
        squares += mixed * mixed
        sent[:, here] = (mixed * gain[:, here]).astype(jnp.bfloat16)
    squares = jnp.sum(squares, -1, keepdims=True)
    sent[:, width:] = pair(squares)


def places(blocks, workers):
    middle = blocks // 2
    leaving = [b for b in range(blocks) if b != middle]
    found = []
    for b in range(blocks):
        for shift in range(workers):
            nth = leaving.index(b) * workers + shift if b != middle else None
            found.append(nth)
    return found


def forward_kernel(blocks, workers, narrow, *refs):
    count = blocks * workers
    arrived, (gate_held, up_held, gate, up), rest = refs[:blocks], refs[blocks:][:4], refs[blocks + 4 :]
    outs, (x, slots, sems) = rest[:-3], rest[-3:]
    me = lax.axis_index("wide") - count
    features, columns = gate.shape
    half = features // narrow
    early = gate_held.shape[1]
    room, _, _, tile = slots.shape
    units = list(range(early, columns, tile))

    def stream(j):
        s = j % room
        here = pl.ds(units[j], tile)
        size = features // PARTS if j == len(units) - 1 else features
        depths = [pl.ds(at, size) for at in range(0, features, size)]
        return [
            pltpu.make_async_copy(m.at[k, here], slots.at[s, i, k], sems.at[s, i, part])
            for part, k in enumerate(depths)
            for i, m in enumerate((gate, up))
        ]

    @pl.when(me >= 0)
    def _():
        for j in range(min(room, len(units))):
            for copy in stream(j):
                copy.start()
        lines, tails = [], []
        for block in arrived:
            for shift in range(workers):
                owner = lax.rem(me + shift, workers)
                halves = [block[owner * narrow + n] for n in range(narrow)]
                lines.append(
                    jnp.concatenate([h[:, :half] for h in halves], 1).astype(jnp.float32)
                )
                tails.append(sum(h[:, half:].astype(jnp.float32) for h in halves))
        pad = x.shape[0] - STEPS * count
        if pad:
            lines.append(jnp.zeros((pad, features), jnp.float32))
            tails.append(jnp.zeros((pad, TAIL), jnp.float32))
        x[...] = jnp.concatenate(lines, 0).astype(jnp.bfloat16)
        squares = jnp.sum(jnp.concatenate(tails, 0), -1, keepdims=True)
        r = lax.rsqrt(squares / D + EPS)

        def multiply(depth, sums, tiles):
            for at in range(depth.start, depth.stop, CHUNK):
                k = slice(at, min(at + CHUNK, depth.stop))
                for i, some in enumerate(tiles):
                    more = jnp.dot(x[:, k], some(k), preferred_element_type=jnp.float32)
                    sums[i] = more if sums[i] is None else sums[i] + more
            return sums

        def produce(at, g, u):
            g, u = g * r, u * r
            hidden = (g / (1.0 + jnp.exp(-g)) * u).astype(jnp.bfloat16)
            for i, place in enumerate(places(blocks, workers)):
                rows = hidden[i * STEPS : (i + 1) * STEPS]
                if place is None:
                    outs[-1][i % workers, :, at : at + tile] = rows
                else:
                    outs[place][:, at : at + tile] = rows

        waiting = list(range(0, early, tile))

        def resident(some):
            for at in waiting[:some]:
                here = slice(at, at + tile)
                tiles = [lambda k, m=m: m[k, here] for m in (gate_held, up_held)]
                produce(at, *multiply(slice(0, features), [None] * 2, tiles))
            del waiting[:some]

        for j, at in enumerate(units):
            resident(AHEAD[j] if j < len(AHEAD) else 0)
            if j == len(units) - 1:
                resident(len(waiting))
            copies, sums = stream(j), [None] * 2
            tiles = [lambda k, i=i, s=j % room: slots[s, i, k, :] for i in range(2)]
            size = features * 2 // len(copies)
            for part in range(len(copies) // 2):
                for copy in copies[part * 2 : part * 2 + 2]:
                    copy.wait()
                multiply(slice(part * size, (part + 1) * size), sums, tiles)
            produce(at, *sums)
            if j + room < len(units):
                for copy in stream(j + room):
                    copy.start()
        if not units:
            resident(len(waiting))


def finish_kernel(blocks, workers, attended, gathered, *refs):
    results, (attended_out, out) = refs[:-2], refs[-2:]
    me = lax.axis_index("wide")
    block, place = me // workers, lax.rem(me, workers)
    columns = gathered.shape[3]
    attended_out[...] = attended[...]

    @pl.when(block >= blocks)
    def _():
        out[...] = jnp.zeros_like(out)

    @pl.when(block == blocks // 2)
    def _():
        for k in range(workers):
            shift = lax.rem(place + workers - k, workers)
            out[:, k * columns : (k + 1) * columns] = gathered[k, shift]

    if not results:
        return

    for i, nth in enumerate(places(blocks, workers)):
        if nth is not None:

            @pl.when(block == i // workers)
            def _(i=i, nth=nth):
                k = lax.rem(place + workers - i % workers, workers)
                out[:, pl.ds(pl.multiple_of(k * columns, 128), columns)] = results[nth][...]


def shards(queries, new_kv, keys, values, lengths, residual, gain, gate, up):
    wide = lax.axis_size("wide")
    narrow = lax.axis_size("narrow")
    serving = wide * 3 // 4
    workers = wide - serving
    blocks = serving // workers
    half = queries.shape[2]
    features, _, columns = gate.shape
    vmem = pl.BlockSpec(memory_space=pltpu.VMEM)
    hbm = pl.BlockSpec(memory_space=pltpu.HBM)
    owner = lax.axis_index("wide") < serving

    def in_hbm(a):
        return pltpu.with_memory_space_constraint(a, pltpu.HBM)

    gate = in_hbm(gate.reshape(features, columns))
    up = in_hbm(up.reshape(features, columns))
    operands = (
        lengths.reshape(1, 1),
        queries.reshape(STEPS, half),
        new_kv.reshape(STEPS, 2, -1),
        keys.reshape(keys.shape[1:]),
        values.reshape(values.shape[1:]),
        residual.reshape(STEPS, half),
        gain.reshape(1, half),
    )
    groups = [
        [w * narrow + n for w in range(at, at + workers) for n in range(narrow)]
        for at in range(0, wide, workers)
    ]
    shapes = (
        jax.ShapeDtypeStruct((STEPS, half), jnp.bfloat16),
        jax.ShapeDtypeStruct((workers * narrow, STEPS, half + TAIL), jnp.bfloat16),
    )

    def serve(*operands):
        attended, sent = pl.pallas_call(
            attend_kernel,
            out_shape=(
                pltpu.VMEM(shapes[0].shape, jnp.bfloat16),
                jax.ShapeDtypeStruct(shapes[1].shape[1:], jnp.bfloat16),
            ),
            in_specs=[hbm] * 7,
            out_specs=(vmem, vmem),
            scratch_shapes=[
                (pltpu.SMEM if o.dtype == jnp.int32 else pltpu.VMEM)(o.shape, o.dtype)
                for o in operands
            ]
            + [pltpu.SemaphoreType.DMA((7,))],
            compiler_params=pltpu.CompilerParams(vmem_limit_bytes=8 << 20),
        )(operands[0], *map(in_hbm, operands[1:]))
        gathered = lax.all_gather(sent, ("wide", "narrow"), axis=0, axis_index_groups=groups)
        return attended, gathered

    def rest(*operands):
        return pl.pallas_call(
            blank_kernel,
            out_shape=(pltpu.VMEM(shapes[0].shape, jnp.bfloat16), shapes[1]),
            out_specs=(vmem, vmem),
            compiler_params=pltpu.CompilerParams(vmem_limit_bytes=8 << 20),
        )()

    attended, block = lax.cond(owner, serve, rest, *operands)
    arrived = [
        lax.ppermute(block, "wide", [(b * workers + j, serving + j) for j in range(workers)])
        for b in range(blocks)
    ]
    tile = TILE if columns % (2 * TILE) == 0 else columns
    early = columns // 2 // tile * tile or columns
    held = pl.pallas_call(
        functools.partial(fetch_kernel, serving),
        out_shape=[pltpu.VMEM((features, early), jnp.bfloat16)] * 2,
        in_specs=[pl.BlockSpec(memory_space=pl.ANY), hbm, hbm],
        out_specs=[vmem] * 2,
        scratch_shapes=[pltpu.SemaphoreType.DMA((2, PARTS))],
        compiler_params=pltpu.CompilerParams(vmem_limit_bytes=4 << 20),
        cost_estimate=pl.CostEstimate(
            flops=0, bytes_accessed=early * 4 * features, transcendentals=0
        ),
    )(block, gate, up)
    padded = -(-STEPS * serving // 16) * 16
    together = jax.ShapeDtypeStruct((workers, STEPS, columns), jnp.bfloat16)
    *hidden, shared = pl.pallas_call(
        functools.partial(forward_kernel, blocks, workers, narrow),
        out_shape=[jax.ShapeDtypeStruct((STEPS, columns), jnp.bfloat16)] * (serving - workers)
        + [together],
        in_specs=[vmem] * (blocks + 2) + [hbm, hbm],
        out_specs=[vmem] * (serving - workers + 1),
        scratch_shapes=[
            pltpu.VMEM((padded, features), jnp.bfloat16),
            pltpu.VMEM((SLOTS, 2, features, tile), jnp.bfloat16),
            pltpu.SemaphoreType.DMA((SLOTS, 2, PARTS)),
        ],
        compiler_params=pltpu.CompilerParams(vmem_limit_bytes=19 << 20),
    )(*arrived, *held, gate, up)
    middle = blocks // 2
    shared = lax.ppermute(
        shared, "wide", [(serving + k, middle * workers + k) for k in range(workers)]
    )
    peers = [list(range(at, at + workers)) for at in range(0, wide, workers)]

    def skip(shared):
        return pl.pallas_call(
            blank_kernel,
            out_shape=jax.ShapeDtypeStruct((workers, *shared.shape), jnp.bfloat16),
            out_specs=vmem,
            compiler_params=pltpu.CompilerParams(vmem_limit_bytes=8 << 20),
        )()

    gathered = lax.cond(
        lax.axis_index("wide") // workers == middle,
        lambda shared: lax.all_gather(shared, "wide", axis=0, axis_index_groups=peers),
        skip,
        shared,
    )
    results = list(hidden)
    for i, nth in enumerate(places(blocks, workers)):
        if nth is not None:
            b, s = divmod(i, workers)
            pairs = [(serving + k, b * workers + (k + s) % workers) for k in range(workers)]
            results[nth] = lax.ppermute(hidden[nth], "wide", pairs)
    aligned = columns % 128 == 0
    attended, activated = pl.pallas_call(
        functools.partial(finish_kernel, blocks, workers),
        out_shape=(
            jax.ShapeDtypeStruct((STEPS, half), jnp.bfloat16),
            jax.ShapeDtypeStruct((STEPS, workers * columns), jnp.bfloat16),
        ),
        in_specs=[vmem] * (2 + (len(results) if aligned else 0)),
        out_specs=(vmem, vmem),
        compiler_params=pltpu.CompilerParams(vmem_limit_bytes=8 << 20),
    )(attended, gathered, *(results if aligned else []))
    if not aligned:
        me = lax.axis_index("wide")
        pieces = []
        for k in range(workers):
            piece = activated[:, k * columns : (k + 1) * columns]
            for i, nth in enumerate(places(blocks, workers)):
                if nth is not None:
                    mine = me == i // workers * workers + (k + i) % workers
                    piece = jnp.where(mine, results[nth], piece)
            pieces.append(piece)
        activated = jnp.concatenate(pieces, 1)
    return attended.reshape(STEPS, 1, half), activated.reshape(STEPS, 1, -1)


def solution(mesh):
    rows = P(None, ("parts", "wide"), "narrow")
    placed = (
        rows,
        P(None, ("parts", "wide"), None, "narrow"),
        P(("parts", "wide"), "narrow", None, None),
        P(("parts", "wide"), "narrow", None, None),
        P(("parts", "wide")),
        rows,
        P("narrow"),
        P(None, "narrow", "wide"),
        P(None, "narrow", "wide"),
    )
    return jax.shard_map(
        shards, mesh=mesh, in_specs=placed, out_specs=(rows, rows), check_vma=False
    )
```

```python
import functools

import jax
import jax.numpy as jnp
from jax import lax
from jax.experimental import pallas as pl
from jax.experimental.pallas import tpu as pltpu
from jax.sharding import PartitionSpec as P

D = 4096
HEAD_SIZE = 128
STEPS = 2
TAIL = 128
EPS = 1e-05
TILE = 256
SLOTS = 4
AHEAD = (3, 1, 1, 1, 1)
CHUNK = 512


def pair(squares):
    high = squares.astype(jnp.bfloat16).astype(jnp.float32)
    lane = lax.broadcasted_iota(jnp.int32, (squares.shape[0], TAIL), 1)
    both = jnp.where(lane == 0, high, jnp.where(lane == 1, squares - high, 0.0))
    return both.astype(jnp.bfloat16)


def fetch_kernel(serving, _, gate, up, gate_held, up_held, sems):
    @pl.when(lax.axis_index("wide") >= serving)
    def _():
        here = pl.ds(0, gate_held.shape[1])
        copies = [
            pltpu.make_async_copy(gate.at[:, here], gate_held, sems.at[0]),
            pltpu.make_async_copy(up.at[:, here], up_held, sems.at[1]),
        ]
        for c in copies:
            c.start()
        for c in copies:
            c.wait()


def blank_kernel(*outs):
    for out in outs:
        out[...] = jnp.zeros_like(out)


def attend_kernel(*refs):
    sources, (attended, sent), held, sems = refs[:7], refs[7:9], refs[9:16], refs[16]
    lengths, q, kv, keys, values, residual, gain = held
    heads, hist, _ = keys.shape
    width = q.shape[1]
    group = width // (heads * HEAD_SIZE)
    copies = [
        pltpu.make_async_copy(source, place, sems.at[i])
        for i, (source, place) in enumerate(zip(sources, held))
    ]
    for c in copies:
        c.start()
    for c in copies:
        c.wait()
    length = lengths[0, 0]
    first = hist - STEPS
    for h in range(heads):
        lanes = slice(h * HEAD_SIZE, (h + 1) * HEAD_SIZE)
        for t in range(STEPS):
            keys[h, first + t : first + t + 1, :] = kv[t, 0:1, lanes]
            values[h, first + t : first + t + 1, :] = kv[t, 1:2, lanes]
    rows = heads * group * STEPS
    place = lax.broadcasted_iota(jnp.int32, (rows, hist), 1)
    step = lax.broadcasted_iota(jnp.int32, (rows, hist), 0) % STEPS
    seen = (place < length) | ((place >= first) & (place - first <= step))
    cols = [c * HEAD_SIZE for c in range(heads * group)]
    query = jnp.concatenate([q[:, c : c + HEAD_SIZE].astype(jnp.float32) for c in cols], 0)
    query = query.astype(jnp.bfloat16).reshape(heads, group * STEPS, HEAD_SIZE)
    scores = jnp.concatenate(
        [
            lax.dot_general(
                query[h], keys[h], (((1,), (1,)), ((), ())), preferred_element_type=jnp.float32
            )
            for h in range(heads)
        ],
        0,
    ) * (1.0 / HEAD_SIZE**0.5)
    scores = jnp.where(seen, scores, -1e30)
    top = jnp.max(scores, -1, keepdims=True)
    e = jnp.where(seen, jnp.exp(scores - top), 0.0)
    weights = (e / jnp.sum(e, -1, keepdims=True)).astype(jnp.bfloat16)
    weights = weights.reshape(heads, group * STEPS, hist)
    outs = [
        jnp.dot(weights[h], values[h], preferred_element_type=jnp.float32) for h in range(heads)
    ]
    squares = jnp.zeros((STEPS, HEAD_SIZE), jnp.float32)
    for i, c in enumerate(cols):
        here = slice(c, c + HEAD_SIZE)
        g = i % group * STEPS
        got = outs[i // group][g : g + STEPS].astype(jnp.bfloat16)
        attended[:, here] = got
        mixed = residual[:, here].astype(jnp.float32) + got.astype(jnp.float32)
        squares += mixed * mixed
        sent[:, here] = (mixed * gain[:, here]).astype(jnp.bfloat16)
    squares = jnp.sum(squares, -1, keepdims=True)
    sent[:, width:] = pair(squares)


def places(blocks, workers):
    middle = blocks // 2
    leaving = [b for b in range(blocks) if b != middle]
    found = []
    for b in range(blocks):
        for shift in range(workers):
            nth = leaving.index(b) * workers + shift if b != middle else None
            found.append(nth)
    return found


def forward_kernel(blocks, workers, narrow, *refs):
    count = blocks * workers
    arrived, (gate_held, up_held, gate, up), rest = refs[:blocks], refs[blocks:][:4], refs[blocks + 4 :]
    outs, (x, slots, sems) = rest[:-3], rest[-3:]
    me = lax.axis_index("wide") - count
    features, columns = gate.shape
    half = features // narrow
    early = gate_held.shape[1]
    room, _, _, tile = slots.shape
    units = list(range(early, columns, tile))

    def stream(j):
        s = j % room
        here = pl.ds(units[j], tile)
        size = features // 2 if j == len(units) - 1 else features
        depths = [pl.ds(at, size) for at in range(0, features, size)]
        return [
            pltpu.make_async_copy(m.at[k, here], slots.at[s, i, k], sems.at[s, i, part])
            for part, k in enumerate(depths)
            for i, m in enumerate((gate, up))
        ]

    @pl.when(me >= 0)
    def _():
        for j in range(min(room, len(units))):
            for copy in stream(j):
                copy.start()
        lines, tails = [], []
        for block in arrived:
            for shift in range(workers):
                owner = lax.rem(me + shift, workers)
                halves = [block[owner * narrow + n] for n in range(narrow)]
                lines.append(
                    jnp.concatenate([h[:, :half] for h in halves], 1).astype(jnp.float32)
                )
                tails.append(sum(h[:, half:].astype(jnp.float32) for h in halves))
        pad = x.shape[0] - STEPS * count
        if pad:
            lines.append(jnp.zeros((pad, features), jnp.float32))
            tails.append(jnp.zeros((pad, TAIL), jnp.float32))
        x[...] = jnp.concatenate(lines, 0).astype(jnp.bfloat16)
        squares = jnp.sum(jnp.concatenate(tails, 0), -1, keepdims=True)
        r = lax.rsqrt(squares / D + EPS)

        def multiply(depth, sums, tiles):
            for at in range(depth.start, depth.stop, CHUNK):
                k = slice(at, min(at + CHUNK, depth.stop))
                for i, some in enumerate(tiles):
                    more = jnp.dot(x[:, k], some(k), preferred_element_type=jnp.float32)
                    sums[i] = more if sums[i] is None else sums[i] + more
            return sums

        def produce(at, g, u):
            g, u = g * r, u * r
            hidden = (g / (1.0 + jnp.exp(-g)) * u).astype(jnp.bfloat16)
            for i, place in enumerate(places(blocks, workers)):
                rows = hidden[i * STEPS : (i + 1) * STEPS]
                if place is None:
                    outs[-1][i % workers, :, at : at + tile] = rows
                else:
                    outs[place][:, at : at + tile] = rows

        waiting = list(range(0, early, tile))

        def resident(some):
            for at in waiting[:some]:
                here = slice(at, at + tile)
                tiles = [lambda k, m=m: m[k, here] for m in (gate_held, up_held)]
                produce(at, *multiply(slice(0, features), [None] * 2, tiles))
            del waiting[:some]

        for j, at in enumerate(units):
            resident(AHEAD[j] if j < len(AHEAD) else 0)
            if j == len(units) - 1:
                resident(len(waiting))
            copies, sums = stream(j), [None] * 2
            tiles = [lambda k, i=i, s=j % room: slots[s, i, k, :] for i in range(2)]
            size = features * 2 // len(copies)
            for part in range(len(copies) // 2):
                for copy in copies[part * 2 : part * 2 + 2]:
                    copy.wait()
                multiply(slice(part * size, (part + 1) * size), sums, tiles)
            produce(at, *sums)
            if j + room < len(units):
                for copy in stream(j + room):
                    copy.start()
        if not units:
            resident(len(waiting))


def finish_kernel(blocks, workers, attended, gathered, *refs):
    results, (attended_out, out) = refs[:-2], refs[-2:]
    me = lax.axis_index("wide")
    block, place = me // workers, lax.rem(me, workers)
    columns = gathered.shape[3]
    attended_out[...] = attended[...]

    @pl.when(block >= blocks)
    def _():
        out[...] = jnp.zeros_like(out)

    @pl.when(block == blocks // 2)
    def _():
        for k in range(workers):
            shift = lax.rem(place + workers - k, workers)
            out[:, k * columns : (k + 1) * columns] = gathered[k, shift]

    if not results:
        return

    for i, nth in enumerate(places(blocks, workers)):
        if nth is not None:

            @pl.when(block == i // workers)
            def _(i=i, nth=nth):
                k = lax.rem(place + workers - i % workers, workers)
                out[:, pl.ds(pl.multiple_of(k * columns, 128), columns)] = results[nth][...]


def shards(queries, new_kv, keys, values, lengths, residual, gain, gate, up):
    wide = lax.axis_size("wide")
    narrow = lax.axis_size("narrow")
    serving = wide * 3 // 4
    workers = wide - serving
    blocks = serving // workers
    half = queries.shape[2]
    features, _, columns = gate.shape
    vmem = pl.BlockSpec(memory_space=pltpu.VMEM)
    hbm = pl.BlockSpec(memory_space=pltpu.HBM)
    owner = lax.axis_index("wide") < serving

    def in_hbm(a):
        return pltpu.with_memory_space_constraint(a, pltpu.HBM)

    gate = in_hbm(gate.reshape(features, columns))
    up = in_hbm(up.reshape(features, columns))
    operands = (
        lengths.reshape(1, 1),
        queries.reshape(STEPS, half),
        new_kv.reshape(STEPS, 2, -1),
        keys.reshape(keys.shape[1:]),
        values.reshape(values.shape[1:]),
        residual.reshape(STEPS, half),
        gain.reshape(1, half),
    )
    groups = [
        [w * narrow + n for w in range(at, at + workers) for n in range(narrow)]
        for at in range(0, wide, workers)
    ]
    shapes = (
        jax.ShapeDtypeStruct((STEPS, half), jnp.bfloat16),
        jax.ShapeDtypeStruct((workers * narrow, STEPS, half + TAIL), jnp.bfloat16),
    )

    def serve(*operands):
        attended, sent = pl.pallas_call(
            attend_kernel,
            out_shape=(
                pltpu.VMEM(shapes[0].shape, jnp.bfloat16),
                jax.ShapeDtypeStruct(shapes[1].shape[1:], jnp.bfloat16),
            ),
            in_specs=[hbm] * 7,
            out_specs=(vmem, vmem),
            scratch_shapes=[
                (pltpu.SMEM if o.dtype == jnp.int32 else pltpu.VMEM)(o.shape, o.dtype)
                for o in operands
            ]
            + [pltpu.SemaphoreType.DMA((7,))],
            compiler_params=pltpu.CompilerParams(vmem_limit_bytes=8 << 20),
        )(operands[0], *map(in_hbm, operands[1:]))
        gathered = lax.all_gather(sent, ("wide", "narrow"), axis=0, axis_index_groups=groups)
        return attended, gathered

    def rest(*operands):
        return pl.pallas_call(
            blank_kernel,
            out_shape=(pltpu.VMEM(shapes[0].shape, jnp.bfloat16), shapes[1]),
            out_specs=(vmem, vmem),
            compiler_params=pltpu.CompilerParams(vmem_limit_bytes=8 << 20),
        )()

    attended, block = lax.cond(owner, serve, rest, *operands)
    arrived = [
        lax.ppermute(block, "wide", [(b * workers + j, serving + j) for j in range(workers)])
        for b in range(blocks)
    ]
    tile = TILE if columns % (2 * TILE) == 0 else columns
    early = columns // 2 // tile * tile or columns
    held = pl.pallas_call(
        functools.partial(fetch_kernel, serving),
        out_shape=[pltpu.VMEM((features, early), jnp.bfloat16)] * 2,
        in_specs=[pl.BlockSpec(memory_space=pl.ANY), hbm, hbm],
        out_specs=[vmem] * 2,
        scratch_shapes=[pltpu.SemaphoreType.DMA((2,))],
        compiler_params=pltpu.CompilerParams(vmem_limit_bytes=4 << 20),
        cost_estimate=pl.CostEstimate(
            flops=0, bytes_accessed=early * 4 * features, transcendentals=0
        ),
    )(block, gate, up)
    padded = -(-STEPS * serving // 16) * 16
    together = jax.ShapeDtypeStruct((workers, STEPS, columns), jnp.bfloat16)
    *hidden, shared = pl.pallas_call(
        functools.partial(forward_kernel, blocks, workers, narrow),
        out_shape=[jax.ShapeDtypeStruct((STEPS, columns), jnp.bfloat16)] * (serving - workers)
        + [together],
        in_specs=[vmem] * (blocks + 2) + [hbm, hbm],
        out_specs=[vmem] * (serving - workers + 1),
        scratch_shapes=[
            pltpu.VMEM((padded, features), jnp.bfloat16),
            pltpu.VMEM((SLOTS, 2, features, tile), jnp.bfloat16),
            pltpu.SemaphoreType.DMA((SLOTS, 2, 2)),
        ],
        compiler_params=pltpu.CompilerParams(vmem_limit_bytes=19 << 20),
    )(*arrived, *held, gate, up)
    middle = blocks // 2
    shared = lax.ppermute(
        shared, "wide", [(serving + k, middle * workers + k) for k in range(workers)]
    )
    peers = [list(range(at, at + workers)) for at in range(0, wide, workers)]

    def skip(shared):
        return pl.pallas_call(
            blank_kernel,
            out_shape=jax.ShapeDtypeStruct((workers, *shared.shape), jnp.bfloat16),
            out_specs=vmem,
            compiler_params=pltpu.CompilerParams(vmem_limit_bytes=8 << 20),
        )()

    gathered = lax.cond(
        lax.axis_index("wide") // workers == middle,
        lambda shared: lax.all_gather(shared, "wide", axis=0, axis_index_groups=peers),
        skip,
        shared,
    )
    results = list(hidden)
    for i, nth in enumerate(places(blocks, workers)):
        if nth is not None:
            b, s = divmod(i, workers)
            pairs = [(serving + k, b * workers + (k + s) % workers) for k in range(workers)]
            results[nth] = lax.ppermute(hidden[nth], "wide", pairs)
    aligned = columns % 128 == 0
    attended, activated = pl.pallas_call(
        functools.partial(finish_kernel, blocks, workers),
        out_shape=(
            jax.ShapeDtypeStruct((STEPS, half), jnp.bfloat16),
            jax.ShapeDtypeStruct((STEPS, workers * columns), jnp.bfloat16),
        ),
        in_specs=[vmem] * (2 + (len(results) if aligned else 0)),
        out_specs=(vmem, vmem),
        compiler_params=pltpu.CompilerParams(vmem_limit_bytes=8 << 20),
    )(attended, gathered, *(results if aligned else []))
    if not aligned:
        me = lax.axis_index("wide")
        pieces = []
        for k in range(workers):
            piece = activated[:, k * columns : (k + 1) * columns]
            for i, nth in enumerate(places(blocks, workers)):
                if nth is not None:
                    mine = me == i // workers * workers + (k + i) % workers
                    piece = jnp.where(mine, results[nth], piece)
            pieces.append(piece)
        activated = jnp.concatenate(pieces, 1)
    return attended.reshape(STEPS, 1, half), activated.reshape(STEPS, 1, -1)


def solution(mesh):
    rows = P(None, ("parts", "wide"), "narrow")
    placed = (
        rows,
        P(None, ("parts", "wide"), None, "narrow"),
        P(("parts", "wide"), "narrow", None, None),
        P(("parts", "wide"), "narrow", None, None),
        P(("parts", "wide")),
        rows,
        P("narrow"),
        P(None, "narrow", "wide"),
        P(None, "narrow", "wide"),
    )
    return jax.shard_map(
        shards, mesh=mesh, in_specs=placed, out_specs=(rows, rows), check_vma=False
    )
```

```python
import functools

import jax
import jax.numpy as jnp
from jax import lax
from jax.experimental import pallas as pl
from jax.experimental.pallas import tpu as pltpu
from jax.sharding import PartitionSpec as P

D = 4096
HEAD_SIZE = 128
STEPS = 2
TAIL = 128
EPS = 1e-05
TILE = 256
SLOTS = 4
AHEAD = (3, 1, 1, 1, 1)
CHUNK = 1024


def pair(squares):
    high = squares.astype(jnp.bfloat16).astype(jnp.float32)
    lane = lax.broadcasted_iota(jnp.int32, (squares.shape[0], TAIL), 1)
    both = jnp.where(lane == 0, high, jnp.where(lane == 1, squares - high, 0.0))
    return both.astype(jnp.bfloat16)


def fetch_kernel(serving, _, gate, up, gate_held, up_held, sems):
    @pl.when(lax.axis_index("wide") >= serving)
    def _():
        here = pl.ds(0, gate_held.shape[1])
        copies = [
            pltpu.make_async_copy(gate.at[:, here], gate_held, sems.at[0]),
            pltpu.make_async_copy(up.at[:, here], up_held, sems.at[1]),
        ]
        for c in copies:
            c.start()
        for c in copies:
            c.wait()


def blank_kernel(*outs):
    for out in outs:
        out[...] = jnp.zeros_like(out)


def attend_kernel(*refs):
    sources, (attended, sent), held, sems = refs[:7], refs[7:9], refs[9:16], refs[16]
    lengths, q, kv, keys, values, residual, gain = held
    heads, hist, _ = keys.shape
    width = q.shape[1]
    group = width // (heads * HEAD_SIZE)
    copies = [
        pltpu.make_async_copy(source, place, sems.at[i])
        for i, (source, place) in enumerate(zip(sources, held))
    ]
    for c in copies:
        c.start()
    for c in copies:
        c.wait()
    length = lengths[0, 0]
    first = hist - STEPS
    for h in range(heads):
        lanes = slice(h * HEAD_SIZE, (h + 1) * HEAD_SIZE)
        for t in range(STEPS):
            keys[h, first + t : first + t + 1, :] = kv[t, 0:1, lanes]
            values[h, first + t : first + t + 1, :] = kv[t, 1:2, lanes]
    rows = heads * group * STEPS
    place = lax.broadcasted_iota(jnp.int32, (rows, hist), 1)
    step = lax.broadcasted_iota(jnp.int32, (rows, hist), 0) % STEPS
    seen = (place < length) | ((place >= first) & (place - first <= step))
    cols = [c * HEAD_SIZE for c in range(heads * group)]
    query = jnp.concatenate([q[:, c : c + HEAD_SIZE].astype(jnp.float32) for c in cols], 0)
    query = query.astype(jnp.bfloat16).reshape(heads, group * STEPS, HEAD_SIZE)
    scores = jnp.concatenate(
        [
            lax.dot_general(
                query[h], keys[h], (((1,), (1,)), ((), ())), preferred_element_type=jnp.float32
            )
            for h in range(heads)
        ],
        0,
    ) * (1.0 / HEAD_SIZE**0.5)
    scores = jnp.where(seen, scores, -1e30)
    top = jnp.max(scores, -1, keepdims=True)
    e = jnp.where(seen, jnp.exp(scores - top), 0.0)
    weights = (e / jnp.sum(e, -1, keepdims=True)).astype(jnp.bfloat16)
    weights = weights.reshape(heads, group * STEPS, hist)
    outs = [
        jnp.dot(weights[h], values[h], preferred_element_type=jnp.float32) for h in range(heads)
    ]
    squares = jnp.zeros((STEPS, HEAD_SIZE), jnp.float32)
    for i, c in enumerate(cols):
        here = slice(c, c + HEAD_SIZE)
        g = i % group * STEPS
        got = outs[i // group][g : g + STEPS].astype(jnp.bfloat16)
        attended[:, here] = got
        mixed = residual[:, here].astype(jnp.float32) + got.astype(jnp.float32)
        squares += mixed * mixed
        sent[:, here] = (mixed * gain[:, here]).astype(jnp.bfloat16)
    squares = jnp.sum(squares, -1, keepdims=True)
    sent[:, width:] = pair(squares)


def places(blocks, workers):
    middle = blocks // 2
    leaving = [b for b in range(blocks) if b != middle]
    found = []
    for b in range(blocks):
        for shift in range(workers):
            nth = leaving.index(b) * workers + shift if b != middle else None
            found.append(nth)
    return found


PAIRED = (
    ((1, 0), (0, 0)),
    ((1, 1), (1, 0)),
    ((0, 0), (1, 1)),
    ((0, 1), (2, 1)),
    ((2, 0), (0, 1)),
    ((2, 1), (2, 0)),
)


def forward_kernel(blocks, workers, narrow, *refs):
    count = blocks * workers
    arrived, (gate_held, up_held, gate, up), rest = refs[:blocks], refs[blocks:][:4], refs[blocks + 4 :]
    outs, (x, slots, sems) = rest[:-3], rest[-3:]
    me = lax.axis_index("wide") - count
    paired = (blocks, workers) == (3, 2)
    features, columns = gate.shape
    half = features // narrow
    early = gate_held.shape[1]
    room, _, _, tile = slots.shape
    units = list(range(early, columns, tile))

    def stream(j):
        s = j % room
        here = pl.ds(units[j], tile)
        size = features // 2 if j == len(units) - 1 else features
        depths = [pl.ds(at, size) for at in range(0, features, size)]
        return [
            pltpu.make_async_copy(m.at[k, here], slots.at[s, i, k], sems.at[s, i, part])
            for part, k in enumerate(depths)
            for i, m in enumerate((gate, up))
        ]

    @pl.when(me >= 0)
    def _():
        for j in range(min(room, len(units))):
            for copy in stream(j):
                copy.start()
        lines, tails = [], []
        for i in range(count):
            b, shift = divmod(i, workers)
            parts = [arrived[b][lax.rem(me + shift, workers) * narrow + n] for n in range(narrow)]
            parts = [p.astype(jnp.float32) for p in parts]
            if paired:
                parts = []
                for n in range(narrow):
                    first, second = [
                        arrived[b][o * narrow + n].astype(jnp.float32) for b, o in PAIRED[i]
                    ]
                    parts.append(jnp.where(me == 0, first, second))
            lines.append(jnp.concatenate([p[:, :half] for p in parts], 1))
            tails.append(sum(p[:, half:] for p in parts))
        pad = x.shape[0] - STEPS * count
        if pad:
            lines.append(jnp.zeros((pad, features), jnp.float32))
            tails.append(jnp.zeros((pad, TAIL), jnp.float32))
        x[...] = jnp.concatenate(lines, 0).astype(jnp.bfloat16)
        squares = jnp.sum(jnp.concatenate(tails, 0), -1, keepdims=True)
        r = lax.rsqrt(squares / D + EPS)

        def multiply(depth, sums, tiles):
            for at in range(depth.start, depth.stop, CHUNK):
                k = slice(at, min(at + CHUNK, depth.stop))
                for i, some in enumerate(tiles):
                    more = jnp.dot(x[:, k], some(k), preferred_element_type=jnp.float32)
                    sums[i] = more if sums[i] is None else sums[i] + more
            return sums

        def produce(at, g, u):
            g, u = g * r, u * r
            hidden = (g / (1.0 + jnp.exp(-g)) * u).astype(jnp.bfloat16)
            here = slice(at, at + tile)
            if paired:
                rows = [hidden[i * STEPS : (i + 1) * STEPS] for i in range(count)]
                outs[0][0, :, here], outs[0][1, :, here] = rows[0], rows[1]
                outs[1][0, :, here], outs[1][1, :, here] = rows[2], rows[1]
                for out, some in zip(outs[2:], rows[3:]):
                    out[:, here] = some
                return
            for i, place in enumerate(places(blocks, workers)):
                rows = hidden[i * STEPS : (i + 1) * STEPS]
                if place is None:
                    outs[-1][i % workers, :, at : at + tile] = rows
                else:
                    outs[place][:, at : at + tile] = rows

        waiting = list(range(0, early, tile))

        def resident(some):
            for at in waiting[:some]:
                here = slice(at, at + tile)
                tiles = [lambda k, m=m: m[k, here] for m in (gate_held, up_held)]
                produce(at, *multiply(slice(0, features), [None] * 2, tiles))
            del waiting[:some]

        for j, at in enumerate(units):
            resident(AHEAD[j] if j < len(AHEAD) else 0)
            if j == len(units) - 1:
                resident(len(waiting))
            copies, sums = stream(j), [None] * 2
            tiles = [lambda k, i=i, s=j % room: slots[s, i, k, :] for i in range(2)]
            size = features * 2 // len(copies)
            for part in range(len(copies) // 2):
                for copy in copies[part * 2 : part * 2 + 2]:
                    copy.wait()
                multiply(slice(part * size, (part + 1) * size), sums, tiles)
            produce(at, *sums)
            if j + room < len(units):
                for copy in stream(j + room):
                    copy.start()
        if not units:
            resident(len(waiting))


def other_kernel(first, second, out):
    @pl.when(lax.rem(lax.axis_index("wide"), 2) == 0)
    def _():
        out[...] = first[1]

    @pl.when(lax.rem(lax.axis_index("wide"), 2) == 1)
    def _():
        out[...] = second[1]


def finish_paired_kernel(attended, swapped, first, second, third, fourth, fifth, attended_out, out):
    me = lax.axis_index("wide")
    columns = swapped.shape[1]
    attended_out[...] = attended[...]
    found = (
        (second.at[0], first.at[0]),
        (third, fourth),
        (first.at[0], swapped),
        (swapped, second.at[0]),
        (fourth, fifth),
        (fifth, third),
    )

    @pl.when(me >= len(found))
    def _():
        out[...] = jnp.zeros_like(out)

    for i, halves in enumerate(found):

        @pl.when(me == i)
        def _(halves=halves):
            for k, some in enumerate(halves):
                out[:, k * columns : (k + 1) * columns] = some[...]


def finish_kernel(blocks, workers, attended, gathered, *refs):
    results, (attended_out, out) = refs[:-2], refs[-2:]
    me = lax.axis_index("wide")
    block, place = me // workers, lax.rem(me, workers)
    columns = gathered.shape[3]
    attended_out[...] = attended[...]

    @pl.when(block >= blocks)
    def _():
        out[...] = jnp.zeros_like(out)

    @pl.when(block == blocks // 2)
    def _():
        for k in range(workers):
            shift = lax.rem(place + workers - k, workers)
            out[:, k * columns : (k + 1) * columns] = gathered[k, shift]

    if not results:
        return

    for i, nth in enumerate(places(blocks, workers)):
        if nth is not None:

            @pl.when(block == i // workers)
            def _(i=i, nth=nth):
                k = lax.rem(place + workers - i % workers, workers)
                out[:, pl.ds(pl.multiple_of(k * columns, 128), columns)] = results[nth][...]


def shards(queries, new_kv, keys, values, lengths, residual, gain, gate, up):
    wide = lax.axis_size("wide")
    narrow = lax.axis_size("narrow")
    serving = wide * 3 // 4
    workers = wide - serving
    blocks = serving // workers
    half = queries.shape[2]
    features, _, columns = gate.shape
    vmem = pl.BlockSpec(memory_space=pltpu.VMEM)
    hbm = pl.BlockSpec(memory_space=pltpu.HBM)
    owner = lax.axis_index("wide") < serving

    def in_hbm(a):
        return pltpu.with_memory_space_constraint(a, pltpu.HBM)

    gate = in_hbm(gate.reshape(features, columns))
    up = in_hbm(up.reshape(features, columns))
    operands = (
        lengths.reshape(1, 1),
        queries.reshape(STEPS, half),
        new_kv.reshape(STEPS, 2, -1),
        keys.reshape(keys.shape[1:]),
        values.reshape(values.shape[1:]),
        residual.reshape(STEPS, half),
        gain.reshape(1, half),
    )
    groups = [
        [w * narrow + n for w in range(at, at + workers) for n in range(narrow)]
        for at in range(0, wide, workers)
    ]
    shapes = (
        jax.ShapeDtypeStruct((STEPS, half), jnp.bfloat16),
        jax.ShapeDtypeStruct((workers * narrow, STEPS, half + TAIL), jnp.bfloat16),
    )

    def serve(*operands):
        attended, sent = pl.pallas_call(
            attend_kernel,
            out_shape=(
                pltpu.VMEM(shapes[0].shape, jnp.bfloat16),
                jax.ShapeDtypeStruct(shapes[1].shape[1:], jnp.bfloat16),
            ),
            in_specs=[hbm] * 7,
            out_specs=(vmem, vmem),
            scratch_shapes=[
                (pltpu.SMEM if o.dtype == jnp.int32 else pltpu.VMEM)(o.shape, o.dtype)
                for o in operands
            ]
            + [pltpu.SemaphoreType.DMA((7,))],
            compiler_params=pltpu.CompilerParams(vmem_limit_bytes=8 << 20),
        )(operands[0], *map(in_hbm, operands[1:]))
        gathered = lax.all_gather(sent, ("wide", "narrow"), axis=0, axis_index_groups=groups)
        return attended, gathered

    def rest(*operands):
        return pl.pallas_call(
            blank_kernel,
            out_shape=(pltpu.VMEM(shapes[0].shape, jnp.bfloat16), shapes[1]),
            out_specs=(vmem, vmem),
            compiler_params=pltpu.CompilerParams(vmem_limit_bytes=8 << 20),
        )()

    attended, block = lax.cond(owner, serve, rest, *operands)
    arrived = [
        lax.ppermute(block, "wide", [(b * workers + j, serving + j) for j in range(workers)])
        for b in range(blocks)
    ]
    tile = TILE if columns % (2 * TILE) == 0 else columns
    early = columns // 2 // tile * tile or columns
    held = pl.pallas_call(
        functools.partial(fetch_kernel, serving),
        out_shape=[pltpu.VMEM((features, early), jnp.bfloat16)] * 2,
        in_specs=[pl.BlockSpec(memory_space=pl.ANY), hbm, hbm],
        out_specs=[vmem] * 2,
        scratch_shapes=[pltpu.SemaphoreType.DMA((2,))],
        compiler_params=pltpu.CompilerParams(vmem_limit_bytes=4 << 20),
        cost_estimate=pl.CostEstimate(
            flops=0, bytes_accessed=early * 4 * features, transcendentals=0
        ),
    )(block, gate, up)
    padded = -(-STEPS * serving // 16) * 16
    together = jax.ShapeDtypeStruct((workers, STEPS, columns), jnp.bfloat16)
    paired = (blocks, workers) == (3, 2)
    single = jax.ShapeDtypeStruct((STEPS, columns), jnp.bfloat16)
    messages = [single] * (serving - workers) + [together]
    if paired:
        messages = [together] * 2 + [single] * 3
    *hidden, shared = pl.pallas_call(
        functools.partial(forward_kernel, blocks, workers, narrow),
        out_shape=messages,
        in_specs=[vmem] * (blocks + 2) + [hbm, hbm],
        out_specs=[vmem] * len(messages),
        scratch_shapes=[
            pltpu.VMEM((padded, features), jnp.bfloat16),
            pltpu.VMEM((SLOTS, 2, features, tile), jnp.bfloat16),
            pltpu.SemaphoreType.DMA((SLOTS, 2, 2)),
        ],
        compiler_params=pltpu.CompilerParams(vmem_limit_bytes=19 << 20),
    )(*arrived, *held, gate, up)
    ends = (
        jax.ShapeDtypeStruct((STEPS, half), jnp.bfloat16),
        jax.ShapeDtypeStruct((STEPS, workers * columns), jnp.bfloat16),
    )
    if paired:
        got = []
        for message, place in zip([*hidden, shared], (0, 2, 3, 4, 5)):
            targets = [b * workers + o for b, o in PAIRED[place]]
            got.append(lax.ppermute(message, "wide", [(serving + k, t) for k, t in enumerate(targets)]))

        def exchange(first, second):
            other = pl.pallas_call(
                other_kernel,
                out_shape=single,
                in_specs=[vmem] * 2,
                out_specs=vmem,
                compiler_params=pltpu.CompilerParams(vmem_limit_bytes=8 << 20),
            )(first, second)
            return lax.ppermute(other, "wide", [(w, w ^ 1) for w in range(wide)])

        def none(first, second):
            return pl.pallas_call(
                blank_kernel,
                out_shape=single,
                out_specs=vmem,
                compiler_params=pltpu.CompilerParams(vmem_limit_bytes=8 << 20),
            )()

        middle = lax.axis_index("wide") // workers == 1
        swapped = lax.cond(middle, exchange, none, got[0], got[1])
        attended, activated = pl.pallas_call(
            finish_paired_kernel,
            out_shape=ends,
            in_specs=[vmem] * 7,
            out_specs=(vmem, vmem),
            compiler_params=pltpu.CompilerParams(vmem_limit_bytes=8 << 20),
        )(attended, swapped, *got)
        return attended.reshape(STEPS, 1, half), activated.reshape(STEPS, 1, -1)
    middle = blocks // 2
    shared = lax.ppermute(
        shared, "wide", [(serving + k, middle * workers + k) for k in range(workers)]
    )
    peers = [list(range(at, at + workers)) for at in range(0, wide, workers)]

    def skip(shared):
        return pl.pallas_call(
            blank_kernel,
            out_shape=jax.ShapeDtypeStruct((workers, *shared.shape), jnp.bfloat16),
            out_specs=vmem,
            compiler_params=pltpu.CompilerParams(vmem_limit_bytes=8 << 20),
        )()

    gathered = lax.cond(
        lax.axis_index("wide") // workers == middle,
        lambda shared: lax.all_gather(shared, "wide", axis=0, axis_index_groups=peers),
        skip,
        shared,
    )
    results = list(hidden)
    for i, nth in enumerate(places(blocks, workers)):
        if nth is not None:
            b, s = divmod(i, workers)
            pairs = [(serving + k, b * workers + (k + s) % workers) for k in range(workers)]
            results[nth] = lax.ppermute(hidden[nth], "wide", pairs)
    aligned = columns % 128 == 0
    attended, activated = pl.pallas_call(
        functools.partial(finish_kernel, blocks, workers),
        out_shape=(
            jax.ShapeDtypeStruct((STEPS, half), jnp.bfloat16),
            jax.ShapeDtypeStruct((STEPS, workers * columns), jnp.bfloat16),
        ),
        in_specs=[vmem] * (2 + (len(results) if aligned else 0)),
        out_specs=(vmem, vmem),
        compiler_params=pltpu.CompilerParams(vmem_limit_bytes=8 << 20),
    )(attended, gathered, *(results if aligned else []))
    if not aligned:
        me = lax.axis_index("wide")
        pieces = []
        for k in range(workers):
            piece = activated[:, k * columns : (k + 1) * columns]
            for i, nth in enumerate(places(blocks, workers)):
                if nth is not None:
                    mine = me == i // workers * workers + (k + i) % workers
                    piece = jnp.where(mine, results[nth], piece)
            pieces.append(piece)
        activated = jnp.concatenate(pieces, 1)
    return attended.reshape(STEPS, 1, half), activated.reshape(STEPS, 1, -1)


def solution(mesh):
    rows = P(None, ("parts", "wide"), "narrow")
    placed = (
        rows,
        P(None, ("parts", "wide"), None, "narrow"),
        P(("parts", "wide"), "narrow", None, None),
        P(("parts", "wide"), "narrow", None, None),
        P(("parts", "wide")),
        rows,
        P("narrow"),
        P(None, "narrow", "wide"),
        P(None, "narrow", "wide"),
    )
    return jax.shard_map(
        shards, mesh=mesh, in_specs=placed, out_specs=(rows, rows), check_vma=False
    )
```

```python
import functools

import jax
import jax.numpy as jnp
from jax import lax
from jax.experimental import pallas as pl
from jax.experimental.pallas import tpu as pltpu
from jax.sharding import PartitionSpec as P

D = 4096
HEAD_SIZE = 128
STEPS = 2
TAIL = 128
EPS = 1e-05
TILE = 256
SLOTS = 4
AHEAD = (3, 1, 1, 1, 1)
CHUNK = 1024


def pair(squares):
    high = squares.astype(jnp.bfloat16).astype(jnp.float32)
    lane = lax.broadcasted_iota(jnp.int32, (squares.shape[0], TAIL), 1)
    both = jnp.where(lane == 0, high, jnp.where(lane == 1, squares - high, 0.0))
    return both.astype(jnp.bfloat16)


def fetch_kernel(serving, _, gate, up, gate_held, up_held, sems):
    @pl.when(lax.axis_index("wide") >= serving)
    def _():
        here = pl.ds(0, gate_held.shape[1])
        copies = [
            pltpu.make_async_copy(gate.at[:, here], gate_held, sems.at[0]),
            pltpu.make_async_copy(up.at[:, here], up_held, sems.at[1]),
        ]
        for c in copies:
            c.start()
        for c in copies:
            c.wait()


def blank_kernel(*outs):
    for out in outs:
        out[...] = jnp.zeros_like(out)


def attend_kernel(*refs):
    sources, (attended, sent), held, sems = refs[:7], refs[7:9], refs[9:16], refs[16]
    lengths, q, kv, keys, values, residual, gain = held
    heads, hist, _ = keys.shape
    width = q.shape[1]
    group = width // (heads * HEAD_SIZE)
    copies = [
        pltpu.make_async_copy(source, place, sems.at[i])
        for i, (source, place) in enumerate(zip(sources, held))
    ]
    for c in copies:
        c.start()
    for c in copies:
        c.wait()
    length = lengths[0, 0]
    first = hist - STEPS
    for h in range(heads):
        lanes = slice(h * HEAD_SIZE, (h + 1) * HEAD_SIZE)
        for t in range(STEPS):
            keys[h, first + t : first + t + 1, :] = kv[t, 0:1, lanes]
            values[h, first + t : first + t + 1, :] = kv[t, 1:2, lanes]
    rows = heads * group * STEPS
    place = lax.broadcasted_iota(jnp.int32, (rows, hist), 1)
    step = lax.broadcasted_iota(jnp.int32, (rows, hist), 0) % STEPS
    seen = (place < length) | ((place >= first) & (place - first <= step))
    cols = [c * HEAD_SIZE for c in range(heads * group)]
    query = jnp.concatenate([q[:, c : c + HEAD_SIZE].astype(jnp.float32) for c in cols], 0)
    query = query.astype(jnp.bfloat16).reshape(heads, group * STEPS, HEAD_SIZE)
    scores = jnp.concatenate(
        [
            lax.dot_general(
                query[h], keys[h], (((1,), (1,)), ((), ())), preferred_element_type=jnp.float32
            )
            for h in range(heads)
        ],
        0,
    ) * (1.0 / HEAD_SIZE**0.5)
    scores = jnp.where(seen, scores, -1e30)
    top = jnp.max(scores, -1, keepdims=True)
    e = jnp.where(seen, jnp.exp(scores - top), 0.0)
    weights = (e / jnp.sum(e, -1, keepdims=True)).astype(jnp.bfloat16)
    weights = weights.reshape(heads, group * STEPS, hist)
    outs = [
        jnp.dot(weights[h], values[h], preferred_element_type=jnp.float32) for h in range(heads)
    ]
    squares = jnp.zeros((STEPS, HEAD_SIZE), jnp.float32)
    for i, c in enumerate(cols):
        here = slice(c, c + HEAD_SIZE)
        g = i % group * STEPS
        got = outs[i // group][g : g + STEPS].astype(jnp.bfloat16)
        attended[:, here] = got
        mixed = residual[:, here].astype(jnp.float32) + got.astype(jnp.float32)
        squares += mixed * mixed
        sent[:, here] = (mixed * gain[:, here]).astype(jnp.bfloat16)
    squares = jnp.sum(squares, -1, keepdims=True)
    sent[:, width:] = pair(squares)


def places(blocks, workers):
    middle = blocks // 2
    leaving = [b for b in range(blocks) if b != middle]
    found = []
    for b in range(blocks):
        for shift in range(workers):
            nth = leaving.index(b) * workers + shift if b != middle else None
            found.append(nth)
    return found


def forward_kernel(blocks, workers, narrow, *refs):
    count = blocks * workers
    arrived, (gate_held, up_held, gate, up), rest = refs[:blocks], refs[blocks:][:4], refs[blocks + 4 :]
    outs, (x, slots, sems) = rest[:-3], rest[-3:]
    me = lax.axis_index("wide") - count
    features, columns = gate.shape
    half = features // narrow
    early = gate_held.shape[1]
    room, _, _, tile = slots.shape
    units = list(range(early, columns, tile))

    def stream(j):
        s = j % room
        here = pl.ds(units[j], tile)
        size = features // 2 if j == len(units) - 1 else features
        depths = [pl.ds(at, size) for at in range(0, features, size)]
        return [
            pltpu.make_async_copy(m.at[k, here], slots.at[s, i, k], sems.at[s, i, part])
            for part, k in enumerate(depths)
            for i, m in enumerate((gate, up))
        ]

    @pl.when(me >= 0)
    def _():
        for j in range(min(room, len(units))):
            for copy in stream(j):
                copy.start()
        lines, tails = [], []
        for block in arrived:
            for shift in range(workers):
                owner = lax.rem(me + shift, workers)
                halves = [block[owner * narrow + n] for n in range(narrow)]
                lines.append(
                    jnp.concatenate([h[:, :half] for h in halves], 1)
                )
                tails.append(sum(h[:, half:].astype(jnp.float32) for h in halves))
        pad = x.shape[0] - STEPS * count
        if pad:
            lines.append(jnp.zeros((pad, features), jnp.bfloat16))
            tails.append(jnp.zeros((pad, TAIL), jnp.float32))
        x[...] = jnp.concatenate(lines, 0)
        squares = jnp.sum(jnp.concatenate(tails, 0), -1, keepdims=True)
        r = lax.rsqrt(squares / D + EPS)

        def multiply(depth, sums, tiles):
            for at in range(depth.start, depth.stop, CHUNK):
                k = slice(at, min(at + CHUNK, depth.stop))
                for i, some in enumerate(tiles):
                    more = jnp.dot(x[:, k], some(k), preferred_element_type=jnp.float32)
                    sums[i] = more if sums[i] is None else sums[i] + more
            return sums

        def produce(at, g, u):
            g, u = g * r, u * r
            hidden = (g / (1.0 + jnp.exp(-g)) * u).astype(jnp.bfloat16)
            for i, place in enumerate(places(blocks, workers)):
                rows = hidden[i * STEPS : (i + 1) * STEPS]
                if place is None:
                    outs[-1][i % workers, :, at : at + tile] = rows
                else:
                    outs[place][:, at : at + tile] = rows

        waiting = list(range(0, early, tile))

        def resident(some):
            for at in waiting[:some]:
                here = slice(at, at + tile)
                tiles = [lambda k, m=m: m[k, here] for m in (gate_held, up_held)]
                produce(at, *multiply(slice(0, features), [None] * 2, tiles))
            del waiting[:some]

        for j, at in enumerate(units):
            resident(AHEAD[j] if j < len(AHEAD) else 0)
            if j == len(units) - 1:
                resident(len(waiting))
            copies, sums = stream(j), [None] * 2
            tiles = [lambda k, i=i, s=j % room: slots[s, i, k, :] for i in range(2)]
            size = features * 2 // len(copies)
            for part in range(len(copies) // 2):
                for copy in copies[part * 2 : part * 2 + 2]:
                    copy.wait()
                multiply(slice(part * size, (part + 1) * size), sums, tiles)
            produce(at, *sums)
            if j + room < len(units):
                for copy in stream(j + room):
                    copy.start()
        if not units:
            resident(len(waiting))


def finish_kernel(blocks, workers, attended, gathered, *refs):
    results, (attended_out, out) = refs[:-2], refs[-2:]
    me = lax.axis_index("wide")
    block, place = me // workers, lax.rem(me, workers)
    columns = gathered.shape[3]
    attended_out[...] = attended[...]

    @pl.when(block >= blocks)
    def _():
        out[...] = jnp.zeros_like(out)

    @pl.when(block == blocks // 2)
    def _():
        for k in range(workers):
            shift = lax.rem(place + workers - k, workers)
            out[:, k * columns : (k + 1) * columns] = gathered[k, shift]

    if not results:
        return

    for i, nth in enumerate(places(blocks, workers)):
        if nth is not None:

            @pl.when(block == i // workers)
            def _(i=i, nth=nth):
                k = lax.rem(place + workers - i % workers, workers)
                out[:, pl.ds(pl.multiple_of(k * columns, 128), columns)] = results[nth][...]


def shards(queries, new_kv, keys, values, lengths, residual, gain, gate, up):
    wide = lax.axis_size("wide")
    narrow = lax.axis_size("narrow")
    serving = wide * 3 // 4
    workers = wide - serving
    blocks = serving // workers
    half = queries.shape[2]
    features, _, columns = gate.shape
    vmem = pl.BlockSpec(memory_space=pltpu.VMEM)
    hbm = pl.BlockSpec(memory_space=pltpu.HBM)
    owner = lax.axis_index("wide") < serving

    def in_hbm(a):
        return pltpu.with_memory_space_constraint(a, pltpu.HBM)

    gate = in_hbm(gate.reshape(features, columns))
    up = in_hbm(up.reshape(features, columns))
    operands = (
        lengths.reshape(1, 1),
        queries.reshape(STEPS, half),
        new_kv.reshape(STEPS, 2, -1),
        keys.reshape(keys.shape[1:]),
        values.reshape(values.shape[1:]),
        residual.reshape(STEPS, half),
        gain.reshape(1, half),
    )
    groups = [
        [w * narrow + n for w in range(at, at + workers) for n in range(narrow)]
        for at in range(0, wide, workers)
    ]
    shapes = (
        jax.ShapeDtypeStruct((STEPS, half), jnp.bfloat16),
        jax.ShapeDtypeStruct((workers * narrow, STEPS, half + TAIL), jnp.bfloat16),
    )

    def serve(*operands):
        attended, sent = pl.pallas_call(
            attend_kernel,
            out_shape=(
                pltpu.VMEM(shapes[0].shape, jnp.bfloat16),
                jax.ShapeDtypeStruct(shapes[1].shape[1:], jnp.bfloat16),
            ),
            in_specs=[hbm] * 7,
            out_specs=(vmem, vmem),
            scratch_shapes=[
                (pltpu.SMEM if o.dtype == jnp.int32 else pltpu.VMEM)(o.shape, o.dtype)
                for o in operands
            ]
            + [pltpu.SemaphoreType.DMA((7,))],
            compiler_params=pltpu.CompilerParams(vmem_limit_bytes=8 << 20),
        )(operands[0], *map(in_hbm, operands[1:]))
        gathered = lax.all_gather(sent, ("wide", "narrow"), axis=0, axis_index_groups=groups)
        return attended, gathered

    def rest(*operands):
        return pl.pallas_call(
            blank_kernel,
            out_shape=(pltpu.VMEM(shapes[0].shape, jnp.bfloat16), shapes[1]),
            out_specs=(vmem, vmem),
            compiler_params=pltpu.CompilerParams(vmem_limit_bytes=8 << 20),
        )()

    attended, block = lax.cond(owner, serve, rest, *operands)
    arrived = [
        lax.ppermute(block, "wide", [(b * workers + j, serving + j) for j in range(workers)])
        for b in range(blocks)
    ]
    tile = TILE if columns % (2 * TILE) == 0 else columns
    early = columns // 2 // tile * tile or columns
    held = pl.pallas_call(
        functools.partial(fetch_kernel, serving),
        out_shape=[pltpu.VMEM((features, early), jnp.bfloat16)] * 2,
        in_specs=[pl.BlockSpec(memory_space=pl.ANY), hbm, hbm],
        out_specs=[vmem] * 2,
        scratch_shapes=[pltpu.SemaphoreType.DMA((2,))],
        compiler_params=pltpu.CompilerParams(vmem_limit_bytes=4 << 20),
        cost_estimate=pl.CostEstimate(
            flops=0, bytes_accessed=early * 4 * features, transcendentals=0
        ),
    )(block, gate, up)
    padded = -(-STEPS * serving // 16) * 16
    together = jax.ShapeDtypeStruct((workers, STEPS, columns), jnp.bfloat16)
    *hidden, shared = pl.pallas_call(
        functools.partial(forward_kernel, blocks, workers, narrow),
        out_shape=[jax.ShapeDtypeStruct((STEPS, columns), jnp.bfloat16)] * (serving - workers)
        + [together],
        in_specs=[vmem] * (blocks + 2) + [hbm, hbm],
        out_specs=[vmem] * (serving - workers + 1),
        scratch_shapes=[
            pltpu.VMEM((padded, features), jnp.bfloat16),
            pltpu.VMEM((SLOTS, 2, features, tile), jnp.bfloat16),
            pltpu.SemaphoreType.DMA((SLOTS, 2, 2)),
        ],
        compiler_params=pltpu.CompilerParams(vmem_limit_bytes=19 << 20),
    )(*arrived, *held, gate, up)
    middle = blocks // 2
    shared = lax.ppermute(
        shared, "wide", [(serving + k, middle * workers + k) for k in range(workers)]
    )
    peers = [list(range(at, at + workers)) for at in range(0, wide, workers)]

    def skip(shared):
        return pl.pallas_call(
            blank_kernel,
            out_shape=jax.ShapeDtypeStruct((workers, *shared.shape), jnp.bfloat16),
            out_specs=vmem,
            compiler_params=pltpu.CompilerParams(vmem_limit_bytes=8 << 20),
        )()

    gathered = lax.cond(
        lax.axis_index("wide") // workers == middle,
        lambda shared: lax.all_gather(shared, "wide", axis=0, axis_index_groups=peers),
        skip,
        shared,
    )
    results = list(hidden)
    for i, nth in enumerate(places(blocks, workers)):
        if nth is not None:
            b, s = divmod(i, workers)
            pairs = [(serving + k, b * workers + (k + s) % workers) for k in range(workers)]
            results[nth] = lax.ppermute(hidden[nth], "wide", pairs)
    aligned = columns % 128 == 0
    attended, activated = pl.pallas_call(
        functools.partial(finish_kernel, blocks, workers),
        out_shape=(
            jax.ShapeDtypeStruct((STEPS, half), jnp.bfloat16),
            jax.ShapeDtypeStruct((STEPS, workers * columns), jnp.bfloat16),
        ),
        in_specs=[vmem] * (2 + (len(results) if aligned else 0)),
        out_specs=(vmem, vmem),
        compiler_params=pltpu.CompilerParams(vmem_limit_bytes=8 << 20),
    )(attended, gathered, *(results if aligned else []))
    if not aligned:
        me = lax.axis_index("wide")
        pieces = []
        for k in range(workers):
            piece = activated[:, k * columns : (k + 1) * columns]
            for i, nth in enumerate(places(blocks, workers)):
                if nth is not None:
                    mine = me == i // workers * workers + (k + i) % workers
                    piece = jnp.where(mine, results[nth], piece)
            pieces.append(piece)
        activated = jnp.concatenate(pieces, 1)
    return attended.reshape(STEPS, 1, half), activated.reshape(STEPS, 1, -1)


def solution(mesh):
    rows = P(None, ("parts", "wide"), "narrow")
    placed = (
        rows,
        P(None, ("parts", "wide"), None, "narrow"),
        P(("parts", "wide"), "narrow", None, None),
        P(("parts", "wide"), "narrow", None, None),
        P(("parts", "wide")),
        rows,
        P("narrow"),
        P(None, "narrow", "wide"),
        P(None, "narrow", "wide"),
    )
    return jax.shard_map(
        shards, mesh=mesh, in_specs=placed, out_specs=(rows, rows), check_vma=False
    )
```

```python
import functools

import jax
import jax.numpy as jnp
from jax import lax
from jax.experimental import pallas as pl
from jax.experimental.pallas import tpu as pltpu
from jax.sharding import PartitionSpec as P

D = 4096
HEAD_SIZE = 128
STEPS = 2
TAIL = 128
EPS = 1e-05
TILE = 256
SLOTS = 4
AHEAD = (3, 1, 1, 1, 1)
CHUNK = 1024


def pair(squares):
    high = squares.astype(jnp.bfloat16).astype(jnp.float32)
    lane = lax.broadcasted_iota(jnp.int32, (squares.shape[0], TAIL), 1)
    both = jnp.where(lane == 0, high, jnp.where(lane == 1, squares - high, 0.0))
    return both.astype(jnp.bfloat16)


def fetch_kernel(serving, _, gate, up, gate_held, up_held, sems):
    @pl.when(lax.axis_index("wide") >= serving)
    def _():
        here = pl.ds(0, gate_held.shape[1])
        copies = [
            pltpu.make_async_copy(gate.at[:, here], gate_held, sems.at[0]),
            pltpu.make_async_copy(up.at[:, here], up_held, sems.at[1]),
        ]
        for c in copies:
            c.start()
        for c in copies:
            c.wait()


def blank_kernel(*outs):
    for out in outs:
        out[...] = jnp.zeros_like(out)


def attend_kernel(*refs):
    sources, (attended, sent), held, sems = refs[:7], refs[7:9], refs[9:16], refs[16]
    lengths, q, kv, keys, values, residual, gain = held
    heads, hist, _ = keys.shape
    width = q.shape[1]
    group = width // (heads * HEAD_SIZE)
    copies = [
        pltpu.make_async_copy(source, place, sems.at[i])
        for i, (source, place) in enumerate(zip(sources, held))
    ]
    for c in copies:
        c.start()
    for c in copies:
        c.wait()
    length = lengths[0, 0]
    first = hist - STEPS
    for h in range(heads):
        lanes = slice(h * HEAD_SIZE, (h + 1) * HEAD_SIZE)
        for t in range(STEPS):
            keys[h, first + t : first + t + 1, :] = kv[t, 0:1, lanes]
            values[h, first + t : first + t + 1, :] = kv[t, 1:2, lanes]
    rows = heads * group * STEPS
    place = lax.broadcasted_iota(jnp.int32, (rows, hist), 1)
    step = lax.broadcasted_iota(jnp.int32, (rows, hist), 0) % STEPS
    seen = (place < length) | ((place >= first) & (place - first <= step))
    cols = [c * HEAD_SIZE for c in range(heads * group)]
    query = jnp.concatenate([q[:, c : c + HEAD_SIZE].astype(jnp.float32) for c in cols], 0)
    query = query.astype(jnp.bfloat16).reshape(heads, group * STEPS, HEAD_SIZE)
    scores = jnp.concatenate(
        [
            lax.dot_general(
                query[h], keys[h], (((1,), (1,)), ((), ())), preferred_element_type=jnp.float32
            )
            for h in range(heads)
        ],
        0,
    ) * (1.0 / HEAD_SIZE**0.5)
    scores = jnp.where(seen, scores, -1e30)
    top = jnp.max(scores, -1, keepdims=True)
    e = jnp.where(seen, jnp.exp(scores - top), 0.0)
    weights = (e / jnp.sum(e, -1, keepdims=True)).astype(jnp.bfloat16)
    weights = weights.reshape(heads, group * STEPS, hist)
    outs = [
        jnp.dot(weights[h], values[h], preferred_element_type=jnp.float32) for h in range(heads)
    ]
    squares = jnp.zeros((STEPS, HEAD_SIZE), jnp.float32)
    for i, c in enumerate(cols):
        here = slice(c, c + HEAD_SIZE)
        g = i % group * STEPS
        got = outs[i // group][g : g + STEPS].astype(jnp.bfloat16)
        attended[:, here] = got
        mixed = residual[:, here].astype(jnp.float32) + got.astype(jnp.float32)
        squares += mixed * mixed
        sent[:, here] = (mixed * gain[:, here]).astype(jnp.bfloat16)
    squares = jnp.sum(squares, -1, keepdims=True)
    sent[:, width:] = pair(squares)


def places(blocks, workers):
    middle = blocks // 2
    leaving = [b for b in range(blocks) if b != middle]
    found = []
    for b in range(blocks):
        for shift in range(workers):
            nth = leaving.index(b) * workers + shift if b != middle else None
            found.append(nth)
    return found


def forward_kernel(blocks, workers, narrow, *refs):
    count = blocks * workers
    arrived, (gate_held, up_held, gate, up), rest = refs[:blocks], refs[blocks:][:4], refs[blocks + 4 :]
    outs, (x, wide_rows, slots, sems) = rest[:-4], rest[-4:]
    me = lax.axis_index("wide") - count
    features, columns = gate.shape
    half = features // narrow
    early = gate_held.shape[1]
    room, _, _, tile = slots.shape
    units = list(range(early, columns, tile))

    def stream(j):
        s = j % room
        here = pl.ds(units[j], tile)
        size = features // 2 if j == len(units) - 1 else features
        depths = [pl.ds(at, size) for at in range(0, features, size)]
        return [
            pltpu.make_async_copy(m.at[k, here], slots.at[s, i, k], sems.at[s, i, part])
            for part, k in enumerate(depths)
            for i, m in enumerate((gate, up))
        ]

    @pl.when(me >= 0)
    def _():
        for j in range(min(room, len(units))):
            for copy in stream(j):
                copy.start()
        tails = []
        for b, block in enumerate(arrived):
            for shift in range(workers):
                owner = lax.rem(me + shift, workers)
                at = (b * workers + shift) * STEPS
                tail = jnp.zeros((STEPS, TAIL), jnp.float32)
                for n in range(narrow):
                    piece = block[owner * narrow + n].astype(jnp.float32)
                    wide_rows[at : at + STEPS, n * half : (n + 1) * half] = piece[:, :half]
                    tail += piece[:, half:]
                tails.append(tail)
        pad = x.shape[0] - STEPS * count
        if pad:
            wide_rows[STEPS * count :, :] = jnp.zeros((pad, features), jnp.float32)
            tails.append(jnp.zeros((pad, TAIL), jnp.float32))
        x[...] = wide_rows[...].astype(jnp.bfloat16)
        squares = jnp.sum(jnp.concatenate(tails, 0), -1, keepdims=True)
        r = lax.rsqrt(squares / D + EPS)

        def multiply(depth, sums, tiles):
            for at in range(depth.start, depth.stop, CHUNK):
                k = slice(at, min(at + CHUNK, depth.stop))
                for i, some in enumerate(tiles):
                    more = jnp.dot(x[:, k], some(k), preferred_element_type=jnp.float32)
                    sums[i] = more if sums[i] is None else sums[i] + more
            return sums

        def produce(at, g, u):
            g, u = g * r, u * r
            hidden = (g / (1.0 + jnp.exp(-g)) * u).astype(jnp.bfloat16)
            for i, place in enumerate(places(blocks, workers)):
                rows = hidden[i * STEPS : (i + 1) * STEPS]
                if place is None:
                    outs[-1][i % workers, :, at : at + tile] = rows
                else:
                    outs[place][:, at : at + tile] = rows

        waiting = list(range(0, early, tile))

        def resident(some):
            for at in waiting[:some]:
                here = slice(at, at + tile)
                tiles = [lambda k, m=m: m[k, here] for m in (gate_held, up_held)]
                produce(at, *multiply(slice(0, features), [None] * 2, tiles))
            del waiting[:some]

        for j, at in enumerate(units):
            resident(AHEAD[j] if j < len(AHEAD) else 0)
            if j == len(units) - 1:
                resident(len(waiting))
            copies, sums = stream(j), [None] * 2
            tiles = [lambda k, i=i, s=j % room: slots[s, i, k, :] for i in range(2)]
            size = features * 2 // len(copies)
            for part in range(len(copies) // 2):
                for copy in copies[part * 2 : part * 2 + 2]:
                    copy.wait()
                multiply(slice(part * size, (part + 1) * size), sums, tiles)
            produce(at, *sums)
            if j + room < len(units):
                for copy in stream(j + room):
                    copy.start()
        if not units:
            resident(len(waiting))


def finish_kernel(blocks, workers, attended, gathered, *refs):
    results, (attended_out, out) = refs[:-2], refs[-2:]
    me = lax.axis_index("wide")
    block, place = me // workers, lax.rem(me, workers)
    columns = gathered.shape[3]
    attended_out[...] = attended[...]

    @pl.when(block >= blocks)
    def _():
        out[...] = jnp.zeros_like(out)

    @pl.when(block == blocks // 2)
    def _():
        for k in range(workers):
            shift = lax.rem(place + workers - k, workers)
            out[:, k * columns : (k + 1) * columns] = gathered[k, shift]

    if not results:
        return

    for i, nth in enumerate(places(blocks, workers)):
        if nth is not None:

            @pl.when(block == i // workers)
            def _(i=i, nth=nth):
                k = lax.rem(place + workers - i % workers, workers)
                out[:, pl.ds(pl.multiple_of(k * columns, 128), columns)] = results[nth][...]


def shards(queries, new_kv, keys, values, lengths, residual, gain, gate, up):
    wide = lax.axis_size("wide")
    narrow = lax.axis_size("narrow")
    serving = wide * 3 // 4
    workers = wide - serving
    blocks = serving // workers
    half = queries.shape[2]
    features, _, columns = gate.shape
    vmem = pl.BlockSpec(memory_space=pltpu.VMEM)
    hbm = pl.BlockSpec(memory_space=pltpu.HBM)
    owner = lax.axis_index("wide") < serving

    def in_hbm(a):
        return pltpu.with_memory_space_constraint(a, pltpu.HBM)

    gate = in_hbm(gate.reshape(features, columns))
    up = in_hbm(up.reshape(features, columns))
    operands = (
        lengths.reshape(1, 1),
        queries.reshape(STEPS, half),
        new_kv.reshape(STEPS, 2, -1),
        keys.reshape(keys.shape[1:]),
        values.reshape(values.shape[1:]),
        residual.reshape(STEPS, half),
        gain.reshape(1, half),
    )
    groups = [
        [w * narrow + n for w in range(at, at + workers) for n in range(narrow)]
        for at in range(0, wide, workers)
    ]
    shapes = (
        jax.ShapeDtypeStruct((STEPS, half), jnp.bfloat16),
        jax.ShapeDtypeStruct((workers * narrow, STEPS, half + TAIL), jnp.bfloat16),
    )

    def serve(*operands):
        attended, sent = pl.pallas_call(
            attend_kernel,
            out_shape=(
                pltpu.VMEM(shapes[0].shape, jnp.bfloat16),
                jax.ShapeDtypeStruct(shapes[1].shape[1:], jnp.bfloat16),
            ),
            in_specs=[hbm] * 7,
            out_specs=(vmem, vmem),
            scratch_shapes=[
                (pltpu.SMEM if o.dtype == jnp.int32 else pltpu.VMEM)(o.shape, o.dtype)
                for o in operands
            ]
            + [pltpu.SemaphoreType.DMA((7,))],
            compiler_params=pltpu.CompilerParams(vmem_limit_bytes=8 << 20),
        )(operands[0], *map(in_hbm, operands[1:]))
        gathered = lax.all_gather(sent, ("wide", "narrow"), axis=0, axis_index_groups=groups)
        return attended, gathered

    def rest(*operands):
        return pl.pallas_call(
            blank_kernel,
            out_shape=(pltpu.VMEM(shapes[0].shape, jnp.bfloat16), shapes[1]),
            out_specs=(vmem, vmem),
            compiler_params=pltpu.CompilerParams(vmem_limit_bytes=8 << 20),
        )()

    attended, block = lax.cond(owner, serve, rest, *operands)
    arrived = [
        lax.ppermute(block, "wide", [(b * workers + j, serving + j) for j in range(workers)])
        for b in range(blocks)
    ]
    tile = TILE if columns % (2 * TILE) == 0 else columns
    early = columns // 2 // tile * tile or columns
    held = pl.pallas_call(
        functools.partial(fetch_kernel, serving),
        out_shape=[pltpu.VMEM((features, early), jnp.bfloat16)] * 2,
        in_specs=[pl.BlockSpec(memory_space=pl.ANY), hbm, hbm],
        out_specs=[vmem] * 2,
        scratch_shapes=[pltpu.SemaphoreType.DMA((2,))],
        compiler_params=pltpu.CompilerParams(vmem_limit_bytes=4 << 20),
        cost_estimate=pl.CostEstimate(
            flops=0, bytes_accessed=early * 4 * features, transcendentals=0
        ),
    )(block, gate, up)
    padded = -(-STEPS * serving // 16) * 16
    together = jax.ShapeDtypeStruct((workers, STEPS, columns), jnp.bfloat16)
    *hidden, shared = pl.pallas_call(
        functools.partial(forward_kernel, blocks, workers, narrow),
        out_shape=[jax.ShapeDtypeStruct((STEPS, columns), jnp.bfloat16)] * (serving - workers)
        + [together],
        in_specs=[vmem] * (blocks + 2) + [hbm, hbm],
        out_specs=[vmem] * (serving - workers + 1),
        scratch_shapes=[
            pltpu.VMEM((padded, features), jnp.bfloat16),
            pltpu.VMEM((padded, features), jnp.float32),
            pltpu.VMEM((SLOTS, 2, features, tile), jnp.bfloat16),
            pltpu.SemaphoreType.DMA((SLOTS, 2, 2)),
        ],
        compiler_params=pltpu.CompilerParams(vmem_limit_bytes=19 << 20),
    )(*arrived, *held, gate, up)
    middle = blocks // 2
    shared = lax.ppermute(
        shared, "wide", [(serving + k, middle * workers + k) for k in range(workers)]
    )
    peers = [list(range(at, at + workers)) for at in range(0, wide, workers)]

    def skip(shared):
        return pl.pallas_call(
            blank_kernel,
            out_shape=jax.ShapeDtypeStruct((workers, *shared.shape), jnp.bfloat16),
            out_specs=vmem,
            compiler_params=pltpu.CompilerParams(vmem_limit_bytes=8 << 20),
        )()

    gathered = lax.cond(
        lax.axis_index("wide") // workers == middle,
        lambda shared: lax.all_gather(shared, "wide", axis=0, axis_index_groups=peers),
        skip,
        shared,
    )
    results = list(hidden)
    for i, nth in enumerate(places(blocks, workers)):
        if nth is not None:
            b, s = divmod(i, workers)
            pairs = [(serving + k, b * workers + (k + s) % workers) for k in range(workers)]
            results[nth] = lax.ppermute(hidden[nth], "wide", pairs)
    aligned = columns % 128 == 0
    attended, activated = pl.pallas_call(
        functools.partial(finish_kernel, blocks, workers),
        out_shape=(
            jax.ShapeDtypeStruct((STEPS, half), jnp.bfloat16),
            jax.ShapeDtypeStruct((STEPS, workers * columns), jnp.bfloat16),
        ),
        in_specs=[vmem] * (2 + (len(results) if aligned else 0)),
        out_specs=(vmem, vmem),
        compiler_params=pltpu.CompilerParams(vmem_limit_bytes=8 << 20),
    )(attended, gathered, *(results if aligned else []))
    if not aligned:
        me = lax.axis_index("wide")
        pieces = []
        for k in range(workers):
            piece = activated[:, k * columns : (k + 1) * columns]
            for i, nth in enumerate(places(blocks, workers)):
                if nth is not None:
                    mine = me == i // workers * workers + (k + i) % workers
                    piece = jnp.where(mine, results[nth], piece)
            pieces.append(piece)
        activated = jnp.concatenate(pieces, 1)
    return attended.reshape(STEPS, 1, half), activated.reshape(STEPS, 1, -1)


def solution(mesh):
    rows = P(None, ("parts", "wide"), "narrow")
    placed = (
        rows,
        P(None, ("parts", "wide"), None, "narrow"),
        P(("parts", "wide"), "narrow", None, None),
        P(("parts", "wide"), "narrow", None, None),
        P(("parts", "wide")),
        rows,
        P("narrow"),
        P(None, "narrow", "wide"),
        P(None, "narrow", "wide"),
    )
    return jax.shard_map(
        shards, mesh=mesh, in_specs=placed, out_specs=(rows, rows), check_vma=False
    )
```

```python
import functools

import jax
import jax.numpy as jnp
from jax import lax
from jax.experimental import pallas as pl
from jax.experimental.pallas import tpu as pltpu
from jax.sharding import PartitionSpec as P

D = 4096
HEAD_SIZE = 128
STEPS = 2
TAIL = 128
EPS = 1e-05
TILE = 256
SLOTS = 4
AHEAD = (2, 1, 1, 1, 1)
CHUNK = 1024


def pair(squares):
    high = squares.astype(jnp.bfloat16).astype(jnp.float32)
    lane = lax.broadcasted_iota(jnp.int32, (squares.shape[0], TAIL), 1)
    both = jnp.where(lane == 0, high, jnp.where(lane == 1, squares - high, 0.0))
    return both.astype(jnp.bfloat16)


def fetch_kernel(serving, _, gate, up, gate_held, up_held, sems):
    @pl.when(lax.axis_index("wide") >= serving)
    def _():
        here = pl.ds(0, gate_held.shape[1])
        copies = [
            pltpu.make_async_copy(gate.at[:, here], gate_held, sems.at[0]),
            pltpu.make_async_copy(up.at[:, here], up_held, sems.at[1]),
        ]
        for c in copies:
            c.start()
        for c in copies:
            c.wait()


def blank_kernel(*outs):
    for out in outs:
        out[...] = jnp.zeros_like(out)


def attend_kernel(*refs):
    sources, (attended, sent), held, sems = refs[:7], refs[7:9], refs[9:16], refs[16]
    lengths, q, kv, keys, values, residual, gain = held
    heads, hist, _ = keys.shape
    width = q.shape[1]
    group = width // (heads * HEAD_SIZE)
    copies = [
        pltpu.make_async_copy(source, place, sems.at[i])
        for i, (source, place) in enumerate(zip(sources, held))
    ]
    for c in copies:
        c.start()
    for c in copies:
        c.wait()
    length = lengths[0, 0]
    first = hist - STEPS
    for h in range(heads):
        lanes = slice(h * HEAD_SIZE, (h + 1) * HEAD_SIZE)
        for t in range(STEPS):
            keys[h, first + t : first + t + 1, :] = kv[t, 0:1, lanes]
            values[h, first + t : first + t + 1, :] = kv[t, 1:2, lanes]
    rows = heads * group * STEPS
    place = lax.broadcasted_iota(jnp.int32, (rows, hist), 1)
    step = lax.broadcasted_iota(jnp.int32, (rows, hist), 0) % STEPS
    seen = (place < length) | ((place >= first) & (place - first <= step))
    cols = [c * HEAD_SIZE for c in range(heads * group)]
    query = jnp.concatenate([q[:, c : c + HEAD_SIZE].astype(jnp.float32) for c in cols], 0)
    query = query.astype(jnp.bfloat16).reshape(heads, group * STEPS, HEAD_SIZE)
    scores = jnp.concatenate(
        [
            lax.dot_general(
                query[h], keys[h], (((1,), (1,)), ((), ())), preferred_element_type=jnp.float32
            )
            for h in range(heads)
        ],
        0,
    ) * (1.0 / HEAD_SIZE**0.5)
    scores = jnp.where(seen, scores, -1e30)
    top = jnp.max(scores, -1, keepdims=True)
    e = jnp.where(seen, jnp.exp(scores - top), 0.0)
    weights = (e / jnp.sum(e, -1, keepdims=True)).astype(jnp.bfloat16)
    weights = weights.reshape(heads, group * STEPS, hist)
    outs = [
        jnp.dot(weights[h], values[h], preferred_element_type=jnp.float32) for h in range(heads)
    ]
    squares = jnp.zeros((STEPS, HEAD_SIZE), jnp.float32)
    for i, c in enumerate(cols):
        here = slice(c, c + HEAD_SIZE)
        g = i % group * STEPS
        got = outs[i // group][g : g + STEPS].astype(jnp.bfloat16)
        attended[:, here] = got
        mixed = residual[:, here].astype(jnp.float32) + got.astype(jnp.float32)
        squares += mixed * mixed
        sent[:, here] = (mixed * gain[:, here]).astype(jnp.bfloat16)
    squares = jnp.sum(squares, -1, keepdims=True)
    sent[:, width:] = pair(squares)


def places(blocks, workers):
    middle = blocks // 2
    leaving = [b for b in range(blocks) if b != middle]
    found = []
    for b in range(blocks):
        for shift in range(workers):
            nth = leaving.index(b) * workers + shift if b != middle else None
            found.append(nth)
    return found


def forward_kernel(blocks, workers, narrow, *refs):
    count = blocks * workers
    arrived, (gate_held, up_held, gate, up), rest = refs[:blocks], refs[blocks:][:4], refs[blocks + 4 :]
    outs, (x, slots, sems) = rest[:-3], rest[-3:]
    me = lax.axis_index("wide") - count
    features, columns = gate.shape
    half = features // narrow
    early = gate_held.shape[1]
    room, _, _, tile = slots.shape
    units = list(range(early, columns, tile))

    def stream(j):
        s = j % room
        here = pl.ds(units[j], tile)
        size = features // 2 if j == len(units) - 1 else features
        depths = [pl.ds(at, size) for at in range(0, features, size)]
        return [
            pltpu.make_async_copy(m.at[k, here], slots.at[s, i, k], sems.at[s, i, part])
            for part, k in enumerate(depths)
            for i, m in enumerate((gate, up))
        ]

    @pl.when(me >= 0)
    def _():
        for j in range(min(room, len(units))):
            for copy in stream(j):
                copy.start()
        lines, tails = [], []
        for block in arrived:
            for shift in range(workers):
                owner = lax.rem(me + shift, workers)
                halves = [block[owner * narrow + n] for n in range(narrow)]
                lines.append(
                    jnp.concatenate([h[:, :half] for h in halves], 1).astype(jnp.float32)
                )
                tails.append(sum(h[:, half:].astype(jnp.float32) for h in halves))
        pad = x.shape[0] - STEPS * count
        if pad:
            lines.append(jnp.zeros((pad, features), jnp.float32))
            tails.append(jnp.zeros((pad, TAIL), jnp.float32))
        x[...] = jnp.concatenate(lines, 0).astype(jnp.bfloat16)
        squares = jnp.sum(jnp.concatenate(tails, 0), -1, keepdims=True)
        r = lax.rsqrt(squares / D + EPS)

        def multiply(depth, sums, tiles):
            for at in range(depth.start, depth.stop, CHUNK):
                k = slice(at, min(at + CHUNK, depth.stop))
                for i, some in enumerate(tiles):
                    more = jnp.dot(x[:, k], some(k), preferred_element_type=jnp.float32)
                    sums[i] = more if sums[i] is None else sums[i] + more
            return sums

        def produce(at, g, u):
            g, u = g * r, u * r
            hidden = (g / (1.0 + jnp.exp(-g)) * u).astype(jnp.bfloat16)
            for i, place in enumerate(places(blocks, workers)):
                rows = hidden[i * STEPS : (i + 1) * STEPS]
                if place is None:
                    outs[-1][i % workers, :, at : at + tile] = rows
                else:
                    outs[place][:, at : at + tile] = rows

        waiting = list(range(0, early, tile))

        def resident(some):
            for at in waiting[:some]:
                here = slice(at, at + tile)
                tiles = [lambda k, m=m: m[k, here] for m in (gate_held, up_held)]
                produce(at, *multiply(slice(0, features), [None] * 2, tiles))
            del waiting[:some]

        for j, at in enumerate(units):
            resident(AHEAD[j] if j < len(AHEAD) else 0)
            if j == len(units) - 1:
                resident(len(waiting))
            copies, sums = stream(j), [None] * 2
            tiles = [lambda k, i=i, s=j % room: slots[s, i, k, :] for i in range(2)]
            size = features * 2 // len(copies)
            for part in range(len(copies) // 2):
                for copy in copies[part * 2 : part * 2 + 2]:
                    copy.wait()
                multiply(slice(part * size, (part + 1) * size), sums, tiles)
            produce(at, *sums)
            if j + room < len(units):
                for copy in stream(j + room):
                    copy.start()
        if not units:
            resident(len(waiting))


def finish_kernel(blocks, workers, attended, gathered, *refs):
    results, (attended_out, out) = refs[:-2], refs[-2:]
    me = lax.axis_index("wide")
    block, place = me // workers, lax.rem(me, workers)
    columns = gathered.shape[3]
    attended_out[...] = attended[...]

    @pl.when(block >= blocks)
    def _():
        out[...] = jnp.zeros_like(out)

    @pl.when(block == blocks // 2)
    def _():
        for k in range(workers):
            shift = lax.rem(place + workers - k, workers)
            out[:, k * columns : (k + 1) * columns] = gathered[k, shift]

    if not results:
        return

    for i, nth in enumerate(places(blocks, workers)):
        if nth is not None:

            @pl.when(block == i // workers)
            def _(i=i, nth=nth):
                k = lax.rem(place + workers - i % workers, workers)
                out[:, pl.ds(pl.multiple_of(k * columns, 128), columns)] = results[nth][...]


def shards(queries, new_kv, keys, values, lengths, residual, gain, gate, up):
    wide = lax.axis_size("wide")
    narrow = lax.axis_size("narrow")
    serving = wide * 3 // 4
    workers = wide - serving
    blocks = serving // workers
    half = queries.shape[2]
    features, _, columns = gate.shape
    vmem = pl.BlockSpec(memory_space=pltpu.VMEM)
    hbm = pl.BlockSpec(memory_space=pltpu.HBM)
    owner = lax.axis_index("wide") < serving

    def in_hbm(a):
        return pltpu.with_memory_space_constraint(a, pltpu.HBM)

    gate = in_hbm(gate.reshape(features, columns))
    up = in_hbm(up.reshape(features, columns))
    operands = (
        lengths.reshape(1, 1),
        queries.reshape(STEPS, half),
        new_kv.reshape(STEPS, 2, -1),
        keys.reshape(keys.shape[1:]),
        values.reshape(values.shape[1:]),
        residual.reshape(STEPS, half),
        gain.reshape(1, half),
    )
    groups = [
        [w * narrow + n for w in range(at, at + workers) for n in range(narrow)]
        for at in range(0, wide, workers)
    ]
    shapes = (
        jax.ShapeDtypeStruct((STEPS, half), jnp.bfloat16),
        jax.ShapeDtypeStruct((workers * narrow, STEPS, half + TAIL), jnp.bfloat16),
    )

    def serve(*operands):
        attended, sent = pl.pallas_call(
            attend_kernel,
            out_shape=(
                pltpu.VMEM(shapes[0].shape, jnp.bfloat16),
                jax.ShapeDtypeStruct(shapes[1].shape[1:], jnp.bfloat16),
            ),
            in_specs=[hbm] * 7,
            out_specs=(vmem, vmem),
            scratch_shapes=[
                (pltpu.SMEM if o.dtype == jnp.int32 else pltpu.VMEM)(o.shape, o.dtype)
                for o in operands
            ]
            + [pltpu.SemaphoreType.DMA((7,))],
            compiler_params=pltpu.CompilerParams(vmem_limit_bytes=8 << 20),
        )(operands[0], *map(in_hbm, operands[1:]))
        gathered = lax.all_gather(sent, ("wide", "narrow"), axis=0, axis_index_groups=groups)
        return attended, gathered

    def rest(*operands):
        return pl.pallas_call(
            blank_kernel,
            out_shape=(pltpu.VMEM(shapes[0].shape, jnp.bfloat16), shapes[1]),
            out_specs=(vmem, vmem),
            compiler_params=pltpu.CompilerParams(vmem_limit_bytes=8 << 20),
        )()

    attended, block = lax.cond(owner, serve, rest, *operands)
    arrived = [
        lax.ppermute(block, "wide", [(b * workers + j, serving + j) for j in range(workers)])
        for b in range(blocks)
    ]
    tile = TILE if columns % (2 * TILE) == 0 else columns
    early = columns * 3 // 7 // tile * tile or columns
    held = pl.pallas_call(
        functools.partial(fetch_kernel, serving),
        out_shape=[pltpu.VMEM((features, early), jnp.bfloat16)] * 2,
        in_specs=[pl.BlockSpec(memory_space=pl.ANY), hbm, hbm],
        out_specs=[vmem] * 2,
        scratch_shapes=[pltpu.SemaphoreType.DMA((2,))],
        compiler_params=pltpu.CompilerParams(vmem_limit_bytes=4 << 20),
        cost_estimate=pl.CostEstimate(
            flops=0, bytes_accessed=early * 4 * features, transcendentals=0
        ),
    )(block, gate, up)
    padded = -(-STEPS * serving // 16) * 16
    together = jax.ShapeDtypeStruct((workers, STEPS, columns), jnp.bfloat16)
    *hidden, shared = pl.pallas_call(
        functools.partial(forward_kernel, blocks, workers, narrow),
        out_shape=[jax.ShapeDtypeStruct((STEPS, columns), jnp.bfloat16)] * (serving - workers)
        + [together],
        in_specs=[vmem] * (blocks + 2) + [hbm, hbm],
        out_specs=[vmem] * (serving - workers + 1),
        scratch_shapes=[
            pltpu.VMEM((padded, features), jnp.bfloat16),
            pltpu.VMEM((SLOTS, 2, features, tile), jnp.bfloat16),
            pltpu.SemaphoreType.DMA((SLOTS, 2, 2)),
        ],
        compiler_params=pltpu.CompilerParams(vmem_limit_bytes=19 << 20),
    )(*arrived, *held, gate, up)
    middle = blocks // 2
    shared = lax.ppermute(
        shared, "wide", [(serving + k, middle * workers + k) for k in range(workers)]
    )
    peers = [list(range(at, at + workers)) for at in range(0, wide, workers)]

    def skip(shared):
        return pl.pallas_call(
            blank_kernel,
            out_shape=jax.ShapeDtypeStruct((workers, *shared.shape), jnp.bfloat16),
            out_specs=vmem,
            compiler_params=pltpu.CompilerParams(vmem_limit_bytes=8 << 20),
        )()

    gathered = lax.cond(
        lax.axis_index("wide") // workers == middle,
        lambda shared: lax.all_gather(shared, "wide", axis=0, axis_index_groups=peers),
        skip,
        shared,
    )
    results = list(hidden)
    for i, nth in enumerate(places(blocks, workers)):
        if nth is not None:
            b, s = divmod(i, workers)
            pairs = [(serving + k, b * workers + (k + s) % workers) for k in range(workers)]
            results[nth] = lax.ppermute(hidden[nth], "wide", pairs)
    aligned = columns % 128 == 0
    attended, activated = pl.pallas_call(
        functools.partial(finish_kernel, blocks, workers),
        out_shape=(
            jax.ShapeDtypeStruct((STEPS, half), jnp.bfloat16),
            jax.ShapeDtypeStruct((STEPS, workers * columns), jnp.bfloat16),
        ),
        in_specs=[vmem] * (2 + (len(results) if aligned else 0)),
        out_specs=(vmem, vmem),
        compiler_params=pltpu.CompilerParams(vmem_limit_bytes=8 << 20),
    )(attended, gathered, *(results if aligned else []))
    if not aligned:
        me = lax.axis_index("wide")
        pieces = []
        for k in range(workers):
            piece = activated[:, k * columns : (k + 1) * columns]
            for i, nth in enumerate(places(blocks, workers)):
                if nth is not None:
                    mine = me == i // workers * workers + (k + i) % workers
                    piece = jnp.where(mine, results[nth], piece)
            pieces.append(piece)
        activated = jnp.concatenate(pieces, 1)
    return attended.reshape(STEPS, 1, half), activated.reshape(STEPS, 1, -1)


def solution(mesh):
    rows = P(None, ("parts", "wide"), "narrow")
    placed = (
        rows,
        P(None, ("parts", "wide"), None, "narrow"),
        P(("parts", "wide"), "narrow", None, None),
        P(("parts", "wide"), "narrow", None, None),
        P(("parts", "wide")),
        rows,
        P("narrow"),
        P(None, "narrow", "wide"),
        P(None, "narrow", "wide"),
    )
    return jax.shard_map(
        shards, mesh=mesh, in_specs=placed, out_specs=(rows, rows), check_vma=False
    )
```
